128 devices in a mesh: ctx: 16 (over x, z_lo, core), tp: 8 (over y, z_hi).
Axes of the slice: x: 4, y: 4, z: 4 (z_hi: 2, z_lo: 2; z = z_hi * 2 + z_lo), core: 2. Of those that a mesh axis runs over, the one named last changes fastest.
Arguments:
- tokens: bfloat16 [16384, 1024], P(('ctx', 'tp')), may hold values from -6 to 6
- block_ids: int32 [16384], P('ctx'), may hold values from 0 to 127, never falling along the last dimension, each value on 1 to 256 neighbouring positions
- ln1_gain: bfloat16 [1024], replicated, may hold values from 0.099609375 to 1.8984375
- ln1_shift: bfloat16 [1024], replicated, may hold values from -1.75 to 1.75
- qkv_weight: bfloat16 [1024, 3, 1024], P(None, None, 'tp'), may hold values from -0.1875 to 0.1875
- qv_bias: bfloat16 [2, 1024], P(None, 'tp'), may hold values from -3 to 3
- out_weight: bfloat16 [1024, 1024], P('tp'), may hold values from -0.5 to 0.5
- out_bias: bfloat16 [1024], replicated, may hold values from -1.75 to 1.75
- ln2_gain: bfloat16 [1024], replicated, may hold values from 0.099609375 to 1.8984375
- ln2_shift: bfloat16 [1024], replicated, may hold values from -1.75 to 1.75
- up_weight: bfloat16 [1024, 4096], P(None, 'tp'), may hold values from -0.1875 to 0.1875
- up_bias: bfloat16 [4096], P('tp'), may hold values from -3 to 3
- down_weight: bfloat16 [4096, 1024], P('tp'), may hold values from -0.09375 to 0.09375
- down_bias: bfloat16 [1024], replicated, may hold values from -1.75 to 1.75
- cotangent: bfloat16 [16384, 1024], P(('ctx', 'tp')), may hold values from -6 to 6
Outputs:
- output: float32 [16384, 1024], P(('ctx', 'tp'))
- grad_tokens: float32 [16384, 1024], P(('ctx', 'tp'))
- grad_ln1_gain: float32 [1024], replicated
- grad_ln1_shift: float32 [1024], replicated
- grad_qkv_weight: float32 [1024, 3, 1024], P(None, None, 'tp')
- grad_qv_bias: float32 [2, 1024], P(None, 'tp')
- grad_out_weight: float32 [1024, 1024], P('tp')
- grad_out_bias: float32 [1024], replicated
- grad_ln2_gain: float32 [1024], replicated
- grad_ln2_shift: float32 [1024], replicated
- grad_up_weight: float32 [1024, 4096], P(None, 'tp')
- grad_up_bias: float32 [4096], P('tp')
- grad_down_weight: float32 [4096, 1024], P('tp')
- grad_down_bias: float32 [1024], replicated
The draws below stay inside these ranges and needn't reach their ends.
Inputs may be any that keep to these rules, and one draw needn't show every extreme that they name: `block_ids`: block numbers never fall along the sequence; each block holds 1 to 256 positions, one exactly 256, and every number is used.
All inputs are finite; a program needn't handle non-finite values.
Results may differ from the reference program's by a relative error of at most 0.019.
Values may be sent and summed in bfloat16 or wider, within the bound.
No kernel may reach another device: no remote copies, remote signals or barrier semaphores. Data moves between devices by JAX's collectives and lax.ppermute only.
A program may use at most 128 MiB of HBM per device.

```python
import math
import jax
import jax.numpy as jnp
import numpy as np
from jax import lax

D = 1024
HEADS = 16
HEAD_DIM = 64
FF = 4096
BLOCK = 256
TOK_DEV = 128
SEQ = 16384
BLOCKS = 128


def block_levels(stream_key, extent, shards, least, largest):
    level, own = 1.0, jax.random.fold_in(stream_key, 6)
    for dim, parts in shards:
        heights = jnp.exp(jax.random.uniform(jax.random.fold_in(own, dim), (parts,), jnp.float32, least / len(shards), largest / len(shards)))
        level = level * jnp.repeat(heights, extent[dim] // parts).reshape([-1 if axis == dim else 1 for axis in range(len(extent))])
    return level


def length_profile(amount, total, reach, lean):
    loads = [(1 << 20) // math.isqrt(grade ** lean) + 1 for grade in range(2, amount + 1)]
    spare, given = total - reach - (amount - 1), [1] * (amount - 1)
    while spare > 0:
        movable = [i for i in range(amount - 1) if given[i] < reach]
        whole, budget = sum([loads[i] for i in movable]), spare
        for i in movable:
            extra = min(reach - given[i], max(1, budget * loads[i] // whole), spare)
            given[i] = given[i] + extra
            spare = spare - extra
    return np.array([reach] + given)


def ragged(rng, amount, total, most, skew):
    if amount == 2:
        one = jax.random.randint(rng, (), max(1, total - most), min(most, total - 1) + 1)
        return jnp.stack([one, total - one])
    tallies = jnp.asarray(length_profile(amount, total, most, skew), jnp.int32)
    pairs = (amount - 1) // 2
    source_of, receiver = tallies[1:1 + 2 * pairs:2], tallies[2:2 + 2 * pairs:2]
    slack = jnp.minimum(source_of - 1, most - receiver)
    moved = jax.random.randint(jax.random.fold_in(rng, 1), (pairs,), 0, 1 << 20) % (slack + 1)
    tallies = tallies.at[1:1 + 2 * pairs:2].set(source_of - moved).at[2:2 + 2 * pairs:2].set(receiver + moved)
    return tallies[jax.random.permutation(jax.random.fold_in(rng, 2), amount)]


def centred(rng, dims, deviation, bound, shards=(), dtype=jnp.bfloat16):
    array = deviation * jax.random.normal(rng, dims, jnp.float32)
    if shards:
        array = array * block_levels(rng, dims, shards, -0.22, 0.18)
    return jnp.clip(array, -bound, bound).astype(dtype)


def setup_inputs(seed: int = 0) -> dict:
    key_of = jax.random.split(jax.random.key(seed), 16)
    tokens = centred(key_of[0], (SEQ, D), 1.0, 6.0, ((0, 128),))
    block_ids = jnp.searchsorted(jnp.cumsum(ragged(key_of[1], BLOCKS, SEQ, BLOCK, 0)), jnp.arange(SEQ), side="right").astype(jnp.int32)
    ln1_gain = jnp.clip(1.0 + 0.18 * jax.random.normal(key_of[2], (D,), jnp.float32), 0.099609375, 1.8984375).astype(jnp.bfloat16)
    ln1_shift = centred(key_of[3], (D,), 0.3, 1.75)
    qkv_weight = centred(key_of[4], (D, 3, D), D ** -0.5, 0.1875, ((2, 8),))
    qv_bias = centred(key_of[5], (2, D), 0.5, 3.0, ((1, 8),))
    out_weight = centred(key_of[6], (D, D), (max(SEQ // (16 * D), 1) ** 0.5 * D ** -0.5), 0.5, ((0, 8),))
    out_bias = centred(key_of[7], (D,), 0.3, 1.75)
    ln2_gain = jnp.clip(1.0 + 0.18 * jax.random.normal(key_of[8], (D,), jnp.float32), 0.099609375, 1.8984375).astype(jnp.bfloat16)
    ln2_shift = centred(key_of[9], (D,), 0.3, 1.75)
    up_weight = centred(key_of[10], (D, FF), D ** -0.5, 0.1875, ((1, 8),))
    up_bias = centred(key_of[11], (FF,), 0.5, 3.0, ((0, 8),))
    down_weight = centred(key_of[12], (FF, D), FF ** -0.5, 0.09375, ((0, 8),))
    down_bias = centred(key_of[13], (D,), 0.3, 1.75)
    cotangent = centred(key_of[14], (SEQ, D), 1.0, 6.0, ((0, 128),))
    return {"tokens": tokens, "block_ids": block_ids, "ln1_gain": ln1_gain, "ln1_shift": ln1_shift, "qkv_weight": qkv_weight, "qv_bias": qv_bias, "out_weight": out_weight, "out_bias": out_bias, "ln2_gain": ln2_gain, "ln2_shift": ln2_shift, "up_weight": up_weight, "up_bias": up_bias, "down_weight": down_weight, "down_bias": down_bias, "cotangent": cotangent}


@jax.custom_vjp
def low(v):
    return lax.optimization_barrier(v.astype(jnp.bfloat16)).astype(jnp.float32)

@jax.custom_vjp
def low_back(v):
    return v

def low_keep(v):
    return (low(v), None)

def low_pass(kept, grad):
    return (grad,)

def back_keep(v):
    return (v, None)

def back_low(kept, grad):
    return (low(grad),)
low.defvjp(low_keep, low_pass)
low_back.defvjp(back_keep, back_low)
EPSILON = 1e-05
MASKED = -1e+30
HIGHEST_PRECISION = lax.Precision.HIGHEST

def layer_norm(values, norm_gain, norm_shift):
    average = lax.optimization_barrier(jnp.mean(values, axis=-1, keepdims=True))
    centered = values - average
    variance = lax.optimization_barrier(jnp.mean(centered * centered, axis=-1, keepdims=True))
    return centered * lax.rsqrt(variance + EPSILON) * norm_gain + norm_shift

def gelu_tanh(values):
    return 0.5 * values * (1.0 + jnp.tanh(0.7978845608028654 * (values + 0.044715 * values * values * values)))

def forward(tokens_wide, params, block_ids):
    ln1_gain, ln1_shift, qkv_weight, qv_bias, out_weight, out_bias, ln2_gain, ln2_shift, up_weight, up_bias, down_weight, down_bias = params
    normed = low(layer_norm(tokens_wide, ln1_gain, ln1_shift))
    projected = jnp.dot(normed, qkv_weight.reshape(D, 3 * D), precision=HIGHEST_PRECISION).reshape(SEQ, 3, D)
    queries = low_back(low(projected[:, 0] + qv_bias[0]))
    keys = low_back(low(projected[:, 1]))
    values = low_back(low(projected[:, 2] + qv_bias[1]))
    key_heads = keys.reshape(SEQ, HEADS, HEAD_DIM)
    value_heads = values.reshape(SEQ, HEADS, HEAD_DIM)
    scale = HEAD_DIM ** (-0.5)

    def attend(block_pair):
        query_block, query_ids = block_pair
        scores = low_back(jnp.einsum('qhd,khd->hqk', query_block, key_heads, precision=HIGHEST_PRECISION) * scale)
        allowed = block_ids[None, None, :] <= query_ids[None, :, None]
        masked = jnp.where(allowed, scores, MASKED)
        row_max = lax.optimization_barrier(jnp.max(masked, axis=-1, keepdims=True))
        exponents = jnp.where(allowed, jnp.exp(masked - row_max), 0.0)
        weights = exponents / lax.optimization_barrier(jnp.sum(exponents, axis=-1, keepdims=True))
        return jnp.einsum('hqk,khd->qhd', low(weights), value_heads, precision=HIGHEST_PRECISION)
    mixed = lax.map(jax.checkpoint(attend), (queries.reshape(SEQ // TOK_DEV, TOK_DEV, HEADS, HEAD_DIM), block_ids.reshape(SEQ // TOK_DEV, TOK_DEV)))
    attended = low_back(low(mixed.reshape(SEQ, D)))
    branch = low_back(jnp.dot(attended, out_weight, precision=HIGHEST_PRECISION))
    resid = tokens_wide + branch + out_bias
    normed_mid = low(layer_norm(resid, ln2_gain, ln2_shift))
    hidden = low_back(jnp.dot(normed_mid, up_weight, precision=HIGHEST_PRECISION) + up_bias)
    active = low(gelu_tanh(hidden))
    return resid + jnp.dot(active, down_weight, precision=HIGHEST_PRECISION) + down_bias

def reference(tokens, block_ids, ln1_gain, ln1_shift, qkv_weight, qv_bias, out_weight, out_bias, ln2_gain, ln2_shift, up_weight, up_bias, down_weight, down_bias, cotangent):
    params = (ln1_gain.astype(jnp.float32), ln1_shift.astype(jnp.float32), qkv_weight.astype(jnp.float32), qv_bias.astype(jnp.float32), out_weight.astype(jnp.float32), out_bias.astype(jnp.float32), ln2_gain.astype(jnp.float32), ln2_shift.astype(jnp.float32), up_weight.astype(jnp.float32), up_bias.astype(jnp.float32), down_weight.astype(jnp.float32), down_bias.astype(jnp.float32))
    output, backward = jax.vjp(lambda tokens_wide, weights: forward(tokens_wide, weights, block_ids), tokens.astype(jnp.float32), params)
    grad_tokens, grads = backward(cotangent.astype(jnp.float32))
    return (output, grad_tokens, grads[0], grads[1], grads[2], grads[3], grads[4], grads[5], grads[6], grads[7], grads[8], grads[9], grads[10], grads[11])
```

```python
import functools

import jax
import jax.numpy as jnp
from jax import lax
from jax.experimental import pallas as pl
from jax.experimental.pallas import tpu as pltpu
from jax.sharding import Mesh
from jax.sharding import PartitionSpec as P

HEAD_DIM = 64
EPSILON = 1e-05
MASKED = -1e30
LOG2E = 1.4426950408889634
TO_LOG2 = LOG2E * HEAD_DIM ** (-0.5)
AXES = ("x", "zl", "co", "y", "zh")
BF16, F32 = jnp.bfloat16, jnp.float32
SLICE = 1024
FWD_Q, FWD_K = 1024, 1024
BWD_Q, BWD_K = 512, 1024


def layer_norm(values, norm_gain, norm_shift):
    average = jnp.mean(values, axis=-1, keepdims=True)
    centered = values - average
    variance = jnp.mean(centered * centered, axis=-1, keepdims=True)
    return centered * lax.rsqrt(variance + EPSILON) * norm_gain + norm_shift


def gelu_tanh(values):
    return (
        0.5
        * values
        * (1.0 + jnp.tanh(0.7978845608028654 * (values + 0.044715 * values * values * values)))
    )


def contract(left, right, left_dim, right_dim):
    return lax.dot_general(
        left, right, (((left_dim,), (right_dim,)), ((), ())), preferred_element_type=F32
    )


def matmul(left, right):
    return contract(left, right, 1, 0)


def shift(values, axis, steps):
    return lax.ppermute(values, axis, [(i, (i + steps) % 4) for i in range(4)])


def swap(values, axis):
    return lax.ppermute(values, axis, [(0, 1), (1, 0)])


def mirror(values):
    return lax.ppermute(values, ("x", "co"), [(i, 7 - i) for i in range(8)])


def exchange(blocks, axes):
    return lax.all_to_all(blocks, axes, 0, 0, tiled=True)


def gather_y(rows):
    out = exchange(jnp.broadcast_to(rows[None], (4,) + rows.shape), "y")
    return out.reshape((4 * rows.shape[0],) + rows.shape[1:])


def scatter_y(partial):
    parts = exchange(partial.astype(BF16).reshape(4, -1, partial.shape[1]), "y")
    return jnp.sum(parts.astype(F32), axis=0)


def in_order(own, other, index):
    return jnp.where(index == 0, jnp.stack([own, other]), jnp.stack([other, own]))


def to_z(rows):
    n = rows.shape[-1]
    return rows.reshape(2, 4, 2, 128, n).transpose(0, 2, 1, 3, 4).reshape(4, 512, n)


def from_z(blocks):
    n = blocks.shape[-1]
    return blocks.reshape(2, 2, 4, 128, n).transpose(0, 2, 1, 3, 4).reshape(2, SLICE, n)


def pack(blocks):
    half = blocks.shape[1] // 2
    return jnp.concatenate([blocks[:, :half], blocks[:, half:]], axis=2)


def unpack(blocks):
    return jnp.concatenate([blocks[..., :HEAD_DIM], blocks[..., HEAD_DIM:]], axis=1)


def forward_kernel(spot, q_ref, end_ref, *refs):
    pieces, (out_t, out, lse_ref, kv_ref, vt_ref, qt_ref, sems) = refs[:10], refs[10:]
    x, core = spot[0], spot[1]
    copies = []

    def bring(piece, half, x_from, slice_in_x, parity):
        where = (4 * x_from + 2 * slice_in_x + parity) * SLICE
        copy = pltpu.make_async_copy(
            piece.at[pl.ds(half * SLICE, SLICE), :],
            kv_ref.at[pl.ds(pl.multiple_of(where, SLICE), SLICE), :],
            sems.at[len(copies)],
        )
        copy.start()
        copies.append(copy)

    for side in range(2):
        parity = core if side == 0 else 1 - core
        own, before, after, far_first, far_second = pieces[5 * side : 5 * side + 5]
        for half in range(2):
            bring(own, half, x, half, parity)
            bring(before, half, lax.rem(x + 3, 4), half, parity)
            bring(after, half, lax.rem(x + 1, 4), half, parity)
        bring(far_first, 0, lax.rem(x + 2, 4), 0, parity)
        bring(far_second, 0, lax.rem(x + 2, 4), 1, parity)
    qt_ref[...] = q_ref[...].T
    vt_ref[HEAD_DIM:, :] = jnp.ones((16, vt_ref.shape[1]), BF16)
    for copy in copies:
        copy.wait()

    @pl.loop(0, 16)
    def _(i):
        rows = pl.ds(pl.multiple_of(i * SLICE, SLICE), SLICE)
        vt_ref[:HEAD_DIM, rows] = kv_ref[rows, :].T[HEAD_DIM:, :]

    parts = 2
    wide = FWD_Q // parts
    for tile in range(2 * SLICE // FWD_Q):
        spans = [pl.ds(tile * FWD_Q + j * wide, wide) for j in range(parts)]
        queries = [qt_ref[:, span] for span in spans]
        ends = [end_ref[:, span] for span in spans]

        def step(masked, at, carry):
            rows = pl.ds(pl.multiple_of(at * FWD_K, FWD_K), FWD_K)
            kv, vt = kv_ref[rows, :], vt_ref[:, rows]
            scores = [matmul(kv, query) for query in queries]
            after = []
            for (top, total), score, end in zip(carry, scores, ends):
                if masked:
                    place = at * FWD_K + lax.broadcasted_iota(jnp.int32, score.shape, 0)
                    score = jnp.where(place < end, score, MASKED)
                new_top = jnp.maximum(top, jnp.max(score, axis=0, keepdims=True))
                weights = jnp.exp2(score * TO_LOG2 - new_top * TO_LOG2)
                factor = jnp.exp2((top - new_top) * TO_LOG2)
                total = total * factor + matmul(vt, weights.astype(BF16))
                after.append((new_top, total))
            return tuple(after)

        start = (jnp.full((1, wide), MASKED, F32), jnp.zeros((HEAD_DIM + 16, wide), F32))
        full, last = spot[2 + 2 * tile], spot[3 + 2 * tile]
        carry = lax.fori_loop(0, full, functools.partial(step, False), (start,) * parts)
        carry = lax.fori_loop(full, last, functools.partial(step, True), carry)
        for (top, total), span in zip(carry, spans):
            weight_sum = total[HEAD_DIM : HEAD_DIM + 1]
            mixed = total[:HEAD_DIM] / weight_sum
            out_t[:, span] = mixed
            out[span, :] = mixed.T.astype(BF16)
            lse_ref[:, span] = top * TO_LOG2 + jnp.log2(weight_sum)


def attention_forward(spot, padded_q, end, pieces):
    rows, total = 2 * SLICE, 16 * SLICE
    whole = pl.BlockSpec(memory_space=pltpu.VMEM)
    return pl.pallas_call(
        forward_kernel,
        out_shape=[
            jax.ShapeDtypeStruct((HEAD_DIM, rows), F32),
            jax.ShapeDtypeStruct((rows, HEAD_DIM), BF16),
            jax.ShapeDtypeStruct((1, rows), F32),
            jax.ShapeDtypeStruct((total, 2 * HEAD_DIM), BF16),
        ],
        in_specs=[pl.BlockSpec(memory_space=pltpu.SMEM), whole, whole]
        + [pl.BlockSpec(memory_space=pl.ANY)] * 10,
        out_specs=[whole] * 4,
        scratch_shapes=[
            pltpu.VMEM((HEAD_DIM + 16, total), BF16),
            pltpu.VMEM((2 * HEAD_DIM, rows), BF16),
            pltpu.SemaphoreType.DMA((16,)),
        ],
        compiler_params=pltpu.CompilerParams(vmem_limit_bytes=40 << 20),
        cost_estimate=pl.CostEstimate(
            flops=40_000_000_000, bytes_accessed=9 << 20, transcendentals=16 << 20
        ),
        name="attention_forward",
    )(spot, padded_q, end, *pieces)


def backward_kernel(spot, qdo_ref, out_t, lse_ref, end_ref, kv_ref, dq_ref, own_ref, other_ref, *rest):
    kt_ref, q_ref, do_ref, qt_ref, dot_ref, sum_ref = rest
    core = spot[1]
    first = lax.broadcasted_iota(jnp.int32, qdo_ref.shape, 1) < HEAD_DIM
    both = qdo_ref[...]
    none = jnp.zeros_like(both)
    q_ref[...] = jnp.where(first, both, none)
    do_ref[...] = jnp.where(first, none, both)
    qt_ref[...] = q_ref[...].T
    dot_ref[...] = do_ref[...].T

    @pl.loop(0, 16)
    def _(i):
        rows = pl.ds(pl.multiple_of(i * SLICE, SLICE), SLICE)
        kt_ref[:, rows] = kv_ref[rows, :].T[:HEAD_DIM, :]
        sum_ref[rows, :] = jnp.zeros((SLICE, 2 * HEAD_DIM), F32)

    for tile in range(2 * SLICE // BWD_Q):
        span = pl.ds(tile * BWD_Q, BWD_Q)
        query_t, grad_t = qt_ref[:, span], dot_ref[:, span]
        query, grad = q_ref[span, :], do_ref[span, :]
        end, lse = end_ref[:, span], lse_ref[:, span]
        delta = jnp.sum(out_t[:, span] * grad_t[HEAD_DIM:].astype(F32), axis=0, keepdims=True)

        def step(masked, at, grad_query):
            rows = pl.ds(pl.multiple_of(at * BWD_K, BWD_K), BWD_K)
            kv = kv_ref[rows, :]
            weights = jnp.exp2(matmul(kv, query_t) * TO_LOG2 - lse)
            if masked:
                place = at * BWD_K + lax.broadcasted_iota(jnp.int32, weights.shape, 0)
                weights = jnp.where(place < end, weights, 0.0)
            grad_scores = (weights * (matmul(kv, grad_t) - delta)).astype(BF16)
            sum_ref[rows, :] += matmul(weights.astype(BF16), grad) + matmul(grad_scores, query)
            return grad_query + matmul(kt_ref[:, rows], grad_scores)

        full, last = spot[2 + 2 * tile], spot[3 + 2 * tile]
        grad_query = jnp.zeros((HEAD_DIM, BWD_Q), F32)
        grad_query = lax.fori_loop(0, full, functools.partial(step, False), grad_query)
        grad_query = lax.fori_loop(full, last, functools.partial(step, True), grad_query)
        dq_ref[span, :] = (grad_query * HEAD_DIM ** (-0.5)).T.astype(BF16)

    is_key = lax.broadcasted_iota(jnp.int32, (1, 2 * HEAD_DIM), 1) < HEAD_DIM
    scale = jnp.where(is_key, HEAD_DIM ** (-0.5), 1.0)

    @pl.loop(0, 8)
    def _(i):
        to = pl.ds(pl.multiple_of(i * SLICE, SLICE), SLICE)
        for ref, parity in ((own_ref, core), (other_ref, 1 - core)):
            rows = pl.ds(pl.multiple_of((2 * i + parity) * SLICE, SLICE), SLICE)
            ref[to, :] = (sum_ref[rows, :] * scale).astype(BF16)


def attention_backward(spot, queries_grads, out_t, lse, end, kv):
    rows, total, wide = 2 * SLICE, 16 * SLICE, 2 * HEAD_DIM
    whole = pl.BlockSpec(memory_space=pltpu.VMEM)
    return pl.pallas_call(
        backward_kernel,
        out_shape=[
            jax.ShapeDtypeStruct((rows, HEAD_DIM), BF16),
            jax.ShapeDtypeStruct((total // 2, wide), BF16),
            jax.ShapeDtypeStruct((total // 2, wide), BF16),
        ],
        in_specs=[pl.BlockSpec(memory_space=pltpu.SMEM)] + [whole] * 5,
        out_specs=[whole] * 3,
        scratch_shapes=[
            pltpu.VMEM((HEAD_DIM, total), BF16),
            pltpu.VMEM((rows, wide), BF16),
            pltpu.VMEM((rows, wide), BF16),
            pltpu.VMEM((wide, rows), BF16),
            pltpu.VMEM((wide, rows), BF16),
            pltpu.VMEM((total, wide), F32),
        ],
        compiler_params=pltpu.CompilerParams(vmem_limit_bytes=48 << 20),
        cost_estimate=pl.CostEstimate(
            flops=60_000_000_000, bytes_accessed=9 << 20, transcendentals=16 << 20
        ),
        name="attention_backward",
    )(spot, queries_grads, out_t, lse, end, kv)


def all_ids(block_ids, place):
    table = jnp.zeros((16, SLICE), jnp.int32)
    table = lax.dynamic_update_slice(table, block_ids[None], (place, 0))
    table = table + swap(table, "co")
    table = table + swap(table, "zl")
    table = table + lax.ppermute(table, "x", [(i, i ^ 1) for i in range(4)])
    return table + lax.ppermute(table, "x", [(i, i ^ 2) for i in range(4)])


def tile_bounds(end, query_tile, key_tile):
    ends = end.reshape(-1, query_tile)
    return jnp.stack([ends[:, 0] // key_tile, (ends[:, -1] + key_tile - 1) // key_tile], axis=1)


def core_half(parts, core):
    kept = lax.dynamic_index_in_dim(parts, core, 1, False)
    sent = lax.dynamic_index_in_dim(parts, 1 - core, 1, False)
    return kept.astype(F32) + swap(sent, "co").astype(F32)


def zh_half(parts, zh):
    parts = parts.astype(BF16)
    kept = lax.dynamic_index_in_dim(parts, zh, 0, False)
    sent = lax.dynamic_index_in_dim(parts, 1 - zh, 0, False)
    return (kept.astype(F32) + swap(sent, "zh").astype(F32)).astype(BF16)


def on_device(
    tokens,
    block_ids,
    ln1_gain,
    ln1_shift,
    qkv_weight,
    qv_bias,
    out_weight,
    out_bias,
    ln2_gain,
    ln2_shift,
    up_weight,
    up_bias,
    down_weight,
    down_bias,
    cotangent,
):
    x, zl, core, zh = (lax.axis_index(name) for name in ("x", "zl", "co", "zh"))
    width = tokens.shape[1]

    qkv_pair = in_order(qkv_weight, swap(qkv_weight, "zh"), zh)
    bias_pair = in_order(qv_bias, swap(qv_bias, "zh"), zh).astype(F32)
    up_pair = lax.all_gather(up_weight, "zh", axis=0)
    down_pair = lax.all_gather(down_weight, "zh", axis=0, tiled=True)
    up_bias_pair = in_order(up_bias, swap(up_bias, "zh"), zh).astype(F32).reshape(-1)
    out_whole = lax.all_gather(out_weight, ("y", "zh"), axis=0, tiled=True)
    cotangent_all = lax.all_gather(cotangent, "y", axis=0, tiled=True)

    by_head = qkv_pair.reshape(2, width, 3, 2, HEAD_DIM)
    kv_cols = jnp.stack([by_head[:, :, 1], by_head[:, :, 2]], axis=3)
    kv_cols = kv_cols.transpose(1, 2, 0, 3, 4).reshape(width, 512)
    q_cols = by_head[:, :, 0].transpose(1, 2, 0, 3).reshape(width, 256)
    flat_qkv = jnp.concatenate([kv_cols, q_cols], axis=1)
    bias_heads = bias_pair.reshape(2, 2, 2, HEAD_DIM).transpose(1, 2, 0, 3)
    kv_bias = jnp.stack([jnp.zeros_like(bias_heads[1]), bias_heads[1]], axis=2).reshape(512)
    flat_bias = jnp.concatenate([kv_bias, bias_heads[0].reshape(256)])

    table = all_ids(block_ids, 4 * x + 2 * zl + core)
    counts = jnp.sum(
        (table.reshape(-1)[None, :] <= jnp.arange(128, dtype=jnp.int32)[:, None]).astype(jnp.int32),
        axis=1,
    )
    early = lax.dynamic_index_in_dim(table, 4 * x + core, 0, False)
    late = lax.dynamic_index_in_dim(table, 15 - 4 * x - core, 0, False)
    query_ids = jnp.concatenate([early, late])
    same = query_ids[None, :] == jnp.arange(128, dtype=jnp.int32)[:, None]
    end = jnp.sum(jnp.where(same, counts[:, None], 0), axis=0)
    spot = jnp.stack([x, core]).astype(jnp.int32)
    forward_spot = jnp.concatenate([spot, tile_bounds(end, FWD_Q, FWD_K).reshape(-1)])
    backward_spot = jnp.concatenate([spot, tile_bounds(end, BWD_Q, BWD_K).reshape(-1)])
    end = end[None, :]

    gain_one, shift_one = ln1_gain.astype(F32), ln1_shift.astype(F32)
    tokens_all = gather_y(tokens).astype(F32)
    centered = tokens_all - jnp.mean(tokens_all, axis=-1, keepdims=True)
    spread = lax.rsqrt(jnp.mean(centered * centered, axis=-1, keepdims=True) + EPSILON)
    unit_all = centered * spread
    normed_all = (unit_all * gain_one + shift_one).astype(BF16)
    projected = (matmul(normed_all, flat_qkv) + flat_bias).astype(BF16)
    kv_blocks = projected[:, :512].reshape(512, 4, 128).transpose(1, 0, 2)
    q_blocks = projected[:, 512:].reshape(512, 4, HEAD_DIM).transpose(1, 0, 2)
    mine = exchange(jnp.concatenate([kv_blocks, pack(q_blocks)], axis=1), ("zl", "zh"))
    queries = from_z(unpack(mine[:, 512:]))
    queries = jnp.concatenate([queries[0], mirror(queries[1])], axis=0)
    kv_own = from_z(mine[:, :512]).reshape(2 * SLICE, 128)

    before, after = shift(kv_own, "x", 1), shift(kv_own, "x", -1)
    far_first, far_second = shift(before[:SLICE], "x", 1), shift(after[SLICE:], "x", -1)
    pieces = [kv_own, before, after, far_first, far_second]
    pieces += [swap(piece, "co") for piece in pieces]
    padded = jnp.pad(queries, ((0, 0), (0, HEAD_DIM)))
    out_t, mixed, lse, kv = attention_forward(forward_spot, padded, end, pieces)

    mixed = jnp.stack([mixed[:SLICE], mirror(mixed[SLICE:])])
    by_z = unpack(exchange(pack(to_z(mixed)), ("zl", "zh")))
    attended_all = (
        by_z.reshape(2, 2, 512, HEAD_DIM).transpose(2, 1, 0, 3).reshape(512, 256)
    )
    attended = exchange(attended_all.reshape(4, 128, 256), "y")
    branch = lax.dot_general(
        attended,
        out_whole.reshape(4, 256, width),
        (((0, 2), (0, 1)), ((), ())),
        preferred_element_type=F32,
    )
    resid = tokens.astype(F32) + branch + out_bias.astype(F32)
    normed_mid, norm_two_back = jax.vjp(
        layer_norm, resid, ln2_gain.astype(F32), ln2_shift.astype(F32)
    )

    mid_all = gather_y(normed_mid.astype(BF16))
    up_cols = up_pair.transpose(1, 0, 2).reshape(width, 1024)
    hidden = matmul(mid_all, up_cols) + up_bias_pair
    active_wide, gelu_back = jax.vjp(gelu_tanh, hidden)
    active = active_wide.astype(BF16)
    grad_active = contract(cotangent_all, down_pair, 1, 1)
    grad_hidden = gelu_back(grad_active)[0].astype(BF16)
    grad_mid = scatter_y(contract(grad_hidden, up_cols, 1, 1))
    down_partial = matmul(active, down_pair).astype(BF16)
    down_sum = lax.psum_scatter(down_partial, "y", scatter_dimension=0, tiled=True)
    output = resid + down_sum.astype(F32) + down_bias.astype(F32)
    grad_down = contract(active, cotangent_all, 0, 0)
    grad_up = contract(mid_all, grad_hidden, 0, 0)
    grad_up_bias = jnp.sum(grad_hidden.astype(F32), axis=0)

    grad_resid_norm, grad_ln2_gain, grad_ln2_shift = norm_two_back(grad_mid)
    grad_resid = cotangent.astype(F32) + grad_resid_norm
    grad_branch = grad_resid.astype(BF16)
    grad_branch_all = lax.all_gather(grad_branch, "y", axis=0, tiled=True)

    grad_down = core_half(grad_down.astype(BF16).reshape(2, 2, 256, width), core)
    grad_up = grad_up.astype(BF16).reshape(2, 512, 2, 512).transpose(2, 0, 1, 3)
    grad_up = core_half(grad_up, core)
    grad_down, grad_up = zh_half(grad_down, zh), zh_half(grad_up, zh)
    grad_down, grad_up = lax.psum((grad_down, grad_up), ("x", "zl"))

    grad_attended = contract(grad_branch, out_whole, 1, 1).astype(BF16)
    grad_y = exchange(grad_attended.reshape(128, 4, 256).transpose(1, 0, 2), "y")
    grad_z = grad_y.reshape(512, 2, 2, HEAD_DIM).transpose(2, 1, 0, 3).reshape(4, 512, HEAD_DIM)
    grad_mixed = from_z(unpack(exchange(pack(grad_z), ("zl", "zh"))))
    grad_mixed = jnp.concatenate([grad_mixed[0], mirror(grad_mixed[1])], axis=0)
    queries_grads = jnp.concatenate([queries, grad_mixed], axis=1)
    grad_q, grad_kv, grad_kv_other = attention_backward(
        backward_spot, queries_grads, out_t, lse, end, kv
    )
    grad_q = jnp.stack([grad_q[:SLICE], mirror(grad_q[SLICE:])])
    grad_kv = (grad_kv.astype(F32) + swap(grad_kv_other, "co").astype(F32)).astype(BF16)
    grad_kv = exchange(grad_kv.reshape(4, 2 * SLICE, 128), "x").astype(F32)
    grad_kv = jnp.sum(grad_kv, axis=0).astype(BF16).reshape(2, SLICE, 128)
    blocks = jnp.concatenate([to_z(grad_kv), pack(to_z(grad_q))], axis=1)
    blocks = exchange(blocks, ("zl", "zh"))
    grad_projected = jnp.concatenate(
        [
            blocks[:, :512].transpose(1, 0, 2).reshape(512, 512),
            unpack(blocks[:, 512:]).transpose(1, 0, 2).reshape(512, 256),
        ],
        axis=1,
    )
    grad_normed_part = contract(grad_projected, flat_qkv, 1, 1)
    grad_qkv = contract(normed_all, grad_projected, 0, 0)
    grad_bias = jnp.sum(grad_projected.astype(F32), axis=0)
    grad_out = contract(attended_all, grad_branch_all, 0, 0)
    part_gain = jnp.sum(grad_normed_part * unit_all, axis=0)
    part_shift = jnp.sum(grad_normed_part, axis=0)
    grad_normed = scatter_y(grad_normed_part)
    _, norm_one_back = jax.vjp(
        lambda v: layer_norm(v, gain_one, shift_one), tokens.astype(F32)
    )
    grad_tokens = grad_resid + norm_one_back(grad_normed)[0]

    kv_bias_grad = grad_bias[:512].reshape(2, 2, 2, HEAD_DIM)[:, :, 1]
    q_bias_grad = grad_bias[512:].reshape(2, 2, HEAD_DIM)
    bias_grad = jnp.stack([q_bias_grad, kv_bias_grad]).transpose(2, 0, 1, 3).reshape(512)
    quarter = 0.25 * jnp.sum(cotangent_all.astype(F32), axis=0)
    rows = [
        part_gain,
        part_shift,
        jnp.sum(grad_resid, axis=0),
        grad_ln2_gain,
        grad_ln2_shift,
        quarter,
        grad_up_bias,
        jnp.pad(bias_grad, (0, 512)),
    ]
    small = jnp.stack(rows)
    for axis in ("co", "zl", "zh"):
        small = small + swap(small, axis)
    for step in (1, 2):
        small = small + lax.ppermute(small, "x", [(i, i ^ step) for i in range(4)])
    tall = small[:6]
    for step in (1, 2):
        tall = tall + lax.ppermute(tall, "y", [(i, i ^ step) for i in range(4)])
    grad_up_bias = lax.dynamic_slice_in_dim(small[6], zh * 512, 512, 0)
    grad_qv_bias = lax.dynamic_slice_in_dim(small[7], zh * 256, 256, 0).reshape(2, 128)

    qkv_kv = grad_qkv[:, :512].reshape(2, 512, 2, 2, 2, HEAD_DIM)
    qkv_q = grad_qkv[:, 512:].reshape(2, 512, 2, 2, HEAD_DIM)
    qkv_all = jnp.concatenate([qkv_q[:, :, :, :, None], qkv_kv], axis=4).astype(BF16)
    qkv_all = qkv_all.transpose(3, 0, 4, 1, 2, 5).reshape(2, 2, 1536, 128)
    out_all = grad_out.astype(BF16).reshape(2, 2, 64, 8, 128).transpose(0, 1, 3, 2, 4)
    rest = jnp.concatenate([qkv_all, out_all.reshape(2, 2, 512, 128)], axis=2)
    rest = zh_half(core_half(rest, core), zh)
    shares = exchange(rest.reshape(8, 256, 128), ("x", "zl"))
    share = jnp.sum(shares.astype(F32), axis=0).astype(BF16)
    rest = exchange(jnp.broadcast_to(share[None], (8, 256, 128)), ("x", "zl"))
    rest = in_order(rest, swap(rest, "co"), core).reshape(2, 2048, 128).astype(F32)
    grad_qkv_weight = rest[:, :1536].reshape(2, 3, 512, 128).transpose(0, 2, 1, 3)
    grad_qkv_weight = grad_qkv_weight.reshape(width, 3, 128)
    grad_out_weight = rest[:, 1536:].reshape(2, 8, 64, 128).transpose(0, 2, 1, 3)
    grad_out_weight = grad_out_weight.reshape(128, width)
    grad_down_weight = in_order(grad_down, swap(grad_down, "co"), core)
    grad_down_weight = grad_down_weight.reshape(512, width).astype(F32)
    grad_up_weight = in_order(grad_up, swap(grad_up, "co"), core)
    grad_up_weight = grad_up_weight.reshape(width, 512).astype(F32)
    return (
        output,
        grad_tokens,
        tall[0],
        tall[1],
        grad_qkv_weight,
        grad_qv_bias,
        grad_out_weight,
        tall[2],
        tall[3],
        tall[4],
        grad_up_weight,
        grad_up_bias,
        grad_down_weight,
        tall[5],
    )


def solution(mesh):
    fine = Mesh(mesh.devices.reshape(4, 2, 2, 4, 2), AXES)
    slices, shards = ("x", "zl", "co"), ("y", "zh")
    return jax.shard_map(
        on_device,
        mesh=fine,
        in_specs=(
            P(AXES, None),
            P(slices),
            P(),
            P(),
            P(None, None, shards),
            P(None, shards),
            P(shards, None),
            P(),
            P(),
            P(),
            P(None, shards),
            P(shards),
            P(shards, None),
            P(),
            P(AXES, None),
        ),
        out_specs=(
            P(AXES, None),
            P(AXES, None),
            P(),
            P(),
            P(None, None, shards),
            P(None, shards),
            P(shards, None),
            P(),
            P(),
            P(),
            P(None, shards),
            P(shards),
            P(shards, None),
            P(),
        ),
        check_vma=False,
    )
```

```python
import functools

import jax
import jax.numpy as jnp
from jax import lax
from jax.experimental import pallas as pl
from jax.experimental.pallas import tpu as pltpu
from jax.sharding import Mesh
from jax.sharding import PartitionSpec as P

HEAD_DIM = 64
EPSILON = 1e-05
MASKED = -1e30
LOG2E = 1.4426950408889634
TO_LOG2 = LOG2E * HEAD_DIM ** (-0.5)
AXES = ("x", "zl", "co", "y", "zh")
BF16, F32 = jnp.bfloat16, jnp.float32
SLICE = 1024
FWD_Q, FWD_K = 1024, 1024
BWD_Q = 1024


def contract(left, right, left_dim, right_dim):
    return lax.dot_general(
        left, right, (((left_dim,), (right_dim,)), ((), ())), preferred_element_type=F32
    )


def matmul(left, right):
    return contract(left, right, 1, 0)


def shift(values, steps):
    return lax.ppermute(values, "y", [(i, (i + steps) % 4) for i in range(4)])


def hop(values, bit, axis="x"):
    return lax.ppermute(values, axis, [(i, i ^ bit) for i in range(4)])


def swap(values, axis):
    return lax.ppermute(values, axis, [(0, 1), (1, 0)])


def to_mirror(rows, zl):
    moved = lax.ppermute(rows, ("x", "zl"), [(i, 8 - i) for i in (1, 3, 5, 7)])
    return jnp.where(zl == 0, rows, moved)


def exchange(blocks, axes):
    return lax.all_to_all(blocks, axes, 0, 0, tiled=True)


def gather(rows, axes, size):
    return exchange(jnp.broadcast_to(rows[None], (size,) + rows.shape), axes)


def gather_y(rows):
    one, three = shift(rows, 1), shift(rows, 3)
    return rows, one, shift(rows, 2), three


def send_y(blocks):
    return blocks[0], shift(blocks[1], -1), shift(blocks[3], -3), shift(blocks[2], -2)


def total(parts):
    return functools.reduce(jnp.add, [part.astype(F32) for part in parts])


def after(value, *others):
    return lax.optimization_barrier((value, others))[0]


def turned(values, dim, index):
    return jnp.where(index == 0, values, jnp.flip(values, dim))


def halves(values, dim, index):
    half = values.shape[dim] // 2
    return (
        lax.dynamic_slice_in_dim(values, index * half, half, dim),
        lax.dynamic_slice_in_dim(values, (1 - index) * half, half, dim),
    )


def to_z(rows):
    n = rows.shape[-1]
    return rows.reshape(2, 4, 2, 128, n).transpose(0, 2, 1, 3, 4).reshape(4, 512, n)


def on_core(kernel, name, outputs, operands, flops, limit=32, scratch=()):
    whole = pl.BlockSpec(memory_space=pltpu.VMEM)
    outputs = [jax.ShapeDtypeStruct(shape, dtype) for shape, dtype in outputs]
    return pl.pallas_call(
        kernel,
        out_shape=outputs,
        in_specs=[pl.BlockSpec(memory_space=pltpu.SMEM)] + [whole] * (len(operands) - 1),
        out_specs=[whole] * len(outputs),
        scratch_shapes=list(scratch),
        compiler_params=pltpu.CompilerParams(vmem_limit_bytes=limit << 20),
        cost_estimate=pl.CostEstimate(flops=flops, bytes_accessed=4 << 20, transcendentals=0),
        name=name,
    )(*operands)


def joined(refs, dim=0):
    return jnp.concatenate([ref[...] for ref in refs], axis=dim)


def unit_rows(rows):
    centered = rows - jnp.mean(rows, axis=-1, keepdims=True)
    scale = lax.rsqrt(jnp.mean(centered * centered, axis=-1, keepdims=True) + EPSILON)
    return centered * scale, scale


def norm_back(grad, unit, scale, gain):
    grad = grad * gain
    along = jnp.mean(grad * unit, axis=-1, keepdims=True)
    return scale * (grad - jnp.mean(grad, axis=-1, keepdims=True) - unit * along)


def y_rows(place, steps):
    return pl.ds(pl.multiple_of(((place[3] - steps) & 3) * 128, 128), 128)


def merge_lanes(left, right):
    left, right = left.astype(F32), right.astype(F32)
    first = lax.broadcasted_iota(jnp.int32, left.shape, 1) < HEAD_DIM
    return (
        jnp.where(first, left, pltpu.roll(right, HEAD_DIM, 1)).astype(BF16),
        jnp.where(first, pltpu.roll(left, HEAD_DIM, 1), right).astype(BF16),
    )


def project_kernel(place, *refs):
    pieces, (gain, bent, own, near, far, own_bias, pair_bias) = refs[:4], refs[4:11]
    blocks, normed_ref, unit_ref = refs[11:]
    core, zh = place[2], place[4]
    for steps, piece in enumerate(pieces):
        rows = y_rows(place, steps)
        unit, _ = unit_rows(piece[...].astype(F32))
        unit_ref[rows, :] = unit.astype(BF16)
        normed_ref[rows, :] = (unit * gain[...] + bent[...]).astype(BF16)
    normed = normed_ref[...]
    first = normed_ref[:, pl.ds(pl.multiple_of(core * 512, 512), 512)]
    second = normed_ref[:, pl.ds(pl.multiple_of((1 - core) * 512, 512), 512)]
    for pair in range(2):
        bias = (pair_bias if pair else own_bias)[...].astype(F32)

        def projected(i, pair=pair):
            if pair:
                return matmul(first, near[i]) + matmul(second, far[i])
            return matmul(normed, own[i])

        queries = (projected(0) + bias[:1]).T.astype(BF16)
        mixed = merge_lanes(projected(1).astype(BF16), (projected(2) + bias[1:]).astype(BF16))
        for head in range(2):
            where = 2 * head + (zh ^ pair)
            blocks[where, pl.ds(0, 512), :] = mixed[head]
            for y in range(4):
                lanes = slice(y * 128, y * 128 + 128)
                piece = queries[head * HEAD_DIM : head * HEAD_DIM + HEAD_DIM, lanes]
                blocks[where, pl.ds(512 + y * HEAD_DIM, HEAD_DIM), :] = piece


def project_back_kernel(place, blocks, unit_ref, own, near, far, *refs):
    outs, sums, grad_ref = refs[:4], refs[4], refs[5]
    core, zh = place[2], place[4]
    for pair in range(2):
        heads = [blocks[2 * head + (zh ^ pair)] for head in range(2)]
        keys, values = merge_lanes(heads[0][:512], heads[1][:512])
        queries = [
            jnp.concatenate([head[512 + y * HEAD_DIM :][:HEAD_DIM] for y in range(4)], axis=1)
            for head in heads
        ]
        parts = (jnp.concatenate(queries, axis=0).T, keys, values)

        def back(weight, parts=parts):
            return functools.reduce(
                jnp.add, [contract(part, weight[i], 1, 1) for i, part in enumerate(parts)]
            )

        if pair:
            first = pl.ds(pl.multiple_of(core * 512, 512), 512)
            second = pl.ds(pl.multiple_of((1 - core) * 512, 512), 512)
            grad_ref[:, first] += back(near)
            grad_ref[:, second] += back(far)
        else:
            grad_ref[...] = back(own)
    grad = grad_ref[...]
    sums[...] = jnp.concatenate(
        [
            jnp.sum(grad * unit_ref[...].astype(F32), axis=0, keepdims=True),
            jnp.sum(grad, axis=0, keepdims=True),
        ]
    )
    for steps, out in enumerate(outs):
        out[...] = grad_ref[y_rows(place, steps), :].astype(BF16)


def qkv_grads_kernel(place, blocks_ref, normed_ref, grad_ref, sums_ref):
    normed, ones = normed_ref[...], jnp.ones((512, 128), BF16)
    for head in range(2):
        for zh in range(2):
            block = blocks_ref[2 * head + zh]
            queries = [block[512 + y * HEAD_DIM :][:HEAD_DIM] for y in range(4)]
            left = jnp.concatenate([block[:512].T, jnp.concatenate(queries, axis=1)], axis=0)
            grad = matmul(left, normed)
            for chunk in range(8):
                piece = grad[:, chunk * 128 : chunk * 128 + 128].astype(BF16)
                grad_ref[place[2] ^ (chunk // 4), chunk % 4, head, zh] = piece
            sums_ref[2 * head + zh] = matmul(left, ones)


def attend_out_kernel(place, heads, kept, sent, tokens, bias, gain, bent, resid_ref, mid_ref, att_ref):
    core, y, zh = place[2], place[3], place[4]
    for side in range(2):
        for steps in range(4):
            for pair in range(2):
                where = 8 * (core ^ side) + 2 * ((y - steps) & 3) + (zh ^ pair)
                att_ref[side, pl.ds(steps * 128 + pair * HEAD_DIM, HEAD_DIM), :] = heads[where]
    branch = matmul(att_ref[0].T, kept[...]) + matmul(att_ref[1].T, sent[...])
    resid = tokens[...].astype(F32) + branch + bias[...]
    resid_ref[...] = resid
    mid_ref[...] = (unit_rows(resid)[0] * gain[...] + bent[...]).astype(BF16)


def mid_back_kernel(place, *refs):
    parts, resid, cotangent, gain, kept, sent = refs[:6]
    grad_resid_ref, branch_ref, heads, sums = refs[6:]
    core, y, zh = place[2], place[3], place[4]
    grad = total([parts[i] for i in range(4)])
    unit, scale = unit_rows(resid[...])
    cot = cotangent[...].astype(F32)
    grad_resid = cot + norm_back(grad, unit, scale, gain[...])
    grad_resid_ref[...] = grad_resid
    branch = grad_resid.astype(BF16)
    branch_ref[...] = branch
    rows = [grad_resid, grad * unit, grad, cot]
    sums[...] = jnp.concatenate([jnp.sum(row, axis=0, keepdims=True) for row in rows])
    for side, weight in enumerate((kept, sent)):
        grads = contract(weight[...], branch, 1, 1).astype(BF16)
        for steps in range(4):
            for pair in range(2):
                where = 8 * (core ^ side) + 2 * ((y - steps) & 3) + (zh ^ pair)
                start = steps * 128 + pair * HEAD_DIM
                heads[where] = grads[start : start + HEAD_DIM]


def feed_forward_kernel(place, *refs):
    mids, cots, (bias,), ups, downs = refs[:4], refs[4:8], refs[8:9], refs[9:13], refs[13:17]
    active_ref, grad_ref, out, bias_grad = refs[17:]
    mid, cot = joined(mids), jnp.concatenate([ref[:128, :] for ref in cots])
    summed = None
    for i, (up_ref, down_ref) in enumerate(zip(ups, downs)):
        span = pl.ds(i * 256, 256)
        up = up_ref[...]
        hidden = matmul(mid, up) + bias[:, span]
        square = hidden * hidden
        bent = jnp.tanh(0.7978845608028654 * hidden * (1.0 + 0.044715 * square))
        active_ref[:, span] = (0.5 * hidden * (1.0 + bent)).astype(BF16)
        slope = 0.7978845608028654 * (1.0 + 3.0 * 0.044715 * square)
        slope = 0.5 * (1.0 + bent) + 0.5 * hidden * (1.0 - bent * bent) * slope
        grad = (slope * contract(cot, down_ref[...], 1, 1)).astype(BF16)
        grad_ref[:, span] = grad
        bias_grad[:, span] = jnp.sum(grad.astype(F32), axis=0, keepdims=True)
        part = contract(grad, up, 1, 1)
        summed = part if summed is None else summed + part
    for steps in range(4):
        piece = summed[steps * 128 : steps * 128 + 128].astype(BF16)
        out[(place[3] - steps) & 3] = piece


def unit_grads_kernel(kept, place, *refs):
    mids, cots, active, grad = refs[:4], refs[4:8], refs[8], refs[9]
    got, out = (refs[10], refs[11]) if kept else (None, refs[10])
    span = pl.ds(0 if kept else 512, 512)
    cot = jnp.concatenate([ref[:128, :] for ref in cots])
    for i, (left, right) in enumerate(((cot, active), (joined(mids), grad))):
        summed = contract(left, right[:, span], 0, 0)
        for share in range(8):
            block = summed[share * 128 : share * 128 + 128]
            if kept:
                block = (block + got[share, i].astype(F32)).astype(BF16)
                for pair in range(2):
                    half = block[:, pair * 256 : pair * 256 + 256]
                    out[2 * share + (place[4] ^ pair), pl.ds(i * 128, 128), :] = half
            else:
                out[share, i] = block.astype(BF16)


def out_down_kernel(place, att, branch, active, *refs):
    downs, outs = refs[:4], refs[4:]
    grads = [matmul(att[side], branch[...]).astype(BF16) for side in range(2)]
    down = total([matmul(active[:, i * 256 : i * 256 + 256], ref[...]) for i, ref in enumerate(downs)])
    for steps, out in enumerate(outs):
        rows = slice(steps * 128, steps * 128 + 128)
        out[pl.ds(0, 128), :] = grads[0][rows]
        out[pl.ds(128, 128), :] = grads[1][rows]
        out[pl.ds(256, 128), :] = down[rows].astype(BF16)


def out_sums_kernel(place, *refs):
    parts, (resid, bias, grad_resid, home, kept, sent) = refs[:4], refs[4:]
    home[0] = total([part[256:, :] for part in parts]) + resid[...] + bias[...]
    home[1] = grad_resid[...]
    for side, ref in enumerate((kept, sent)):
        summed = total([part[side * 128 : side * 128 + 128, :] for part in parts]).astype(ref.dtype)
        for pair in range(2):
            for share in range(8):
                lanes = slice(share * 128, share * 128 + 128)
                piece = summed[pair * HEAD_DIM : pair * HEAD_DIM + HEAD_DIM, lanes]
                ref[share // 2, share % 2, pair] = piece


def shares_kernel(place, heads, head_got, out, out_got, small, shares):
    for x in range(4):
        for zl in range(2):
            share = 2 * x + zl
            for zh in range(2):
                to = 2 * share + zh
                grad = total([heads[0, x, zl, zh], head_got[x, zl, zh]])
                shares[to, pl.ds(0, 192), :] = grad.astype(BF16)
                grad = total([out[x, zl, zh], out_got[x, zl, zh]])
                shares[2 * share + (place[4] ^ zh), pl.ds(192, HEAD_DIM), :] = grad.astype(BF16)
                rows = small[:, share * 128 : share * 128 + 128]
                rows = jnp.concatenate([rows, jnp.zeros_like(rows)]).astype(BF16)
                shares[to, pl.ds(256, 16), :] = rows


def last_norm_kernel(place, *refs):
    parts, (tokens, gain, resid, out) = refs[:4], refs[4:]
    unit, scale = unit_rows(tokens[...].astype(F32))
    out[...] = resid[...] + norm_back(total([part[...] for part in parts]), unit, scale, gain[...])


def unit_weights_kernel(place, own, other, down, up):
    for side, ref in enumerate((own, other)):
        half = place[2] ^ side
        for share in range(8):
            lanes = pl.ds(share * 128, 128)
            down[pl.ds(pl.multiple_of(half * 256, 256), 256), lanes] = ref[share, :256].astype(F32)
            for part in range(2):
                lanes = pl.ds(pl.multiple_of(half * 256 + part * 128, 128), 128)
                piece = ref[share, pl.ds(256 + part * 128, 128), :].astype(F32)
                up[pl.ds(share * 128, 128), lanes] = piece


def head_weights_kernel(place, own, other, qkv, out):
    for side, ref in enumerate((own, other)):
        half = place[2] ^ side
        for x in range(4):
            rows = pl.ds(pl.multiple_of(half * 512 + x * 128, 128), 128)
            for i, which in enumerate((1, 2, 0)):
                span = pl.ds(i * HEAD_DIM, HEAD_DIM)
                both = jnp.concatenate([ref[2 * x, span, :], ref[2 * x + 1, span, :]])
                qkv[which, rows, :] = both.astype(F32).T
            for zl in range(2):
                piece = ref[2 * x + zl, pl.ds(192, HEAD_DIM), :].astype(F32)
                span = pl.ds(pl.multiple_of(half * HEAD_DIM, HEAD_DIM), HEAD_DIM)
                out[span, pl.ds((2 * x + zl) * 128, 128)] = piece


def forward_kernel(spot, q_ref, end_ref, *refs):
    pieces, (state_ref, out, kv_ref, vt_ref, qt_ref, sems) = refs[:14], refs[14:]
    x, core = spot[0], spot[1]
    copies = []

    def bring(piece, half, x_from, slice_in_x, parity):
        where = (4 * x_from + 2 * slice_in_x + parity) * SLICE
        copy = pltpu.make_async_copy(
            piece.at[pl.ds(half * SLICE, SLICE), :],
            kv_ref.at[pl.ds(pl.multiple_of(where, SLICE), SLICE), :],
            sems.at[len(copies)],
        )
        copy.start()
        copies.append(copy)

    for side in range(2):
        parity = core if side == 0 else 1 - core
        pieces_here = pieces[7 * side : 7 * side + 7]
        bring(pieces_here[0], 0, x, 0, parity)
        bring(pieces_here[0], 1, x, 1, parity)
        for i, piece in enumerate(pieces_here[1:]):
            bring(piece, 0, x ^ (1, 1, 3, 3, 2, 2)[i], i % 2, parity)
    qt_ref[HEAD_DIM:, :] = jnp.zeros((HEAD_DIM, 2 * SLICE), BF16)
    for chunk in range(16):
        qt_ref[:HEAD_DIM, pl.ds(chunk * 128, 128)] = q_ref[chunk]
    vt_ref[HEAD_DIM:, :] = jnp.ones((16, vt_ref.shape[1]), BF16)
    for copy in copies:
        copy.wait()

    def turn(i, largest):
        rows = pl.ds(pl.multiple_of(i * SLICE, SLICE), SLICE)
        both = kv_ref[rows, :].T
        vt_ref[:HEAD_DIM, rows] = both[HEAD_DIM:, :]
        keys = both[:HEAD_DIM, :].astype(F32)
        return jnp.maximum(largest, jnp.sum(keys * keys, axis=0, keepdims=True))

    longest = jnp.max(lax.fori_loop(0, 16, turn, jnp.zeros((1, SLICE), F32)))
    norms = qt_ref[:HEAD_DIM, :].astype(F32)
    norms = jnp.sum(norms * norms, axis=0, keepdims=True)
    limit = jnp.sqrt(norms * longest) * TO_LOG2
    level = limit - 90.0

    def finish(total, log_top, start, wide):
        span = pl.ds(start, wide)
        weight_sum = total[HEAD_DIM : HEAD_DIM + 1]
        mixed = total[:HEAD_DIM] / weight_sum
        state_ref[:HEAD_DIM, span] = mixed
        for chunk in range(wide // 128):
            piece = mixed[:, chunk * 128 : chunk * 128 + 128].astype(BF16)
            out[start // 128 + chunk] = piece
        state_ref[HEAD_DIM:, span] = jnp.broadcast_to(log_top + jnp.log2(weight_sum), (8, wide))

    def masked_at(values, begin, end, other):
        place = begin + lax.broadcasted_iota(jnp.int32, values.shape, 0)
        return jnp.where(place < end, values, other)

    def bounded_tile(tile):
        span = pl.ds(tile * FWD_Q, FWD_Q)
        query, end = qt_ref[:, span], end_ref[:, span]
        base = level[:, tile * FWD_Q : tile * FWD_Q + FWD_Q]

        def step(masked, at, total):
            for piece in range(2):
                begin = pl.multiple_of(at * FWD_K + piece * (FWD_K // 2), FWD_K // 2)
                rows = pl.ds(begin, FWD_K // 2)
                weights = jnp.exp2(matmul(kv_ref[rows, :], query) * TO_LOG2 - base)
                if masked:
                    weights = masked_at(weights, begin, end, 0.0)
                total = total + matmul(vt_ref[:, rows], weights.astype(BF16))
            return total

        total = jnp.zeros((HEAD_DIM + 16, FWD_Q), F32)
        full, last = spot[2 + 2 * tile], spot[3 + 2 * tile]
        total = lax.fori_loop(0, full, functools.partial(step, False), total)
        total = lax.fori_loop(full, last, functools.partial(step, True), total)
        finish(total, base, tile * FWD_Q, FWD_Q)

    def running_tile(tile):
        wide = FWD_Q // 2
        starts = [tile * FWD_Q, tile * FWD_Q + wide]
        queries = [qt_ref[:, pl.ds(start, wide)] for start in starts]
        ends = [end_ref[:, pl.ds(start, wide)] for start in starts]

        def step(masked, at, carry):
            rows = pl.ds(pl.multiple_of(at * FWD_K, FWD_K), FWD_K)
            kv, vt = kv_ref[rows, :], vt_ref[:, rows]
            scores = [matmul(kv, query) for query in queries]
            after = []
            for (top, total), score, end in zip(carry, scores, ends):
                if masked:
                    score = masked_at(score, at * FWD_K, end, MASKED)
                new_top = jnp.maximum(top, jnp.max(score, axis=0, keepdims=True))
                weights = jnp.exp2(score * TO_LOG2 - new_top * TO_LOG2)
                factor = jnp.exp2((top - new_top) * TO_LOG2)
                total = total * factor + matmul(vt, weights.astype(BF16))
                after.append((new_top, total))
            return tuple(after)

        begin = (jnp.full((1, wide), MASKED, F32), jnp.zeros((HEAD_DIM + 16, wide), F32))
        full, last = spot[2 + 2 * tile], spot[3 + 2 * tile]
        carry = lax.fori_loop(0, full, functools.partial(step, False), (begin, begin))
        carry = lax.fori_loop(full, last, functools.partial(step, True), carry)
        for (top, total), start in zip(carry, starts):
            finish(total, top * TO_LOG2, start, wide)

    small = jnp.max(limit) <= 100.0

    @pl.when(small)
    def _():
        for tile in range(2 * SLICE // FWD_Q):
            bounded_tile(tile)

    @pl.when(jnp.logical_not(small))
    def _():
        for tile in range(2 * SLICE // FWD_Q):
            running_tile(tile)


def attention_forward(spot, queries, end, pieces):
    rows, total = 2 * SLICE, 16 * SLICE
    whole = pl.BlockSpec(memory_space=pltpu.VMEM)
    return pl.pallas_call(
        forward_kernel,
        out_shape=[
            jax.ShapeDtypeStruct((HEAD_DIM + 8, rows), F32),
            jax.ShapeDtypeStruct((16, HEAD_DIM, 128), BF16),
        ],
        in_specs=[pl.BlockSpec(memory_space=pltpu.SMEM), whole, whole]
        + [pl.BlockSpec(memory_space=pl.ANY)] * 14,
        out_specs=[whole] * 2,
        scratch_shapes=[
            pltpu.VMEM((total, 2 * HEAD_DIM), BF16),
            pltpu.VMEM((HEAD_DIM + 16, total), BF16),
            pltpu.VMEM((2 * HEAD_DIM, rows), BF16),
            pltpu.SemaphoreType.DMA((16,)),
        ],
        compiler_params=pltpu.CompilerParams(vmem_limit_bytes=58 << 20),
        cost_estimate=pl.CostEstimate(
            flops=20_000_000_000, bytes_accessed=9 << 20, transcendentals=1 << 20
        ),
        name="attention_forward",
    )(spot, queries, end, *pieces)


def backward_kernel(last, spot, *refs):
    q_refs, do_refs, state_refs, (end_ref, *kv_refs) = refs[:2], refs[2:4], refs[4:6], refs[6:11]
    if last:
        partial_ref, *refs = refs[11:]
        dq_refs, dkv_refs, scratch = refs[:2], refs[2:4], refs[4:]
    else:
        partial_ref, dkv_refs, scratch = refs[11], refs[12:14], refs[14:]
    kv_ref, kt_ref, q_ref, do_ref, qt_ref, dot_ref, lse_ref, delta_ref, sum_ref = scratch
    x, core = spot[0], spot[1]
    per_core = 2 * SLICE
    none = jnp.zeros((HEAD_DIM, 2 * per_core), BF16)
    qt_ref[HEAD_DIM:, :] = none
    dot_ref[:HEAD_DIM, :] = none
    for side in range(2):
        for chunk in range(16):
            lanes = pl.ds(side * per_core + chunk * 128, 128)
            qt_ref[:HEAD_DIM, lanes] = q_refs[side][chunk]
            dot_ref[HEAD_DIM:, lanes] = do_refs[side][chunk]
        rows = pl.ds(side * per_core, per_core)
        q_ref[rows, :] = qt_ref[:, rows].T
        do_ref[rows, :] = dot_ref[:, rows].T
        state = state_refs[side]
        lse_ref[:, rows] = state[HEAD_DIM:, :]
        product = state[:HEAD_DIM, :] * dot_ref[HEAD_DIM:, rows].astype(F32)
        delta_ref[:, rows] = jnp.broadcast_to(jnp.sum(product, axis=0, keepdims=True), (8, per_core))
    for i, ref in enumerate(kv_refs):
        rows = pl.ds(i * SLICE, SLICE)
        kv_ref[rows, :] = ref[:SLICE, :]
        kt_ref[:, rows] = kv_ref[rows, :].T[:HEAD_DIM, :]
    sum_ref[...] = jnp.zeros_like(sum_ref)

    @pl.loop(0, 2 * per_core // BWD_Q)
    def _(tile):
        span = pl.ds(pl.multiple_of(tile * BWD_Q, BWD_Q), BWD_Q)
        query_t, grad_t = qt_ref[:, span], dot_ref[:, span]
        query, grad = q_ref[span, :], do_ref[span, :]
        end, lse, delta = end_ref[:, span], lse_ref[:1, span], delta_ref[:1, span]
        full, upto = spot[2 + 2 * tile], spot[3 + 2 * tile]

        def step(masked, block, at, grad_query):
            held = pl.ds(pl.multiple_of(block * per_core + at * SLICE, SLICE), SLICE)
            kv = kv_ref[held, :]
            weights = jnp.exp2(matmul(kv, query_t) * TO_LOG2 - lse)
            if masked:
                begin = (4 * x_of[block] + 2 * at + core) * SLICE
                place = begin + lax.broadcasted_iota(jnp.int32, weights.shape, 0)
                weights = jnp.where(place < end, weights, 0.0)
            grad_scores = (weights * (matmul(kv, grad_t) - delta)).astype(BF16)
            sum_ref[held, :] += matmul(weights.astype(BF16), grad) + matmul(grad_scores, query)
            return grad_query + matmul(kt_ref[:, held], grad_scores)

        x_of = [x ^ 3, x] if last else [x ^ 1, x ^ 2]
        grad_query = partial_ref[:, span] if last else jnp.zeros((HEAD_DIM, BWD_Q), F32)
        for block in range(2):
            whole = jnp.clip(full - 2 * x_of[block], 0, 2)
            some = jnp.clip(upto - 2 * x_of[block], 0, 2)
            grad_query = lax.fori_loop(0, whole, functools.partial(step, False, block), grad_query)
            grad_query = lax.fori_loop(whole, some, functools.partial(step, True, block), grad_query)
        if last:
            done = (grad_query * HEAD_DIM ** (-0.5)).astype(BF16)
            chunks = BWD_Q // 128
            for side in range(2):

                @pl.when(tile // (per_core // BWD_Q) == side)
                def _(side=side):
                    base = (tile - side * (per_core // BWD_Q)) * chunks
                    for chunk in range(chunks):
                        dq_refs[side][base + chunk] = done[:, chunk * 128 : chunk * 128 + 128]

        else:
            partial_ref[:, span] = grad_query

    is_key = lax.broadcasted_iota(jnp.int32, (1, 2 * HEAD_DIM), 1) < HEAD_DIM
    scale = jnp.where(is_key, HEAD_DIM ** (-0.5), 1.0)
    for block in range(2):
        dkv_refs[block][...] = (sum_ref[pl.ds(block * per_core, per_core), :] * scale).astype(BF16)


def attention_backward(last, spot, queries, grads, states, end, kvs, partial=None):
    rows, wide = 2 * SLICE, 2 * HEAD_DIM
    whole = pl.BlockSpec(memory_space=pltpu.VMEM)
    block = jax.ShapeDtypeStruct((rows, wide), BF16)
    if last:
        out_shape = [jax.ShapeDtypeStruct((16, HEAD_DIM, 128), BF16)] * 2 + [block] * 2
        operands = (spot, *queries, *grads, *states, end, *kvs, partial)
    else:
        out_shape = [jax.ShapeDtypeStruct((HEAD_DIM, 2 * rows), F32), block, block]
        operands = (spot, *queries, *grads, *states, end, *kvs)
    return pl.pallas_call(
        functools.partial(backward_kernel, last),
        out_shape=out_shape,
        in_specs=[pl.BlockSpec(memory_space=pltpu.SMEM)] + [whole] * (len(operands) - 1),
        out_specs=[whole] * len(out_shape),
        scratch_shapes=[
            pltpu.VMEM((2 * rows, wide), BF16),
            pltpu.VMEM((HEAD_DIM, 2 * rows), BF16),
            pltpu.VMEM((2 * rows, wide), BF16),
            pltpu.VMEM((2 * rows, wide), BF16),
            pltpu.VMEM((wide, 2 * rows), BF16),
            pltpu.VMEM((wide, 2 * rows), BF16),
            pltpu.VMEM((8, 2 * rows), F32),
            pltpu.VMEM((8, 2 * rows), F32),
            pltpu.VMEM((2 * rows, wide), F32),
        ],
        compiler_params=pltpu.CompilerParams(vmem_limit_bytes=58 << 20),
        cost_estimate=pl.CostEstimate(
            flops=8_000_000_000, bytes_accessed=6 << 20, transcendentals=1 << 20
        ),
        name="attention_backward_two" if last else "attention_backward_one",
    )(*operands)


def on_device(
    tokens,
    block_ids,
    ln1_gain,
    ln1_shift,
    qkv_weight,
    qv_bias,
    out_weight,
    out_bias,
    ln2_gain,
    ln2_shift,
    up_weight,
    up_bias,
    down_weight,
    down_bias,
    cotangent,
):
    x, zl, core, y, zh = (lax.axis_index(name) for name in AXES)
    place = jnp.stack([x, zl, core, y, zh]).astype(jnp.int32)
    width = tokens.shape[1]
    gain_one, shift_one, gain_two, shift_two, bias_out = (
        values.astype(F32)[None]
        for values in (ln1_gain, ln1_shift, ln2_gain, ln2_shift, out_bias)
    )

    pieces = gather_y(tokens)
    own3 = qkv_weight.transpose(1, 0, 2)
    near3 = swap(halves(own3, 1, core)[0], "zh")
    far3 = swap(near3, "co")
    out_kept = halves(out_weight, 0, core)[0]
    biases = jnp.concatenate([qv_bias.reshape(256), up_bias])
    biases = jnp.pad(biases[None], ((0, 15), (0, width - 768)))
    out_near = swap(jnp.concatenate([out_kept, biases]), "zh")
    pair_bias, pair_up_bias = out_near[HEAD_DIM, :256].reshape(2, 128), out_near[HEAD_DIM, 256:768]
    out_kept = jnp.concatenate([out_kept, out_near[:HEAD_DIM]])

    table = gather(block_ids, ("x", "zl", "co"), 16)
    counts = jnp.sum(
        (table.reshape(-1)[None, :] <= jnp.arange(128, dtype=jnp.int32)[:, None]).astype(jnp.int32),
        axis=1,
    )
    places = (4 * x + core, 14 - 4 * x + core, 4 * x + 1 - core, 15 - 4 * x - core)
    query_ids = jnp.concatenate([lax.dynamic_index_in_dim(table, p, 0, False) for p in places])
    same = query_ids[None, :] == jnp.arange(128, dtype=jnp.int32)[:, None]
    end = jnp.sum(jnp.where(same, counts[:, None], 0), axis=0)
    spot = jnp.stack([x, core]).astype(jnp.int32)
    ends = end[: 2 * SLICE].reshape(-1, FWD_Q)
    bounds = jnp.stack([ends[:, 0] // FWD_K, (ends[:, -1] + FWD_K - 1) // FWD_K], axis=1)
    forward_spot = jnp.concatenate([spot, bounds.reshape(-1)])
    ends = end.reshape(-1, BWD_Q)
    bounds = jnp.stack([ends[:, 0] // SLICE, (ends[:, -1] + SLICE - 1) // SLICE], axis=1)
    backward_spot = jnp.concatenate([spot, ((bounds - core + 1) // 2).reshape(-1)])
    end = end[None, :]

    blocks, normed, unit = on_core(
        project_kernel,
        "project",
        [((4, 768, 128), BF16), ((512, width), BF16), ((512, width), BF16)],
        (place, *pieces, gain_one, shift_one, own3, near3, far3, qv_bias, pair_bias),
        800_000_000,
    )
    blocks, forward_spot, backward_spot, end, out_kept = lax.optimization_barrier(
        (blocks, forward_spot, backward_spot, end, out_kept)
    )
    mine = exchange(blocks, ("zl", "zh"))
    up_parts, down_parts = halves(up_weight, 1, core), halves(down_weight, 0, core)
    units = jnp.concatenate(
        [up_parts[0], down_parts[0].reshape(256, 4, 256).transpose(1, 0, 2).reshape(width, 256)]
    )
    rows_here = to_mirror(jnp.stack([tokens, cotangent]), zl)
    units = after(units, mine)
    tokens_here, cotangent_here = rows_here[0], rows_here[1]
    kv = mine[:, :512].reshape(2, 2, 4, 128, 128).transpose(0, 2, 1, 3, 4).reshape(2, SLICE, 128)
    near, next_near = [None] * 2, [None] * 2
    queries = mine[:, 512:].reshape(2, 2, 4, HEAD_DIM, 128).transpose(0, 2, 1, 3, 4)
    queries = queries.reshape(2, 512, 128)
    near[0], next_near[1] = hop(kv[0], 1), hop(jnp.concatenate([kv[1], queries[1]]), 3)
    near[1], next_near[0] = hop(kv[1], 1), hop(kv[0], 3)
    units_near = swap(units, "zh")
    far = [hop(near[0], 3), hop(next_near[1][:SLICE], 1)]
    far, near[1], next_near[0], units_near = lax.optimization_barrier(
        (far, near[1], next_near[0], units_near)
    )
    kv_pieces = [kv.reshape(2 * SLICE, 128), *near, *next_near, *far]
    kv_pieces += [swap(piece, "co") for piece in kv_pieces]

    queries = jnp.concatenate([queries[0], next_near[1][SLICE:]]).reshape(16, HEAD_DIM, 128)
    both = gather_y(jnp.concatenate([cotangent_here, out_kept]))
    state, mixed = attention_forward(forward_spot, queries, end[:, : 2 * SLICE], kv_pieces)
    mixed, both = lax.optimization_barrier((mixed, both))
    out_kept = jnp.concatenate([piece[128:] for piece in both])
    out_sent = swap(out_kept, "co")
    units_far = swap(units_near, "co")

    def parts_of(units):
        return units[:width], units[width:].reshape(4, 256, 256).transpose(1, 0, 2).reshape(256, width)

    (up_near, down_near), (up_far, down_far) = parts_of(units_near), parts_of(units_far)
    ups = (up_parts[0], up_near, up_parts[1], up_far)
    downs = (down_parts[0], down_near, down_parts[1], down_far)
    own_half, pair_half = halves(up_bias, 0, core), halves(pair_up_bias, 0, core)
    up_bias_all = jnp.concatenate([own_half[0], pair_half[0], own_half[1], pair_half[1]])
    up_bias_all = up_bias_all.astype(F32)[None]
    other_state, other_queries = swap(state, "co"), swap(queries, "co")

    heads = exchange(mixed, ("zl", "y", "zh"))
    resid, mid, att = on_core(
        attend_out_kernel,
        "attend_out",
        [((128, width), F32), ((128, width), BF16), ((2, 512, 128), BF16)],
        (place, heads, out_kept, out_sent, tokens_here, bias_out, gain_two, shift_two),
        270_000_000,
    )

    mids = gather_y(mid)
    row = ((128, width), BF16)
    active, grad_hidden, grad_mids, grad_up_bias = on_core(
        feed_forward_kernel,
        "feed_forward",
        [((512, width), BF16)] * 2 + [((4, 128, width), BF16), ((1, 1024), F32)],
        (place, *mids, *both, up_bias_all, *ups, *downs),
        3_300_000_000,
    )
    grad_mids = exchange(grad_mids, "y")
    (sent,) = on_core(
        functools.partial(unit_grads_kernel, False),
        "unit_grads_sent",
        [((8, 2, 128, 512), BF16)],
        (place, *mids, *both, active, grad_hidden),
        6_000_000_000,
    )
    got = swap(sent, "co")
    (ff_blocks,) = on_core(
        functools.partial(unit_grads_kernel, True),
        "unit_grads_kept",
        [((16, 256, 256), BF16)],
        (place, *mids, *both, active, grad_hidden, got),
        6_000_000_000,
        limit=56,
    )
    grad_mids = after(grad_mids, ff_blocks)
    grad_resid, grad_branch, grad_heads, norm_sums = on_core(
        mid_back_kernel,
        "mid_back",
        [((128, width), F32), row, ((16, HEAD_DIM, 128), BF16), ((4, width), F32)],
        (place, grad_mids, resid, cotangent_here, gain_two, out_kept, out_sent),
        270_000_000,
    )

    grad_mixed = exchange(grad_heads, ("zl", "y", "zh"))
    late = after((att, grad_branch, active), grad_heads)
    out_downs = on_core(
        out_down_kernel,
        "out_down",
        [((384, width), BF16)] * 4,
        (place, *late, *downs),
        1_400_000_000,
    )
    grad_mixed, backward_spot = after((grad_mixed, backward_spot), ff_blocks, out_downs)
    ff_blocks = after(ff_blocks, out_downs)
    out_downs = send_y(out_downs)
    other_grad = swap(grad_mixed, "co")
    ff_shares = exchange(ff_blocks, ("x", "zl", "zh"))
    all_queries, grads = [queries, other_queries], [grad_mixed, other_grad]
    states = [state, other_state]
    partial, to_near, to_far = attention_backward(
        False, backward_spot, all_queries, grads, states, end, [*near, *far]
    )
    from_near, from_far = hop(to_near, 1), hop(to_far, 2)
    grad_q, grad_q_sent, to_next, grad_kv = attention_backward(
        True, backward_spot, all_queries, grads, states, end, [*next_near, kv[0], kv[1]], partial
    )
    to_next, grad_q_sent, from_near, from_far, ff_shares, out_downs = lax.optimization_barrier(
        (to_next, grad_q_sent, from_near, from_far, ff_shares, out_downs)
    )
    from_next = hop(to_next, 3)
    grad_q = total([grad_q, swap(grad_q_sent, "co")]).astype(BF16)
    grad_q = jnp.stack([grad_q[:8], hop(grad_q[8:], 3)])
    grad_q = grad_q.reshape(2, 4, 2, HEAD_DIM, 128).transpose(0, 2, 1, 3, 4).reshape(4, 256, 128)

    grad_kv = total([grad_kv, from_near, from_far, from_next])
    grad_kv = grad_kv.astype(BF16).reshape(2, SLICE, 128)
    blocks = jnp.concatenate([to_z(grad_kv), grad_q], axis=1)
    ff_shares, out_downs = after((ff_shares, out_downs), blocks)
    blocks = exchange(blocks, ("zl", "zh"))

    ff_share = jnp.sum(ff_shares.astype(F32), axis=0)
    ff_share = jnp.concatenate(
        [ff_share[:128].T, ff_share[128:, :128], ff_share[128:, 128:]]
    ).astype(BF16)
    rows_home, out_kept_sum, out_sent_sum = on_core(
        out_sums_kernel,
        "out_sums",
        [((2, 128, width), F32), ((4, 2, 2, HEAD_DIM, 128), F32), ((4, 2, 2, HEAD_DIM, 128), BF16)],
        (place, *out_downs, resid, down_bias.astype(F32)[None], grad_resid),
        1_000_000,
    )
    unit, out_sent_sum = after((unit, out_sent_sum), rows_home)
    out_got = swap(out_sent_sum, "co")

    *grad_normed, part_sums = on_core(
        project_back_kernel,
        "project_back",
        [row] * 4 + [((2, width), F32)],
        (place, blocks, unit, own3, near3, far3),
        800_000_000,
        scratch=[pltpu.VMEM((512, width), F32)],
    )
    grad_normed = send_y(grad_normed)
    blocks, ff_share = after((blocks, ff_share), part_sums)
    ff_rest = gather(ff_share, ("x", "zl"), 8)

    by_head, head_sums = on_core(
        qkv_grads_kernel,
        "qkv_grads",
        [((2, 4, 2, 2, 192, 128), BF16), ((4, 192, 128), F32)],
        (place, blocks, normed),
        900_000_000,
    )
    head_got = swap(by_head[1], "co")
    rows_home = to_mirror(after(rows_home, head_got), zl)

    head_sums = head_sums[:, :, 0].reshape(2, 2, 3, HEAD_DIM)
    bias = jnp.stack([head_sums[:, :, 2], head_sums[:, :, 1]]).transpose(2, 0, 1, 3)
    up_sums = grad_up_bias.reshape(2, 2, 256)
    up_sums = turned(turned(up_sums, 0, core), 1, zh).transpose(1, 0, 2).reshape(1, width)
    bias = jnp.pad(bias.reshape(1, 512), ((0, 0), (0, 512)))
    small = jnp.concatenate([part_sums, norm_sums, up_sums, bias])
    small = small + swap(small, "co")
    (shares,) = on_core(
        shares_kernel,
        "shares",
        [((16, 272, 128), BF16)],
        (place, by_head, head_got, out_kept_sum, out_got, small),
        1_000_000,
    )
    shares = exchange(shares, ("x", "zl", "zh"))
    share = jnp.sum(shares.astype(F32), axis=0).astype(BF16)
    rest = gather(share, ("x", "zl"), 8)
    small = rest[:, 256:264].astype(F32).transpose(1, 0, 2).reshape(8, width)
    for bit in (1, 3):
        small = jnp.concatenate([small[:6] + hop(small[:6], bit, "y"), small[6:]])
    grad_up_bias = lax.dynamic_slice_in_dim(small[6], zh * 512, 512, 0)
    grad_qv_bias = lax.dynamic_slice_in_dim(small[7], zh * 256, 256, 0).reshape(2, 128)

    (grad_tokens,) = on_core(
        last_norm_kernel,
        "last_norm",
        [((128, width), F32)],
        (place, *grad_normed, tokens, gain_one, rows_home[1]),
        1_000_000,
    )
    grad_down_weight, grad_up_weight = on_core(
        unit_weights_kernel,
        "unit_weights",
        [((512, width), F32), ((width, 512), F32)],
        (place, ff_rest, swap(ff_rest, "co")),
        1_000_000,
    )
    grad_qkv_weight, grad_out_weight = on_core(
        head_weights_kernel,
        "head_weights",
        [((3, width, 128), F32), ((128, width), F32)],
        (place, rest, swap(rest, "co")),
        1_000_000,
    )
    return (
        rows_home[0],
        grad_tokens,
        small[0],
        small[1],
        grad_qkv_weight.transpose(1, 0, 2),
        grad_qv_bias,
        grad_out_weight,
        small[2],
        small[3],
        small[4],
        grad_up_weight,
        grad_up_bias,
        grad_down_weight,
        small[5],
    )


def solution(mesh):
    fine = Mesh(mesh.devices.reshape(4, 2, 2, 4, 2), AXES)
    slices, shards = ("x", "zl", "co"), ("y", "zh")
    return jax.shard_map(
        on_device,
        mesh=fine,
        in_specs=(
            P(AXES, None),
            P(slices),
            P(),
            P(),
            P(None, None, shards),
            P(None, shards),
            P(shards, None),
            P(),
            P(),
            P(),
            P(None, shards),
            P(shards),
            P(shards, None),
            P(),
            P(AXES, None),
        ),
        out_specs=(
            P(AXES, None),
            P(AXES, None),
            P(),
            P(),
            P(None, None, shards),
            P(None, shards),
            P(shards, None),
            P(),
            P(),
            P(),
            P(None, shards),
            P(shards),
            P(shards, None),
            P(),
        ),
        check_vma=False,
    )
```

```python
import functools

import jax
import jax.numpy as jnp
from jax import lax
from jax.experimental import pallas as pl
from jax.experimental.pallas import tpu as pltpu
from jax.sharding import Mesh
from jax.sharding import PartitionSpec as P

HEAD_DIM = 64
EPSILON = 1e-05
MASKED = -1e30
LOG2E = 1.4426950408889634
TO_LOG2 = LOG2E * HEAD_DIM ** (-0.5)
AXES = ("x", "zl", "co", "y", "zh")
BF16, F32 = jnp.bfloat16, jnp.float32
SLICE = 1024
FWD_Q, FWD_K = 1024, 1024
BWD_Q = 1024


def contract(left, right, left_dim, right_dim):
    return lax.dot_general(
        left, right, (((left_dim,), (right_dim,)), ((), ())), preferred_element_type=F32
    )


def matmul(left, right):
    return contract(left, right, 1, 0)


def shift(values, steps):
    return lax.ppermute(values, "y", [(i, (i + steps) % 4) for i in range(4)])


def hop(values, bit, axis="x"):
    return lax.ppermute(values, axis, [(i, i ^ bit) for i in range(4)])


def swap(values, axis):
    return lax.ppermute(values, axis, [(0, 1), (1, 0)])


def to_mirror(rows, zl):
    moved = lax.ppermute(rows, ("x", "zl"), [(i, 8 - i) for i in (1, 3, 5, 7)])
    return jnp.where(zl == 0, rows, moved)


def exchange(blocks, axes):
    return lax.all_to_all(blocks, axes, 0, 0, tiled=True)


def gather(rows, axes, size):
    return exchange(jnp.broadcast_to(rows[None], (size,) + rows.shape), axes)


def gather_y(rows):
    one, three = shift(rows, 1), shift(rows, 3)
    return rows, one, shift(rows, 2), three


def send_y(blocks):
    return blocks[0], shift(blocks[1], -1), shift(blocks[3], -3), shift(blocks[2], -2)


def total(parts):
    return functools.reduce(jnp.add, [part.astype(F32) for part in parts])


def after(value, *others):
    return lax.optimization_barrier((value, others))[0]


def turned(values, dim, index):
    return jnp.where(index == 0, values, jnp.flip(values, dim))


def halves(values, dim, index):
    half = values.shape[dim] // 2
    return (
        lax.dynamic_slice_in_dim(values, index * half, half, dim),
        lax.dynamic_slice_in_dim(values, (1 - index) * half, half, dim),
    )


def to_z(rows):
    n = rows.shape[-1]
    return rows.reshape(2, 4, 2, 128, n).transpose(0, 2, 1, 3, 4).reshape(4, 512, n)


def on_core(kernel, name, outputs, operands, flops, limit=32, scratch=()):
    whole = pl.BlockSpec(memory_space=pltpu.VMEM)
    outputs = [jax.ShapeDtypeStruct(shape, dtype) for shape, dtype in outputs]
    return pl.pallas_call(
        kernel,
        out_shape=outputs,
        in_specs=[pl.BlockSpec(memory_space=pltpu.SMEM)] + [whole] * (len(operands) - 1),
        out_specs=[whole] * len(outputs),
        scratch_shapes=list(scratch),
        compiler_params=pltpu.CompilerParams(vmem_limit_bytes=limit << 20),
        cost_estimate=pl.CostEstimate(flops=flops, bytes_accessed=4 << 20, transcendentals=0),
        name=name,
    )(*operands)


def joined(refs, dim=0):
    return jnp.concatenate([ref[...] for ref in refs], axis=dim)


def unit_rows(rows):
    centered = rows - jnp.mean(rows, axis=-1, keepdims=True)
    scale = lax.rsqrt(jnp.mean(centered * centered, axis=-1, keepdims=True) + EPSILON)
    return centered * scale, scale


def norm_back(grad, unit, scale, gain):
    grad = grad * gain
    along = jnp.mean(grad * unit, axis=-1, keepdims=True)
    return scale * (grad - jnp.mean(grad, axis=-1, keepdims=True) - unit * along)


def y_rows(place, steps):
    return pl.ds(pl.multiple_of(((place[3] - steps) & 3) * 128, 128), 128)


def merge_lanes(left, right):
    left, right = left.astype(F32), right.astype(F32)
    first = lax.broadcasted_iota(jnp.int32, left.shape, 1) < HEAD_DIM
    return (
        jnp.where(first, left, pltpu.roll(right, HEAD_DIM, 1)).astype(BF16),
        jnp.where(first, pltpu.roll(left, HEAD_DIM, 1), right).astype(BF16),
    )


def project_kernel(place, *refs):
    pieces, (gain, bent, own, near, far, own_bias, pair_bias) = refs[:4], refs[4:11]
    blocks, normed_ref, unit_ref = refs[11:]
    core, zh = place[2], place[4]
    for steps, piece in enumerate(pieces):
        rows = y_rows(place, steps)
        unit, _ = unit_rows(piece[...].astype(F32))
        unit_ref[rows, :] = unit.astype(BF16)
        normed_ref[rows, :] = (unit * gain[...] + bent[...]).astype(BF16)
    normed = normed_ref[...]
    first = normed_ref[:, pl.ds(pl.multiple_of(core * 512, 512), 512)]
    second = normed_ref[:, pl.ds(pl.multiple_of((1 - core) * 512, 512), 512)]
    for pair in range(2):
        bias = (pair_bias if pair else own_bias)[...].astype(F32)

        def projected(i, pair=pair):
            if pair:
                return matmul(first, near[i]) + matmul(second, far[i])
            return matmul(normed, own[i])

        queries = (projected(0) + bias[:1]).T.astype(BF16)
        mixed = merge_lanes(projected(1).astype(BF16), (projected(2) + bias[1:]).astype(BF16))
        for head in range(2):
            where = 2 * head + (zh ^ pair)
            blocks[where, pl.ds(0, 512), :] = mixed[head]
            for y in range(4):
                lanes = slice(y * 128, y * 128 + 128)
                piece = queries[head * HEAD_DIM : head * HEAD_DIM + HEAD_DIM, lanes]
                blocks[where, pl.ds(512 + y * HEAD_DIM, HEAD_DIM), :] = piece


def project_back_kernel(place, blocks, unit_ref, own, near, far, *refs):
    outs, sums, grad_ref = refs[:4], refs[4], refs[5]
    core, zh = place[2], place[4]
    for pair in range(2):
        heads = [blocks[2 * head + (zh ^ pair)] for head in range(2)]
        keys, values = merge_lanes(heads[0][:512], heads[1][:512])
        queries = [
            jnp.concatenate([head[512 + y * HEAD_DIM :][:HEAD_DIM] for y in range(4)], axis=1)
            for head in heads
        ]
        parts = (jnp.concatenate(queries, axis=0).T, keys, values)

        def back(weight, parts=parts):
            return functools.reduce(
                jnp.add, [contract(part, weight[i], 1, 1) for i, part in enumerate(parts)]
            )

        if pair:
            first = pl.ds(pl.multiple_of(core * 512, 512), 512)
            second = pl.ds(pl.multiple_of((1 - core) * 512, 512), 512)
            grad_ref[:, first] += back(near)
            grad_ref[:, second] += back(far)
        else:
            grad_ref[...] = back(own)
    grad = grad_ref[...]
    sums[...] = jnp.concatenate(
        [
            jnp.sum(grad * unit_ref[...].astype(F32), axis=0, keepdims=True),
            jnp.sum(grad, axis=0, keepdims=True),
        ]
    )
    for steps, out in enumerate(outs):
        out[...] = grad_ref[y_rows(place, steps), :].astype(BF16)


def qkv_grads_kernel(place, blocks_ref, normed_ref, kept, sent, sums_ref):
    normed, ones = normed_ref[...], jnp.ones((512, 128), BF16)
    for head in range(2):
        for zh in range(2):
            block = blocks_ref[2 * head + zh]
            queries = [block[512 + y * HEAD_DIM :][:HEAD_DIM] for y in range(4)]
            left = jnp.concatenate([block[:512].T, jnp.concatenate(queries, axis=1)], axis=0)
            grad = matmul(left, normed)
            for half in range(2):

                def store(ref, grad=grad, half=half, head=head, zh=zh):
                    for chunk in range(4):
                        lanes = slice((4 * half + chunk) * 128, (4 * half + chunk) * 128 + 128)
                        ref[chunk, head, zh] = grad[:, lanes].astype(BF16)

                pl.when(place[2] == half)(functools.partial(store, kept))
                pl.when(place[2] != half)(functools.partial(store, sent))
            sums_ref[2 * head + zh] = matmul(left, ones)


def attend_out_kernel(place, heads, kept, sent, tokens, bias, gain, bent, resid_ref, mid_ref, att_ref):
    core, y, zh = place[2], place[3], place[4]
    for side in range(2):
        for steps in range(4):
            for pair in range(2):
                where = 8 * (core ^ side) + 2 * ((y - steps) & 3) + (zh ^ pair)
                att_ref[side, pl.ds(steps * 128 + pair * HEAD_DIM, HEAD_DIM), :] = heads[where]
    branch = matmul(att_ref[0].T, kept[...]) + matmul(att_ref[1].T, sent[...])
    resid = tokens[...].astype(F32) + branch + bias[...]
    resid_ref[...] = resid
    mid_ref[...] = (unit_rows(resid)[0] * gain[...] + bent[...]).astype(BF16)


def mid_back_kernel(place, *refs):
    parts, resid, cotangent, gain, kept, sent = refs[:6]
    grad_resid_ref, branch_ref, heads, sums = refs[6:]
    core, y, zh = place[2], place[3], place[4]
    grad = total([parts[i] for i in range(4)])
    unit, scale = unit_rows(resid[...])
    cot = cotangent[...].astype(F32)
    grad_resid = cot + norm_back(grad, unit, scale, gain[...])
    grad_resid_ref[...] = grad_resid
    branch = grad_resid.astype(BF16)
    branch_ref[...] = branch
    rows = [grad_resid, grad * unit, grad, cot]
    sums[...] = jnp.concatenate([jnp.sum(row, axis=0, keepdims=True) for row in rows])
    for side, weight in enumerate((kept, sent)):
        grads = contract(weight[...], branch, 1, 1).astype(BF16)
        for steps in range(4):
            for pair in range(2):
                where = 8 * (core ^ side) + 2 * ((y - steps) & 3) + (zh ^ pair)
                start = steps * 128 + pair * HEAD_DIM
                heads[where] = grads[start : start + HEAD_DIM]


def feed_forward_kernel(place, *refs):
    mids, cots, (bias,), ups, downs = refs[:4], refs[4:8], refs[8:9], refs[9:13], refs[13:17]
    active_ref, grad_ref, out, bias_grad = refs[17:]
    mid, cot = joined(mids), jnp.concatenate([ref[:128, :] for ref in cots])
    summed = None
    for i, (up_ref, down_ref) in enumerate(zip(ups, downs)):
        span = pl.ds(i * 256, 256)
        up = up_ref[...]
        hidden = matmul(mid, up) + bias[:, span]
        square = hidden * hidden
        bent = jnp.tanh(0.7978845608028654 * hidden * (1.0 + 0.044715 * square))
        active_ref[:, span] = (0.5 * hidden * (1.0 + bent)).astype(BF16)
        slope = 0.7978845608028654 * (1.0 + 3.0 * 0.044715 * square)
        slope = 0.5 * (1.0 + bent) + 0.5 * hidden * (1.0 - bent * bent) * slope
        grad = (slope * contract(cot, down_ref[...], 1, 1)).astype(BF16)
        grad_ref[:, span] = grad
        bias_grad[:, span] = jnp.sum(grad.astype(F32), axis=0, keepdims=True)
        part = contract(grad, up, 1, 1)
        summed = part if summed is None else summed + part
    for steps in range(4):
        piece = summed[steps * 128 : steps * 128 + 128].astype(BF16)
        out[(place[3] - steps) & 3] = piece


def unit_grads_kernel(kept, place, *refs):
    mids, cots, active, grad = refs[:4], refs[4:8], refs[8], refs[9]
    got, out = (refs[10], refs[11]) if kept else (None, refs[10])
    span = pl.ds(0 if kept else 512, 512)
    cot = jnp.concatenate([ref[:128, :] for ref in cots])
    for i, (left, right) in enumerate(((cot, active), (joined(mids), grad))):
        summed = contract(left, right[:, span], 0, 0)
        for share in range(8):
            block = summed[share * 128 : share * 128 + 128]
            if kept:
                block = (block + got[share, i].astype(F32)).astype(BF16)
                for pair in range(2):
                    half = block[:, pair * 256 : pair * 256 + 256]
                    out[2 * share + (place[4] ^ pair), pl.ds(i * 128, 128), :] = half
            else:
                out[share, i] = block.astype(BF16)


def out_down_kernel(place, att, branch, active, *refs):
    downs, outs = refs[:4], refs[4:]
    grads = [matmul(att[side], branch[...]).astype(BF16) for side in range(2)]
    down = total([matmul(active[:, i * 256 : i * 256 + 256], ref[...]) for i, ref in enumerate(downs)])
    for steps, out in enumerate(outs):
        rows = slice(steps * 128, steps * 128 + 128)
        out[pl.ds(0, 128), :] = grads[0][rows]
        out[pl.ds(128, 128), :] = grads[1][rows]
        out[pl.ds(256, 128), :] = down[rows].astype(BF16)


def out_sums_kernel(place, *refs):
    parts, (resid, bias, grad_resid, home, kept, sent) = refs[:4], refs[4:]
    home[0] = total([part[256:, :] for part in parts]) + resid[...] + bias[...]
    home[1] = grad_resid[...]
    for side, ref in enumerate((kept, sent)):
        summed = total([part[side * 128 : side * 128 + 128, :] for part in parts]).astype(ref.dtype)
        for pair in range(2):
            for share in range(8):
                lanes = slice(share * 128, share * 128 + 128)
                piece = summed[pair * HEAD_DIM : pair * HEAD_DIM + HEAD_DIM, lanes]
                ref[share // 2, share % 2, pair] = piece


def shares_kernel(place, heads, head_got, out, out_got, small, shares):
    for x in range(4):
        for zl in range(2):
            share = 2 * x + zl
            for zh in range(2):
                to = 2 * share + zh
                grad = total([heads[x, zl, zh], head_got[x, zl, zh]])
                shares[to, pl.ds(0, 192), :] = grad.astype(BF16)
                grad = total([out[x, zl, zh], out_got[x, zl, zh]])
                shares[2 * share + (place[4] ^ zh), pl.ds(192, HEAD_DIM), :] = grad.astype(BF16)
                rows = small[:, share * 128 : share * 128 + 128]
                rows = jnp.concatenate([rows, jnp.zeros_like(rows)]).astype(BF16)
                shares[to, pl.ds(256, 16), :] = rows


def last_norm_kernel(place, *refs):
    parts, (tokens, gain, resid, out) = refs[:4], refs[4:]
    unit, scale = unit_rows(tokens[...].astype(F32))
    out[...] = resid[...] + norm_back(total([part[...] for part in parts]), unit, scale, gain[...])


def unit_weights_kernel(place, own, other, down, up):
    for side, ref in enumerate((own, other)):
        half = place[2] ^ side
        for share in range(8):
            lanes = pl.ds(share * 128, 128)
            down[pl.ds(pl.multiple_of(half * 256, 256), 256), lanes] = ref[share, :256].astype(F32)
            for part in range(2):
                lanes = pl.ds(pl.multiple_of(half * 256 + part * 128, 128), 128)
                piece = ref[share, pl.ds(256 + part * 128, 128), :].astype(F32)
                up[pl.ds(share * 128, 128), lanes] = piece


def head_weights_kernel(place, own, other, qkv, out):
    for side, ref in enumerate((own, other)):
        half = place[2] ^ side
        for x in range(4):
            rows = pl.ds(pl.multiple_of(half * 512 + x * 128, 128), 128)
            for i, which in enumerate((1, 2, 0)):
                span = pl.ds(i * HEAD_DIM, HEAD_DIM)
                both = jnp.concatenate([ref[2 * x, span, :], ref[2 * x + 1, span, :]])
                qkv[which, rows, :] = both.astype(F32).T
            for zl in range(2):
                piece = ref[2 * x + zl, pl.ds(192, HEAD_DIM), :].astype(F32)
                span = pl.ds(pl.multiple_of(half * HEAD_DIM, HEAD_DIM), HEAD_DIM)
                out[span, pl.ds((2 * x + zl) * 128, 128)] = piece


def forward_kernel(spot, q_ref, end_ref, *refs):
    pieces, (state_ref, out, kv_ref, vt_ref, qt_ref, sems) = refs[:14], refs[14:]
    x, core = spot[0], spot[1]
    copies = []

    def bring(piece, half, x_from, slice_in_x, parity):
        where = (4 * x_from + 2 * slice_in_x + parity) * SLICE
        copy = pltpu.make_async_copy(
            piece.at[pl.ds(half * SLICE, SLICE), :],
            kv_ref.at[pl.ds(pl.multiple_of(where, SLICE), SLICE), :],
            sems.at[len(copies)],
        )
        copy.start()
        copies.append(copy)

    for side in range(2):
        parity = core if side == 0 else 1 - core
        pieces_here = pieces[7 * side : 7 * side + 7]
        bring(pieces_here[0], 0, x, 0, parity)
        bring(pieces_here[0], 1, x, 1, parity)
        for i, piece in enumerate(pieces_here[1:]):
            bring(piece, 0, x ^ (1, 1, 3, 3, 2, 2)[i], i % 2, parity)
    qt_ref[HEAD_DIM:, :] = jnp.zeros((HEAD_DIM, 2 * SLICE), BF16)
    for chunk in range(16):
        qt_ref[:HEAD_DIM, pl.ds(chunk * 128, 128)] = q_ref[chunk]
    vt_ref[HEAD_DIM:, :] = jnp.ones((16, vt_ref.shape[1]), BF16)
    for copy in copies:
        copy.wait()

    def turn(i, largest):
        rows = pl.ds(pl.multiple_of(i * SLICE, SLICE), SLICE)
        both = kv_ref[rows, :].T
        vt_ref[:HEAD_DIM, rows] = both[HEAD_DIM:, :]
        keys = both[:HEAD_DIM, :].astype(F32)
        return jnp.maximum(largest, jnp.sum(keys * keys, axis=0, keepdims=True))

    longest = jnp.max(lax.fori_loop(0, 16, turn, jnp.zeros((1, SLICE), F32)))
    norms = qt_ref[:HEAD_DIM, :].astype(F32)
    norms = jnp.sum(norms * norms, axis=0, keepdims=True)
    limit = jnp.sqrt(norms * longest) * TO_LOG2
    level = limit - 90.0

    def finish(total, log_top, start, wide):
        span = pl.ds(start, wide)
        weight_sum = total[HEAD_DIM : HEAD_DIM + 1]
        mixed = total[:HEAD_DIM] / weight_sum
        state_ref[:HEAD_DIM, span] = mixed
        for chunk in range(wide // 128):
            piece = mixed[:, chunk * 128 : chunk * 128 + 128].astype(BF16)
            out[start // 128 + chunk] = piece
        state_ref[HEAD_DIM:, span] = jnp.broadcast_to(log_top + jnp.log2(weight_sum), (8, wide))

    def masked_at(values, begin, end, other):
        place = begin + lax.broadcasted_iota(jnp.int32, values.shape, 0)
        return jnp.where(place < end, values, other)

    def bounded_tile(tile):
        span = pl.ds(tile * FWD_Q, FWD_Q)
        query, end = qt_ref[:, span], end_ref[:, span]
        base = level[:, tile * FWD_Q : tile * FWD_Q + FWD_Q]

        def step(masked, keys, at, total):
            for piece in range(max(keys // 512, 1)):
                size = min(keys, 512)
                begin = pl.multiple_of(at * keys + piece * size, size)
                rows = pl.ds(begin, size)
                weights = jnp.exp2(matmul(kv_ref[rows, :], query) * TO_LOG2 - base)
                if masked:
                    weights = masked_at(weights, begin, end, 0.0)
                total = total + matmul(vt_ref[:, rows], weights.astype(BF16))
            return total

        total = jnp.zeros((HEAD_DIM + 16, FWD_Q), F32)
        full, last, pieces = spot[2 + 3 * tile], spot[3 + 3 * tile], spot[4 + 3 * tile]
        total = lax.fori_loop(0, full, functools.partial(step, False, FWD_K), total)

        def edge(at, total):
            left = pieces - 4 * at
            long = left > 2
            ranges = ((FWD_K, at, jnp.where(long, 1, 0)), (256, 4 * at, jnp.where(long, 0, left)))
            for keys, begin, count in ranges:
                masked = functools.partial(step, True, keys)
                total = lax.fori_loop(begin, begin + count, masked, total)
            return total

        total = lax.fori_loop(full, last, edge, total)
        finish(total, base, tile * FWD_Q, FWD_Q)

    def running_tile(tile):
        wide = FWD_Q // 2
        starts = [tile * FWD_Q, tile * FWD_Q + wide]
        queries = [qt_ref[:, pl.ds(start, wide)] for start in starts]
        ends = [end_ref[:, pl.ds(start, wide)] for start in starts]

        def step(masked, at, carry):
            rows = pl.ds(pl.multiple_of(at * FWD_K, FWD_K), FWD_K)
            kv, vt = kv_ref[rows, :], vt_ref[:, rows]
            scores = [matmul(kv, query) for query in queries]
            after = []
            for (top, total), score, end in zip(carry, scores, ends):
                if masked:
                    score = masked_at(score, at * FWD_K, end, MASKED)
                new_top = jnp.maximum(top, jnp.max(score, axis=0, keepdims=True))
                weights = jnp.exp2(score * TO_LOG2 - new_top * TO_LOG2)
                factor = jnp.exp2((top - new_top) * TO_LOG2)
                total = total * factor + matmul(vt, weights.astype(BF16))
                after.append((new_top, total))
            return tuple(after)

        begin = (jnp.full((1, wide), MASKED, F32), jnp.zeros((HEAD_DIM + 16, wide), F32))
        full, last = spot[2 + 3 * tile], spot[3 + 3 * tile]
        carry = lax.fori_loop(0, full, functools.partial(step, False), (begin, begin))
        carry = lax.fori_loop(full, last, functools.partial(step, True), carry)
        for (top, total), start in zip(carry, starts):
            finish(total, top * TO_LOG2, start, wide)

    small = jnp.max(limit) <= 100.0

    @pl.when(small)
    def _():
        for tile in range(2 * SLICE // FWD_Q):
            bounded_tile(tile)

    @pl.when(jnp.logical_not(small))
    def _():
        for tile in range(2 * SLICE // FWD_Q):
            running_tile(tile)


def attention_forward(spot, queries, end, pieces):
    rows, total = 2 * SLICE, 16 * SLICE
    whole = pl.BlockSpec(memory_space=pltpu.VMEM)
    return pl.pallas_call(
        forward_kernel,
        out_shape=[
            jax.ShapeDtypeStruct((HEAD_DIM + 8, rows), F32),
            jax.ShapeDtypeStruct((16, HEAD_DIM, 128), BF16),
        ],
        in_specs=[pl.BlockSpec(memory_space=pltpu.SMEM), whole, whole]
        + [pl.BlockSpec(memory_space=pl.ANY)] * 14,
        out_specs=[whole] * 2,
        scratch_shapes=[
            pltpu.VMEM((total, 2 * HEAD_DIM), BF16),
            pltpu.VMEM((HEAD_DIM + 16, total), BF16),
            pltpu.VMEM((2 * HEAD_DIM, rows), BF16),
            pltpu.SemaphoreType.DMA((16,)),
        ],
        compiler_params=pltpu.CompilerParams(vmem_limit_bytes=58 << 20),
        cost_estimate=pl.CostEstimate(
            flops=20_000_000_000, bytes_accessed=9 << 20, transcendentals=1 << 20
        ),
        name="attention_forward",
    )(spot, queries, end, *pieces)


def backward_kernel(last, spot, *refs):
    q_refs, do_refs, state_refs, (end_ref, *kv_refs) = refs[:2], refs[2:4], refs[4:6], refs[6:11]
    if last:
        partial_ref, *refs = refs[11:]
        dq_refs, dkv_refs, scratch = refs[:2], refs[2:4], refs[4:]
    else:
        partial_ref, dkv_refs, scratch = refs[11], refs[12:14], refs[14:]
    kv_ref, kt_ref, q_ref, do_ref, qt_ref, dot_ref, lse_ref, delta_ref, sum_ref = scratch
    x, core = spot[0], spot[1]
    per_core = 2 * SLICE
    none = jnp.zeros((HEAD_DIM, 2 * per_core), BF16)
    qt_ref[HEAD_DIM:, :] = none
    dot_ref[:HEAD_DIM, :] = none
    for side in range(2):
        for chunk in range(16):
            lanes = pl.ds(side * per_core + chunk * 128, 128)
            qt_ref[:HEAD_DIM, lanes] = q_refs[side][chunk]
            dot_ref[HEAD_DIM:, lanes] = do_refs[side][chunk]
        rows = pl.ds(side * per_core, per_core)
        q_ref[rows, :] = qt_ref[:, rows].T
        do_ref[rows, :] = dot_ref[:, rows].T
        state = state_refs[side]
        lse_ref[:, rows] = state[HEAD_DIM:, :]
        product = state[:HEAD_DIM, :] * dot_ref[HEAD_DIM:, rows].astype(F32)
        delta_ref[:, rows] = jnp.broadcast_to(jnp.sum(product, axis=0, keepdims=True), (8, per_core))
    for i, ref in enumerate(kv_refs):
        rows = pl.ds(i * SLICE, SLICE)
        kv_ref[rows, :] = ref[:SLICE, :]
        kt_ref[:, rows] = kv_ref[rows, :].T[:HEAD_DIM, :]
    sum_ref[...] = jnp.zeros_like(sum_ref)

    @pl.loop(0, 2 * per_core // BWD_Q)
    def _(tile):
        span = pl.ds(pl.multiple_of(tile * BWD_Q, BWD_Q), BWD_Q)
        query_t, grad_t = qt_ref[:, span], dot_ref[:, span]
        query, grad = q_ref[span, :], do_ref[span, :]
        end, lse, delta = end_ref[:, span], lse_ref[:1, span], delta_ref[:1, span]
        full, upto, pieces = spot[2 + 3 * tile], spot[3 + 3 * tile], spot[4 + 3 * tile]

        def step(masked, keys, block, at, grad_query):
            held = pl.ds(pl.multiple_of(block * per_core + at * keys, keys), keys)
            kv = kv_ref[held, :]
            weights = jnp.exp2(matmul(kv, query_t) * TO_LOG2 - lse)
            if masked:
                slices = at // (SLICE // keys)
                begin = (4 * x_of[block] + slices + core) * SLICE + at * keys
                place = begin + lax.broadcasted_iota(jnp.int32, weights.shape, 0)
                weights = jnp.where(place < end, weights, 0.0)
            grad_scores = (weights * (matmul(kv, grad_t) - delta)).astype(BF16)
            sum_ref[held, :] += matmul(weights.astype(BF16), grad) + matmul(grad_scores, query)
            return grad_query + matmul(kt_ref[:, held], grad_scores)

        x_of = [x ^ 3, x] if last else [x ^ 1, x ^ 2]
        grad_query = partial_ref[:, span] if last else jnp.zeros((HEAD_DIM, BWD_Q), F32)
        for block in range(2):
            whole = jnp.clip(full - 2 * x_of[block], 0, 2)
            some = jnp.clip(upto - 2 * x_of[block], 0, 2)
            plain = functools.partial(step, False, SLICE, block)
            grad_query = lax.fori_loop(0, whole, plain, grad_query)

            def edge(at, grad_query, block=block):
                left = pieces - 4 * (4 * x_of[block] + 2 * at + core)
                long = left > 2
                ranges = ((SLICE, at, jnp.where(long, 1, 0)), (256, 4 * at, jnp.where(long, 0, left)))
                for keys, begin, count in ranges:
                    masked = functools.partial(step, True, keys, block)
                    grad_query = lax.fori_loop(begin, begin + count, masked, grad_query)
                return grad_query

            grad_query = lax.fori_loop(whole, some, edge, grad_query)
        if last:
            done = (grad_query * HEAD_DIM ** (-0.5)).astype(BF16)
            chunks = BWD_Q // 128
            for side in range(2):

                @pl.when(tile // (per_core // BWD_Q) == side)
                def _(side=side):
                    base = (tile - side * (per_core // BWD_Q)) * chunks
                    for chunk in range(chunks):
                        dq_refs[side][base + chunk] = done[:, chunk * 128 : chunk * 128 + 128]

        else:
            partial_ref[:, span] = grad_query

    is_key = lax.broadcasted_iota(jnp.int32, (1, 2 * HEAD_DIM), 1) < HEAD_DIM
    scale = jnp.where(is_key, HEAD_DIM ** (-0.5), 1.0)
    for block in range(2):
        dkv_refs[block][...] = (sum_ref[pl.ds(block * per_core, per_core), :] * scale).astype(BF16)


def attention_backward(last, spot, queries, grads, states, end, kvs, partial=None):
    rows, wide = 2 * SLICE, 2 * HEAD_DIM
    whole = pl.BlockSpec(memory_space=pltpu.VMEM)
    block = jax.ShapeDtypeStruct((rows, wide), BF16)
    if last:
        out_shape = [jax.ShapeDtypeStruct((16, HEAD_DIM, 128), BF16)] * 2 + [block] * 2
        operands = (spot, *queries, *grads, *states, end, *kvs, partial)
    else:
        out_shape = [jax.ShapeDtypeStruct((HEAD_DIM, 2 * rows), F32), block, block]
        operands = (spot, *queries, *grads, *states, end, *kvs)
    return pl.pallas_call(
        functools.partial(backward_kernel, last),
        out_shape=out_shape,
        in_specs=[pl.BlockSpec(memory_space=pltpu.SMEM)] + [whole] * (len(operands) - 1),
        out_specs=[whole] * len(out_shape),
        scratch_shapes=[
            pltpu.VMEM((2 * rows, wide), BF16),
            pltpu.VMEM((HEAD_DIM, 2 * rows), BF16),
            pltpu.VMEM((2 * rows, wide), BF16),
            pltpu.VMEM((2 * rows, wide), BF16),
            pltpu.VMEM((wide, 2 * rows), BF16),
            pltpu.VMEM((wide, 2 * rows), BF16),
            pltpu.VMEM((8, 2 * rows), F32),
            pltpu.VMEM((8, 2 * rows), F32),
            pltpu.VMEM((2 * rows, wide), F32),
        ],
        compiler_params=pltpu.CompilerParams(vmem_limit_bytes=58 << 20),
        cost_estimate=pl.CostEstimate(
            flops=8_000_000_000, bytes_accessed=6 << 20, transcendentals=1 << 20
        ),
        name="attention_backward_two" if last else "attention_backward_one",
    )(*operands)


def on_device(
    tokens,
    block_ids,
    ln1_gain,
    ln1_shift,
    qkv_weight,
    qv_bias,
    out_weight,
    out_bias,
    ln2_gain,
    ln2_shift,
    up_weight,
    up_bias,
    down_weight,
    down_bias,
    cotangent,
):
    x, zl, core, y, zh = (lax.axis_index(name) for name in AXES)
    place = jnp.stack([x, zl, core, y, zh]).astype(jnp.int32)
    width = tokens.shape[1]
    gain_one, shift_one, gain_two, shift_two, bias_out = (
        values.astype(F32)[None]
        for values in (ln1_gain, ln1_shift, ln2_gain, ln2_shift, out_bias)
    )

    pieces = gather_y(tokens)
    own3 = qkv_weight.transpose(1, 0, 2)
    near3 = swap(halves(own3, 1, core)[0], "zh")
    far3 = swap(near3, "co")
    out_kept = halves(out_weight, 0, core)[0]
    biases = jnp.concatenate([qv_bias.reshape(256), up_bias])
    biases = jnp.pad(biases[None], ((0, 15), (0, width - 768)))
    out_near = swap(jnp.concatenate([out_kept, biases]), "zh")
    pair_bias, pair_up_bias = out_near[HEAD_DIM, :256].reshape(2, 128), out_near[HEAD_DIM, 256:768]
    out_kept = jnp.concatenate([out_kept, out_near[:HEAD_DIM]])

    table = gather(block_ids, ("x", "zl", "co"), 16)
    counts = jnp.sum(
        (table.reshape(-1)[None, :] <= jnp.arange(128, dtype=jnp.int32)[:, None]).astype(jnp.int32),
        axis=1,
    )
    places = (4 * x + core, 14 - 4 * x + core, 4 * x + 1 - core, 15 - 4 * x - core)
    query_ids = jnp.concatenate([lax.dynamic_index_in_dim(table, p, 0, False) for p in places])
    same = query_ids[None, :] == jnp.arange(128, dtype=jnp.int32)[:, None]
    end = jnp.sum(jnp.where(same, counts[:, None], 0), axis=0)
    spot = jnp.stack([x, core]).astype(jnp.int32)
    ends = end[: 2 * SLICE].reshape(-1, FWD_Q)
    bounds = [ends[:, 0] // FWD_K, (ends[:, -1] + FWD_K - 1) // FWD_K, (ends[:, -1] + 255) // 256]
    bounds = jnp.stack(bounds, axis=1)
    forward_spot = jnp.concatenate([spot, bounds.reshape(-1)])
    ends = end.reshape(-1, BWD_Q)
    bounds = jnp.stack([ends[:, 0] // SLICE, (ends[:, -1] + SLICE - 1) // SLICE], axis=1)
    bounds = jnp.concatenate([(bounds - core + 1) // 2, (ends[:, -1:] + 255) // 256], axis=1)
    backward_spot = jnp.concatenate([spot, bounds.reshape(-1)])
    end = end[None, :]

    blocks, normed, unit = on_core(
        project_kernel,
        "project",
        [((4, 768, 128), BF16), ((512, width), BF16), ((512, width), BF16)],
        (place, *pieces, gain_one, shift_one, own3, near3, far3, qv_bias, pair_bias),
        800_000_000,
    )
    blocks, forward_spot, backward_spot, end, out_kept = lax.optimization_barrier(
        (blocks, forward_spot, backward_spot, end, out_kept)
    )
    mine = exchange(blocks, ("zl", "zh"))
    up_parts, down_parts = halves(up_weight, 1, core), halves(down_weight, 0, core)
    units = jnp.concatenate(
        [up_parts[0], down_parts[0].reshape(256, 4, 256).transpose(1, 0, 2).reshape(width, 256)]
    )
    rows_here = to_mirror(jnp.stack([tokens, cotangent]), zl)
    units = after(units, mine)
    tokens_here, cotangent_here = rows_here[0], rows_here[1]
    kv = mine[:, :512].reshape(2, 2, 4, 128, 128).transpose(0, 2, 1, 3, 4).reshape(2, SLICE, 128)
    near, next_near = [None] * 2, [None] * 2
    queries = mine[:, 512:].reshape(2, 2, 4, HEAD_DIM, 128).transpose(0, 2, 1, 3, 4)
    queries = queries.reshape(2, 512, 128)
    near[0], next_near[1] = hop(kv[0], 1), hop(jnp.concatenate([kv[1], queries[1]]), 3)
    near[1], next_near[0] = hop(kv[1], 1), hop(kv[0], 3)
    units_near = swap(units, "zh")
    far = [hop(near[0], 3), hop(next_near[1][:SLICE], 1)]
    far, near[1], next_near[0], units_near = lax.optimization_barrier(
        (far, near[1], next_near[0], units_near)
    )
    kv_pieces = [kv.reshape(2 * SLICE, 128), *near, *next_near, *far]
    kv_pieces += [swap(piece, "co") for piece in kv_pieces]

    queries = jnp.concatenate([queries[0], next_near[1][SLICE:]]).reshape(16, HEAD_DIM, 128)
    both = gather_y(jnp.concatenate([cotangent_here, out_kept]))
    state, mixed = attention_forward(forward_spot, queries, end[:, : 2 * SLICE], kv_pieces)
    mixed, both = lax.optimization_barrier((mixed, both))
    out_kept = jnp.concatenate([piece[128:] for piece in both])
    out_sent = swap(out_kept, "co")
    units_far = swap(units_near, "co")

    def parts_of(units):
        return units[:width], units[width:].reshape(4, 256, 256).transpose(1, 0, 2).reshape(256, width)

    (up_near, down_near), (up_far, down_far) = parts_of(units_near), parts_of(units_far)
    ups = (up_parts[0], up_near, up_parts[1], up_far)
    downs = (down_parts[0], down_near, down_parts[1], down_far)
    own_half, pair_half = halves(up_bias, 0, core), halves(pair_up_bias, 0, core)
    up_bias_all = jnp.concatenate([own_half[0], pair_half[0], own_half[1], pair_half[1]])
    up_bias_all = up_bias_all.astype(F32)[None]
    other_state, other_queries = swap(state, "co"), swap(queries, "co")

    heads = exchange(mixed, ("zl", "y", "zh"))
    resid, mid, att = on_core(
        attend_out_kernel,
        "attend_out",
        [((128, width), F32), ((128, width), BF16), ((2, 512, 128), BF16)],
        (place, heads, out_kept, out_sent, tokens_here, bias_out, gain_two, shift_two),
        270_000_000,
    )

    mids = gather_y(mid)
    row = ((128, width), BF16)
    active, grad_hidden, grad_mids, grad_up_bias = on_core(
        feed_forward_kernel,
        "feed_forward",
        [((512, width), BF16)] * 2 + [((4, 128, width), BF16), ((1, 1024), F32)],
        (place, *mids, *both, up_bias_all, *ups, *downs),
        3_300_000_000,
    )
    grad_mids = exchange(grad_mids, "y")
    (sent,) = on_core(
        functools.partial(unit_grads_kernel, False),
        "unit_grads_sent",
        [((8, 2, 128, 512), BF16)],
        (place, *mids, *both, active, grad_hidden),
        6_000_000_000,
    )
    got = swap(sent, "co")
    (ff_blocks,) = on_core(
        functools.partial(unit_grads_kernel, True),
        "unit_grads_kept",
        [((16, 256, 256), BF16)],
        (place, *mids, *both, active, grad_hidden, got),
        6_000_000_000,
        limit=56,
    )
    grad_mids = after(grad_mids, ff_blocks)
    grad_resid, grad_branch, grad_heads, norm_sums = on_core(
        mid_back_kernel,
        "mid_back",
        [((128, width), F32), row, ((16, HEAD_DIM, 128), BF16), ((4, width), F32)],
        (place, grad_mids, resid, cotangent_here, gain_two, out_kept, out_sent),
        270_000_000,
    )

    grad_mixed = exchange(grad_heads, ("zl", "y", "zh"))
    late = after((att, grad_branch, active), grad_heads)
    out_downs = on_core(
        out_down_kernel,
        "out_down",
        [((384, width), BF16)] * 4,
        (place, *late, *downs),
        1_400_000_000,
        limit=56,
    )
    grad_mixed, backward_spot = after((grad_mixed, backward_spot), ff_blocks, out_downs)
    ff_blocks = after(ff_blocks, out_downs)
    out_downs = send_y(out_downs)
    other_grad = swap(grad_mixed, "co")
    ff_shares = exchange(ff_blocks, ("x", "zl", "zh"))
    all_queries, grads = [queries, other_queries], [grad_mixed, other_grad]
    states = [state, other_state]
    partial, to_near, to_far = attention_backward(
        False, backward_spot, all_queries, grads, states, end, [*near, *far]
    )
    from_near, from_far = hop(to_near, 1), hop(to_far, 2)
    grad_q, grad_q_sent, to_next, grad_kv = attention_backward(
        True, backward_spot, all_queries, grads, states, end, [*next_near, kv[0], kv[1]], partial
    )
    to_next, grad_q_sent, from_near, from_far, ff_shares, out_downs = lax.optimization_barrier(
        (to_next, grad_q_sent, from_near, from_far, ff_shares, out_downs)
    )
    from_next = hop(to_next, 3)
    grad_q = total([grad_q, swap(grad_q_sent, "co")]).astype(BF16)
    grad_q = jnp.stack([grad_q[:8], hop(grad_q[8:], 3)])
    grad_q = grad_q.reshape(2, 4, 2, HEAD_DIM, 128).transpose(0, 2, 1, 3, 4).reshape(4, 256, 128)

    grad_kv = total([grad_kv, from_near, from_far, from_next])
    grad_kv = grad_kv.astype(BF16).reshape(2, SLICE, 128)
    blocks = jnp.concatenate([to_z(grad_kv), grad_q], axis=1)
    ff_shares, out_downs = after((ff_shares, out_downs), blocks)
    blocks = exchange(blocks, ("zl", "zh"))

    ff_share = jnp.sum(ff_shares.astype(F32), axis=0)
    ff_share = jnp.concatenate(
        [ff_share[:128].T, ff_share[128:, :128], ff_share[128:, 128:]]
    ).astype(BF16)
    rows_home, out_kept_sum, out_sent_sum = on_core(
        out_sums_kernel,
        "out_sums",
        [((2, 128, width), F32), ((4, 2, 2, HEAD_DIM, 128), F32), ((4, 2, 2, HEAD_DIM, 128), BF16)],
        (place, *out_downs, resid, down_bias.astype(F32)[None], grad_resid),
        1_000_000,
    )
    unit, out_sent_sum = after((unit, out_sent_sum), rows_home)
    out_got = swap(out_sent_sum, "co")

    *grad_normed, part_sums = on_core(
        project_back_kernel,
        "project_back",
        [row] * 4 + [((2, width), F32)],
        (place, blocks, unit, own3, near3, far3),
        800_000_000,
        scratch=[pltpu.VMEM((512, width), F32)],
    )
    grad_normed = send_y(grad_normed)
    blocks, ff_share = after((blocks, ff_share), part_sums)
    ff_rest = gather(ff_share, ("x", "zl"), 8)

    head_kept, head_sent, head_sums = on_core(
        qkv_grads_kernel,
        "qkv_grads",
        [((4, 2, 2, 192, 128), BF16)] * 2 + [((4, 192, 128), F32)],
        (place, blocks, normed),
        900_000_000,
    )
    head_got = swap(head_sent, "co")
    rows_home = to_mirror(after(rows_home, head_got), zl)

    head_sums = head_sums[:, :, 0].reshape(2, 2, 3, HEAD_DIM)
    bias = jnp.stack([head_sums[:, :, 2], head_sums[:, :, 1]]).transpose(2, 0, 1, 3)
    up_sums = grad_up_bias.reshape(2, 2, 256)
    up_sums = turned(turned(up_sums, 0, core), 1, zh).transpose(1, 0, 2).reshape(1, width)
    bias = jnp.pad(bias.reshape(1, 512), ((0, 0), (0, 512)))
    small = jnp.concatenate([part_sums, norm_sums, up_sums, bias])
    small = small + swap(small, "co")
    (shares,) = on_core(
        shares_kernel,
        "shares",
        [((16, 272, 128), BF16)],
        (place, head_kept, head_got, out_kept_sum, out_got, small),
        1_000_000,
    )
    shares = exchange(shares, ("x", "zl", "zh"))
    share = jnp.sum(shares.astype(F32), axis=0).astype(BF16)
    rest = gather(share, ("x", "zl"), 8)
    small = rest[:, 256:264].astype(F32).transpose(1, 0, 2).reshape(8, width)
    small = jnp.concatenate([total(gather_y(small[:6])), small[6:]])
    grad_up_bias = lax.dynamic_slice_in_dim(small[6], zh * 512, 512, 0)
    grad_qv_bias = lax.dynamic_slice_in_dim(small[7], zh * 256, 256, 0).reshape(2, 128)

    (grad_tokens,) = on_core(
        last_norm_kernel,
        "last_norm",
        [((128, width), F32)],
        (place, *grad_normed, tokens, gain_one, rows_home[1]),
        1_000_000,
    )
    grad_down_weight, grad_up_weight = on_core(
        unit_weights_kernel,
        "unit_weights",
        [((512, width), F32), ((width, 512), F32)],
        (place, ff_rest, swap(ff_rest, "co")),
        1_000_000,
    )
    grad_qkv_weight, grad_out_weight = on_core(
        head_weights_kernel,
        "head_weights",
        [((3, width, 128), F32), ((128, width), F32)],
        (place, rest, swap(rest, "co")),
        1_000_000,
    )
    return (
        rows_home[0],
        grad_tokens,
        small[0],
        small[1],
        grad_qkv_weight.transpose(1, 0, 2),
        grad_qv_bias,
        grad_out_weight,
        small[2],
        small[3],
        small[4],
        grad_up_weight,
        grad_up_bias,
        grad_down_weight,
        small[5],
    )


def solution(mesh):
    fine = Mesh(mesh.devices.reshape(4, 2, 2, 4, 2), AXES)
    slices, shards = ("x", "zl", "co"), ("y", "zh")
    return jax.shard_map(
        on_device,
        mesh=fine,
        in_specs=(
            P(AXES, None),
            P(slices),
            P(),
            P(),
            P(None, None, shards),
            P(None, shards),
            P(shards, None),
            P(),
            P(),
            P(),
            P(None, shards),
            P(shards),
            P(shards, None),
            P(),
            P(AXES, None),
        ),
        out_specs=(
            P(AXES, None),
            P(AXES, None),
            P(),
            P(),
            P(None, None, shards),
            P(None, shards),
            P(shards, None),
            P(),
            P(),
            P(),
            P(None, shards),
            P(shards),
            P(shards, None),
            P(),
        ),
        check_vma=False,
    )
```

```python
import functools

import jax
import jax.numpy as jnp
from jax import lax
from jax.experimental import pallas as pl
from jax.experimental.pallas import tpu as pltpu
from jax.sharding import Mesh
from jax.sharding import PartitionSpec as P

HEAD_DIM = 64
EPSILON = 1e-05
MASKED = -1e30
LOG2E = 1.4426950408889634
TO_LOG2 = LOG2E * HEAD_DIM ** (-0.5)
AXES = ("x", "zl", "co", "y", "zh")
BF16, F32 = jnp.bfloat16, jnp.float32
SLICE = 1024
FWD_Q, FWD_K = 1024, 1024
BWD_Q = 1024


def contract(left, right, left_dim, right_dim):
    return lax.dot_general(
        left, right, (((left_dim,), (right_dim,)), ((), ())), preferred_element_type=F32
    )


def matmul(left, right):
    return contract(left, right, 1, 0)


def shift(values, steps):
    return lax.ppermute(values, "y", [(i, (i + steps) % 4) for i in range(4)])


def hop(values, bit, axis="x"):
    return lax.ppermute(values, axis, [(i, i ^ bit) for i in range(4)])


def swap(values, axis):
    return lax.ppermute(values, axis, [(0, 1), (1, 0)])


def to_mirror(rows, zl):
    moved = lax.ppermute(rows, ("x", "zl"), [(i, 8 - i) for i in (1, 3, 5, 7)])
    return jnp.where(zl == 0, rows, moved)


def exchange(blocks, axes):
    return lax.all_to_all(blocks, axes, 0, 0, tiled=True)


def gather(rows, axes, size):
    return exchange(jnp.broadcast_to(rows[None], (size,) + rows.shape), axes)


def gather_y(rows):
    one, three = shift(rows, 1), shift(rows, 3)
    return rows, one, shift(rows, 2), three


def send_y(blocks):
    return blocks[0], shift(blocks[1], -1), shift(blocks[3], -3), shift(blocks[2], -2)


def total(parts):
    return functools.reduce(jnp.add, [part.astype(F32) for part in parts])


def after(value, *others):
    return lax.optimization_barrier((value, others))[0]


def turned(values, dim, index):
    return jnp.where(index == 0, values, jnp.flip(values, dim))


def halves(values, dim, index):
    half = values.shape[dim] // 2
    return (
        lax.dynamic_slice_in_dim(values, index * half, half, dim),
        lax.dynamic_slice_in_dim(values, (1 - index) * half, half, dim),
    )


def to_z(rows):
    n = rows.shape[-1]
    return rows.reshape(2, 4, 2, 128, n).transpose(0, 2, 1, 3, 4).reshape(4, 512, n)


def on_core(kernel, name, outputs, operands, flops, limit=32, scratch=()):
    whole = pl.BlockSpec(memory_space=pltpu.VMEM)
    outputs = [jax.ShapeDtypeStruct(shape, dtype) for shape, dtype in outputs]
    return pl.pallas_call(
        kernel,
        out_shape=outputs,
        in_specs=[pl.BlockSpec(memory_space=pltpu.SMEM)] + [whole] * (len(operands) - 1),
        out_specs=[whole] * len(outputs),
        scratch_shapes=list(scratch),
        compiler_params=pltpu.CompilerParams(vmem_limit_bytes=limit << 20),
        cost_estimate=pl.CostEstimate(flops=flops, bytes_accessed=4 << 20, transcendentals=0),
        name=name,
    )(*operands)


def joined(refs, dim=0):
    return jnp.concatenate([ref[...] for ref in refs], axis=dim)


def unit_rows(rows):
    centered = rows - jnp.mean(rows, axis=-1, keepdims=True)
    scale = lax.rsqrt(jnp.mean(centered * centered, axis=-1, keepdims=True) + EPSILON)
    return centered * scale, scale


def norm_back(grad, unit, scale, gain):
    grad = grad * gain
    along = jnp.mean(grad * unit, axis=-1, keepdims=True)
    return scale * (grad - jnp.mean(grad, axis=-1, keepdims=True) - unit * along)


def y_rows(place, steps):
    return pl.ds(pl.multiple_of(((place[3] - steps) & 3) * 128, 128), 128)


def merge_lanes(left, right):
    left, right = left.astype(F32), right.astype(F32)
    first = lax.broadcasted_iota(jnp.int32, left.shape, 1) < HEAD_DIM
    return (
        jnp.where(first, left, pltpu.roll(right, HEAD_DIM, 1)).astype(BF16),
        jnp.where(first, pltpu.roll(left, HEAD_DIM, 1), right).astype(BF16),
    )


def project_kernel(place, *refs):
    pieces, (gain, bent, own, near, far, own_bias, pair_bias) = refs[:4], refs[4:11]
    blocks, normed_ref, unit_ref = refs[11:]
    core, zh = place[2], place[4]
    for steps, piece in enumerate(pieces):
        rows = y_rows(place, steps)
        unit, _ = unit_rows(piece[...].astype(F32))
        unit_ref[rows, :] = unit.astype(BF16)
        normed_ref[rows, :] = (unit * gain[...] + bent[...]).astype(BF16)
    normed = normed_ref[...]
    first = normed_ref[:, pl.ds(pl.multiple_of(core * 512, 512), 512)]
    second = normed_ref[:, pl.ds(pl.multiple_of((1 - core) * 512, 512), 512)]
    for pair in range(2):
        bias = (pair_bias if pair else own_bias)[...].astype(F32)

        def projected(i, pair=pair):
            if pair:
                return matmul(first, near[i]) + matmul(second, far[i])
            return matmul(normed, own[i])

        queries = (projected(0) + bias[:1]).T.astype(BF16)
        mixed = merge_lanes(projected(1).astype(BF16), (projected(2) + bias[1:]).astype(BF16))
        for head in range(2):
            where = 2 * head + (zh ^ pair)
            blocks[where, pl.ds(0, 512), :] = mixed[head]
            for y in range(4):
                lanes = slice(y * 128, y * 128 + 128)
                piece = queries[head * HEAD_DIM : head * HEAD_DIM + HEAD_DIM, lanes]
                blocks[where, pl.ds(512 + y * HEAD_DIM, HEAD_DIM), :] = piece


def project_back_kernel(place, blocks, unit_ref, own, near, far, *refs):
    outs, sums, grad_ref = refs[:4], refs[4], refs[5]
    core, zh = place[2], place[4]
    for pair in range(2):
        heads = [blocks[2 * head + (zh ^ pair)] for head in range(2)]
        keys, values = merge_lanes(heads[0][:512], heads[1][:512])
        queries = [
            jnp.concatenate([head[512 + y * HEAD_DIM :][:HEAD_DIM] for y in range(4)], axis=1)
            for head in heads
        ]
        parts = (jnp.concatenate(queries, axis=0).T, keys, values)

        def back(weight, parts=parts):
            return functools.reduce(
                jnp.add, [contract(part, weight[i], 1, 1) for i, part in enumerate(parts)]
            )

        if pair:
            first = pl.ds(pl.multiple_of(core * 512, 512), 512)
            second = pl.ds(pl.multiple_of((1 - core) * 512, 512), 512)
            grad_ref[:, first] += back(near)
            grad_ref[:, second] += back(far)
        else:
            grad_ref[...] = back(own)
    grad = grad_ref[...]
    sums[...] = jnp.concatenate(
        [
            jnp.sum(grad * unit_ref[...].astype(F32), axis=0, keepdims=True),
            jnp.sum(grad, axis=0, keepdims=True),
        ]
    )
    for steps, out in enumerate(outs):
        out[...] = grad_ref[y_rows(place, steps), :].astype(BF16)


def qkv_grads_kernel(place, blocks_ref, normed_ref, kept, sent, sums_ref):
    normed, ones = normed_ref[...], jnp.ones((512, 128), BF16)
    for head in range(2):
        for zh in range(2):
            block = blocks_ref[2 * head + zh]
            queries = [block[512 + y * HEAD_DIM :][:HEAD_DIM] for y in range(4)]
            left = jnp.concatenate([block[:512].T, jnp.concatenate(queries, axis=1)], axis=0)
            grad = matmul(left, normed)
            for half in range(2):

                def store(ref, grad=grad, half=half, head=head, zh=zh):
                    for chunk in range(4):
                        lanes = slice((4 * half + chunk) * 128, (4 * half + chunk) * 128 + 128)
                        ref[chunk, head, zh] = grad[:, lanes].astype(BF16)

                pl.when(place[2] == half)(functools.partial(store, kept))
                pl.when(place[2] != half)(functools.partial(store, sent))
            sums_ref[2 * head + zh] = matmul(left, ones)


def attend_out_kernel(place, heads, kept, sent, tokens, bias, gain, bent, resid_ref, mid_ref, att_ref):
    core, y, zh = place[2], place[3], place[4]
    for side in range(2):
        for steps in range(4):
            for pair in range(2):
                where = 8 * (core ^ side) + 2 * ((y - steps) & 3) + (zh ^ pair)
                att_ref[side, pl.ds(steps * 128 + pair * HEAD_DIM, HEAD_DIM), :] = heads[where]
    branch = matmul(att_ref[0].T, kept[...]) + matmul(att_ref[1].T, sent[...])
    resid = tokens[...].astype(F32) + branch + bias[...]
    resid_ref[...] = resid
    mid_ref[...] = (unit_rows(resid)[0] * gain[...] + bent[...]).astype(BF16)


def mid_back_kernel(place, *refs):
    parts, resid, cotangent, gain, kept, sent = refs[:6]
    grad_resid_ref, branch_ref, heads, sums = refs[6:]
    core, y, zh = place[2], place[3], place[4]
    grad = total([parts[i] for i in range(4)])
    unit, scale = unit_rows(resid[...])
    cot = cotangent[...].astype(F32)
    grad_resid = cot + norm_back(grad, unit, scale, gain[...])
    grad_resid_ref[...] = grad_resid
    branch = grad_resid.astype(BF16)
    branch_ref[...] = branch
    rows = [grad_resid, grad * unit, grad, cot]
    sums[...] = jnp.concatenate([jnp.sum(row, axis=0, keepdims=True) for row in rows])
    for side, weight in enumerate((kept, sent)):
        grads = contract(weight[...], branch, 1, 1).astype(BF16)
        for steps in range(4):
            for pair in range(2):
                where = 8 * (core ^ side) + 2 * ((y - steps) & 3) + (zh ^ pair)
                start = steps * 128 + pair * HEAD_DIM
                heads[where] = grads[start : start + HEAD_DIM]


def feed_forward_kernel(place, *refs):
    mids, cots, (bias,), ups, downs = refs[:4], refs[4:8], refs[8:9], refs[9:13], refs[13:17]
    active_ref, grad_ref, out, bias_grad = refs[17:]
    mid, cot = joined(mids), jnp.concatenate([ref[:128, :] for ref in cots])
    summed = None
    for i, (up_ref, down_ref) in enumerate(zip(ups, downs)):
        span = pl.ds(i * 256, 256)
        up = up_ref[...]
        hidden = matmul(mid, up) + bias[:, span]
        square = hidden * hidden
        bent = jnp.tanh(0.7978845608028654 * hidden * (1.0 + 0.044715 * square))
        active_ref[:, span] = (0.5 * hidden * (1.0 + bent)).astype(BF16)
        slope = 0.7978845608028654 * (1.0 + 3.0 * 0.044715 * square)
        slope = 0.5 * (1.0 + bent) + 0.5 * hidden * (1.0 - bent * bent) * slope
        grad = (slope * contract(cot, down_ref[...], 1, 1)).astype(BF16)
        grad_ref[:, span] = grad
        bias_grad[:, span] = jnp.sum(grad.astype(F32), axis=0, keepdims=True)
        part = contract(grad, up, 1, 1)
        summed = part if summed is None else summed + part
    for steps in range(4):
        piece = summed[steps * 128 : steps * 128 + 128].astype(BF16)
        out[(place[3] - steps) & 3] = piece


def unit_grads_kernel(kept, place, *refs):
    mids, cots, active, grad = refs[:4], refs[4:8], refs[8], refs[9]
    got, out = (refs[10], refs[11]) if kept else (None, refs[10])
    span = pl.ds(0 if kept else 512, 512)
    cot = jnp.concatenate([ref[:128, :] for ref in cots])
    for i, (left, right) in enumerate(((cot, active), (joined(mids), grad))):
        summed = contract(left, right[:, span], 0, 0)
        for share in range(8):
            block = summed[share * 128 : share * 128 + 128]
            if kept:
                block = (block + got[share, i].astype(F32)).astype(BF16)
                for pair in range(2):
                    half = block[:, pair * 256 : pair * 256 + 256]
                    out[2 * share + (place[4] ^ pair), pl.ds(i * 128, 128), :] = half
            else:
                out[share, i] = block.astype(BF16)


def out_down_kernel(place, att, branch, active, *refs):
    downs, outs = refs[:4], refs[4:]
    grads = [matmul(att[side], branch[...]).astype(BF16) for side in range(2)]
    down = total([matmul(active[:, i * 256 : i * 256 + 256], ref[...]) for i, ref in enumerate(downs)])
    for steps, out in enumerate(outs):
        rows = slice(steps * 128, steps * 128 + 128)
        out[pl.ds(0, 128), :] = grads[0][rows]
        out[pl.ds(128, 128), :] = grads[1][rows]
        out[pl.ds(256, 128), :] = down[rows].astype(BF16)


def out_sums_kernel(place, *refs):
    parts, (resid, bias, grad_resid, home, kept, sent) = refs[:4], refs[4:]
    home[0] = total([part[256:, :] for part in parts]) + resid[...] + bias[...]
    home[1] = grad_resid[...]
    for side, ref in enumerate((kept, sent)):
        summed = total([part[side * 128 : side * 128 + 128, :] for part in parts]).astype(ref.dtype)
        for pair in range(2):
            for share in range(8):
                lanes = slice(share * 128, share * 128 + 128)
                piece = summed[pair * HEAD_DIM : pair * HEAD_DIM + HEAD_DIM, lanes]
                ref[share // 2, share % 2, pair] = piece


def shares_kernel(place, heads, head_got, out, out_got, small, shares):
    for x in range(4):
        for zl in range(2):
            share = 2 * x + zl
            for zh in range(2):
                to = 2 * share + zh
                grad = total([heads[x, zl, zh], head_got[x, zl, zh]])
                shares[to, pl.ds(0, 192), :] = grad.astype(BF16)
                grad = total([out[x, zl, zh], out_got[x, zl, zh]])
                shares[2 * share + (place[4] ^ zh), pl.ds(192, HEAD_DIM), :] = grad.astype(BF16)
                rows = small[:, share * 128 : share * 128 + 128]
                rows = jnp.concatenate([rows, jnp.zeros_like(rows)]).astype(BF16)
                shares[to, pl.ds(256, 16), :] = rows


def last_norm_kernel(place, *refs):
    parts, (tokens, gain, resid, out) = refs[:4], refs[4:]
    unit, scale = unit_rows(tokens[...].astype(F32))
    out[...] = resid[...] + norm_back(total([part[...] for part in parts]), unit, scale, gain[...])


def unit_weights_kernel(place, own, other, down, up):
    for side, ref in enumerate((own, other)):
        half = place[2] ^ side
        for share in range(8):
            lanes = pl.ds(share * 128, 128)
            down[pl.ds(pl.multiple_of(half * 256, 256), 256), lanes] = ref[share, :256].astype(F32)
            for part in range(2):
                lanes = pl.ds(pl.multiple_of(half * 256 + part * 128, 128), 128)
                piece = ref[share, pl.ds(256 + part * 128, 128), :].astype(F32)
                up[pl.ds(share * 128, 128), lanes] = piece


def head_weights_kernel(place, own, other, qkv, out):
    for side, ref in enumerate((own, other)):
        half = place[2] ^ side
        for x in range(4):
            rows = pl.ds(pl.multiple_of(half * 512 + x * 128, 128), 128)
            for i, which in enumerate((1, 2, 0)):
                span = pl.ds(i * HEAD_DIM, HEAD_DIM)
                both = jnp.concatenate([ref[2 * x, span, :], ref[2 * x + 1, span, :]])
                qkv[which, rows, :] = both.astype(F32).T
            for zl in range(2):
                piece = ref[2 * x + zl, pl.ds(192, HEAD_DIM), :].astype(F32)
                span = pl.ds(pl.multiple_of(half * HEAD_DIM, HEAD_DIM), HEAD_DIM)
                out[span, pl.ds((2 * x + zl) * 128, 128)] = piece


def forward_kernel(spot, q_ref, end_ref, *refs):
    pieces, (state_ref, out, kv_ref, vt_ref, qt_ref) = refs[:14], refs[14:]
    x, core = spot[0], spot[1]

    def bring(piece, half, x_from, slice_in_x, parity):
        where = (4 * x_from + 2 * slice_in_x + parity) * SLICE
        rows = pl.ds(pl.multiple_of(where, SLICE), SLICE)
        kv_ref[rows, :] = piece[pl.ds(half * SLICE, SLICE), :]

    for side in range(2):
        parity = core if side == 0 else 1 - core
        pieces_here = pieces[7 * side : 7 * side + 7]
        bring(pieces_here[0], 0, x, 0, parity)
        bring(pieces_here[0], 1, x, 1, parity)
        for i, piece in enumerate(pieces_here[1:]):
            bring(piece, 0, x ^ (1, 1, 3, 3, 2, 2)[i], i % 2, parity)
    qt_ref[HEAD_DIM:, :] = jnp.zeros((HEAD_DIM, 2 * SLICE), BF16)
    for chunk in range(16):
        qt_ref[:HEAD_DIM, pl.ds(chunk * 128, 128)] = q_ref[chunk]
    vt_ref[HEAD_DIM:, :] = jnp.ones((16, vt_ref.shape[1]), BF16)
    def turn(i, largest):
        rows = pl.ds(pl.multiple_of(i * SLICE, SLICE), SLICE)
        both = kv_ref[rows, :].T
        vt_ref[:HEAD_DIM, rows] = both[HEAD_DIM:, :]
        keys = both[:HEAD_DIM, :].astype(F32)
        return jnp.maximum(largest, jnp.sum(keys * keys, axis=0, keepdims=True))

    longest = jnp.max(lax.fori_loop(0, 16, turn, jnp.zeros((1, SLICE), F32)))
    norms = qt_ref[:HEAD_DIM, :].astype(F32)
    norms = jnp.sum(norms * norms, axis=0, keepdims=True)
    limit = jnp.sqrt(norms * longest) * TO_LOG2
    level = limit - 90.0

    def finish(total, log_top, start, wide):
        span = pl.ds(start, wide)
        weight_sum = total[HEAD_DIM : HEAD_DIM + 1]
        mixed = total[:HEAD_DIM] / weight_sum
        state_ref[:HEAD_DIM, span] = mixed
        for chunk in range(wide // 128):
            piece = mixed[:, chunk * 128 : chunk * 128 + 128].astype(BF16)
            out[start // 128 + chunk] = piece
        state_ref[HEAD_DIM:, span] = jnp.broadcast_to(log_top + jnp.log2(weight_sum), (8, wide))

    def masked_at(values, begin, end, other):
        place = begin + lax.broadcasted_iota(jnp.int32, values.shape, 0)
        return jnp.where(place < end, values, other)

    def bounded_tile(tile):
        span = pl.ds(tile * FWD_Q, FWD_Q)
        query, end = qt_ref[:, span], end_ref[:, span]
        base = level[:, tile * FWD_Q : tile * FWD_Q + FWD_Q]

        def step(masked, keys, at, total):
            for piece in range(max(keys // 512, 1)):
                size = min(keys, 512)
                begin = pl.multiple_of(at * keys + piece * size, size)
                rows = pl.ds(begin, size)
                weights = jnp.exp2(matmul(kv_ref[rows, :], query) * TO_LOG2 - base)
                if masked:
                    weights = masked_at(weights, begin, end, 0.0)
                total = total + matmul(vt_ref[:, rows], weights.astype(BF16))
            return total

        total = jnp.zeros((HEAD_DIM + 16, FWD_Q), F32)
        full, last, pieces = spot[2 + 3 * tile], spot[3 + 3 * tile], spot[4 + 3 * tile]
        total = lax.fori_loop(0, full, functools.partial(step, False, FWD_K), total)

        def edge(at, total):
            left = pieces - 4 * at
            long = left > 2
            ranges = ((FWD_K, at, jnp.where(long, 1, 0)), (256, 4 * at, jnp.where(long, 0, left)))
            for keys, begin, count in ranges:
                masked = functools.partial(step, True, keys)
                total = lax.fori_loop(begin, begin + count, masked, total)
            return total

        total = lax.fori_loop(full, last, edge, total)
        finish(total, base, tile * FWD_Q, FWD_Q)

    def running_tile(tile):
        wide = FWD_Q // 2
        starts = [tile * FWD_Q, tile * FWD_Q + wide]
        queries = [qt_ref[:, pl.ds(start, wide)] for start in starts]
        ends = [end_ref[:, pl.ds(start, wide)] for start in starts]

        def step(masked, at, carry):
            rows = pl.ds(pl.multiple_of(at * FWD_K, FWD_K), FWD_K)
            kv, vt = kv_ref[rows, :], vt_ref[:, rows]
            scores = [matmul(kv, query) for query in queries]
            after = []
            for (top, total), score, end in zip(carry, scores, ends):
                if masked:
                    score = masked_at(score, at * FWD_K, end, MASKED)
                new_top = jnp.maximum(top, jnp.max(score, axis=0, keepdims=True))
                weights = jnp.exp2(score * TO_LOG2 - new_top * TO_LOG2)
                factor = jnp.exp2((top - new_top) * TO_LOG2)
                total = total * factor + matmul(vt, weights.astype(BF16))
                after.append((new_top, total))
            return tuple(after)

        begin = (jnp.full((1, wide), MASKED, F32), jnp.zeros((HEAD_DIM + 16, wide), F32))
        full, last = spot[2 + 3 * tile], spot[3 + 3 * tile]
        carry = lax.fori_loop(0, full, functools.partial(step, False), (begin, begin))
        carry = lax.fori_loop(full, last, functools.partial(step, True), carry)
        for (top, total), start in zip(carry, starts):
            finish(total, top * TO_LOG2, start, wide)

    small = jnp.max(limit) <= 100.0

    @pl.when(small)
    def _():
        for tile in range(2 * SLICE // FWD_Q):
            bounded_tile(tile)

    @pl.when(jnp.logical_not(small))
    def _():
        for tile in range(2 * SLICE // FWD_Q):
            running_tile(tile)


def attention_forward(spot, queries, end, pieces):
    rows, total = 2 * SLICE, 16 * SLICE
    whole = pl.BlockSpec(memory_space=pltpu.VMEM)
    return pl.pallas_call(
        forward_kernel,
        out_shape=[
            jax.ShapeDtypeStruct((HEAD_DIM + 8, rows), F32),
            jax.ShapeDtypeStruct((16, HEAD_DIM, 128), BF16),
        ],
        in_specs=[pl.BlockSpec(memory_space=pltpu.SMEM)] + [whole] * 16,
        out_specs=[whole] * 2,
        scratch_shapes=[
            pltpu.VMEM((total, 2 * HEAD_DIM), BF16),
            pltpu.VMEM((HEAD_DIM + 16, total), BF16),
            pltpu.VMEM((2 * HEAD_DIM, rows), BF16),
        ],
        compiler_params=pltpu.CompilerParams(vmem_limit_bytes=40 << 20),
        cost_estimate=pl.CostEstimate(
            flops=20_000_000_000, bytes_accessed=9 << 20, transcendentals=1 << 20
        ),
        name="attention_forward",
    )(spot, queries, end, *pieces)


def backward_kernel(last, spot, *refs):
    q_refs, do_refs, state_refs, (end_ref, *kv_refs) = refs[:2], refs[2:4], refs[4:6], refs[6:11]
    if last:
        partial_ref, *refs = refs[11:]
        dq_refs, dkv_refs, scratch = refs[:2], refs[2:4], refs[4:]
    else:
        partial_ref, dkv_refs, scratch = refs[11], refs[12:14], refs[14:]
    kv_ref, kt_ref, q_ref, do_ref, qt_ref, dot_ref, lse_ref, delta_ref, sum_ref = scratch
    x, core = spot[0], spot[1]
    per_core = 2 * SLICE
    none = jnp.zeros((HEAD_DIM, 2 * per_core), BF16)
    qt_ref[HEAD_DIM:, :] = none
    dot_ref[:HEAD_DIM, :] = none
    for side in range(2):
        for chunk in range(16):
            lanes = pl.ds(side * per_core + chunk * 128, 128)
            qt_ref[:HEAD_DIM, lanes] = q_refs[side][chunk]
            dot_ref[HEAD_DIM:, lanes] = do_refs[side][chunk]
        rows = pl.ds(side * per_core, per_core)
        q_ref[rows, :] = qt_ref[:, rows].T
        do_ref[rows, :] = dot_ref[:, rows].T
        state = state_refs[side]
        lse_ref[:, rows] = state[HEAD_DIM:, :]
        product = state[:HEAD_DIM, :] * dot_ref[HEAD_DIM:, rows].astype(F32)
        delta_ref[:, rows] = jnp.broadcast_to(jnp.sum(product, axis=0, keepdims=True), (8, per_core))
    for i, ref in enumerate(kv_refs):
        rows = pl.ds(i * SLICE, SLICE)
        kv_ref[rows, :] = ref[:SLICE, :]
        kt_ref[:, rows] = kv_ref[rows, :].T[:HEAD_DIM, :]
    sum_ref[...] = jnp.zeros_like(sum_ref)

    @pl.loop(0, 2 * per_core // BWD_Q)
    def _(tile):
        span = pl.ds(pl.multiple_of(tile * BWD_Q, BWD_Q), BWD_Q)
        query_t, grad_t = qt_ref[:, span], dot_ref[:, span]
        query, grad = q_ref[span, :], do_ref[span, :]
        end, lse, delta = end_ref[:, span], lse_ref[:1, span], delta_ref[:1, span]
        full, upto, pieces = spot[2 + 3 * tile], spot[3 + 3 * tile], spot[4 + 3 * tile]

        def step(masked, keys, block, at, grad_query):
            held = pl.ds(pl.multiple_of(block * per_core + at * keys, keys), keys)
            kv = kv_ref[held, :]
            weights = jnp.exp2(matmul(kv, query_t) * TO_LOG2 - lse)
            if masked:
                slices = at // (SLICE // keys)
                begin = (4 * x_of[block] + slices + core) * SLICE + at * keys
                place = begin + lax.broadcasted_iota(jnp.int32, weights.shape, 0)
                weights = jnp.where(place < end, weights, 0.0)
            grad_scores = (weights * (matmul(kv, grad_t) - delta)).astype(BF16)
            sum_ref[held, :] += matmul(weights.astype(BF16), grad) + matmul(grad_scores, query)
            return grad_query + matmul(kt_ref[:, held], grad_scores)

        x_of = [x ^ 3, x] if last else [x ^ 1, x ^ 2]
        grad_query = partial_ref[:, span] if last else jnp.zeros((HEAD_DIM, BWD_Q), F32)
        for block in range(2):
            whole = jnp.clip(full - 2 * x_of[block], 0, 2)
            some = jnp.clip(upto - 2 * x_of[block], 0, 2)
            plain = functools.partial(step, False, SLICE, block)
            grad_query = lax.fori_loop(0, whole, plain, grad_query)

            def edge(at, grad_query, block=block):
                left = pieces - 4 * (4 * x_of[block] + 2 * at + core)
                long = left > 2
                ranges = ((SLICE, at, jnp.where(long, 1, 0)), (256, 4 * at, jnp.where(long, 0, left)))
                for keys, begin, count in ranges:
                    masked = functools.partial(step, True, keys, block)
                    grad_query = lax.fori_loop(begin, begin + count, masked, grad_query)
                return grad_query

            grad_query = lax.fori_loop(whole, some, edge, grad_query)
        if last:
            done = (grad_query * HEAD_DIM ** (-0.5)).astype(BF16)
            chunks = BWD_Q // 128
            for side in range(2):

                @pl.when(tile // (per_core // BWD_Q) == side)
                def _(side=side):
                    base = (tile - side * (per_core // BWD_Q)) * chunks
                    for chunk in range(chunks):
                        dq_refs[side][base + chunk] = done[:, chunk * 128 : chunk * 128 + 128]

        else:
            partial_ref[:, span] = grad_query

    is_key = lax.broadcasted_iota(jnp.int32, (1, 2 * HEAD_DIM), 1) < HEAD_DIM
    scale = jnp.where(is_key, HEAD_DIM ** (-0.5), 1.0)
    for block in range(2):
        dkv_refs[block][...] = (sum_ref[pl.ds(block * per_core, per_core), :] * scale).astype(BF16)


def attention_backward(last, spot, queries, grads, states, end, kvs, partial=None):
    rows, wide = 2 * SLICE, 2 * HEAD_DIM
    whole = pl.BlockSpec(memory_space=pltpu.VMEM)
    block = jax.ShapeDtypeStruct((rows, wide), BF16)
    if last:
        out_shape = [jax.ShapeDtypeStruct((16, HEAD_DIM, 128), BF16)] * 2 + [block] * 2
        operands = (spot, *queries, *grads, *states, end, *kvs, partial)
    else:
        out_shape = [jax.ShapeDtypeStruct((HEAD_DIM, 2 * rows), F32), block, block]
        operands = (spot, *queries, *grads, *states, end, *kvs)
    return pl.pallas_call(
        functools.partial(backward_kernel, last),
        out_shape=out_shape,
        in_specs=[pl.BlockSpec(memory_space=pltpu.SMEM)] + [whole] * (len(operands) - 1),
        out_specs=[whole] * len(out_shape),
        scratch_shapes=[
            pltpu.VMEM((2 * rows, wide), BF16),
            pltpu.VMEM((HEAD_DIM, 2 * rows), BF16),
            pltpu.VMEM((2 * rows, wide), BF16),
            pltpu.VMEM((2 * rows, wide), BF16),
            pltpu.VMEM((wide, 2 * rows), BF16),
            pltpu.VMEM((wide, 2 * rows), BF16),
            pltpu.VMEM((8, 2 * rows), F32),
            pltpu.VMEM((8, 2 * rows), F32),
            pltpu.VMEM((2 * rows, wide), F32),
        ],
        compiler_params=pltpu.CompilerParams(vmem_limit_bytes=44 << 20),
        cost_estimate=pl.CostEstimate(
            flops=8_000_000_000, bytes_accessed=6 << 20, transcendentals=1 << 20
        ),
        name="attention_backward_two" if last else "attention_backward_one",
    )(*operands)


def on_device(
    tokens,
    block_ids,
    ln1_gain,
    ln1_shift,
    qkv_weight,
    qv_bias,
    out_weight,
    out_bias,
    ln2_gain,
    ln2_shift,
    up_weight,
    up_bias,
    down_weight,
    down_bias,
    cotangent,
):
    x, zl, core, y, zh = (lax.axis_index(name) for name in AXES)
    place = jnp.stack([x, zl, core, y, zh]).astype(jnp.int32)
    width = tokens.shape[1]
    gain_one, shift_one, gain_two, shift_two, bias_out = (
        values.astype(F32)[None]
        for values in (ln1_gain, ln1_shift, ln2_gain, ln2_shift, out_bias)
    )

    pieces = gather_y(tokens)
    own3 = qkv_weight.transpose(1, 0, 2)
    near3 = swap(halves(own3, 1, core)[0], "zh")
    far3 = swap(near3, "co")
    out_kept = halves(out_weight, 0, core)[0]
    biases = jnp.concatenate([qv_bias.reshape(256), up_bias])
    biases = jnp.pad(biases[None], ((0, 15), (0, width - 768)))
    out_near = swap(jnp.concatenate([out_kept, biases]), "zh")
    pair_bias, pair_up_bias = out_near[HEAD_DIM, :256].reshape(2, 128), out_near[HEAD_DIM, 256:768]
    out_kept = jnp.concatenate([out_kept, out_near[:HEAD_DIM]])

    table = gather(block_ids, ("x", "zl", "co"), 16)
    counts = jnp.sum(
        (table.reshape(-1)[None, :] <= jnp.arange(128, dtype=jnp.int32)[:, None]).astype(jnp.int32),
        axis=1,
    )
    places = (4 * x + core, 14 - 4 * x + core, 4 * x + 1 - core, 15 - 4 * x - core)
    query_ids = jnp.concatenate([lax.dynamic_index_in_dim(table, p, 0, False) for p in places])
    same = query_ids[None, :] == jnp.arange(128, dtype=jnp.int32)[:, None]
    end = jnp.sum(jnp.where(same, counts[:, None], 0), axis=0)
    spot = jnp.stack([x, core]).astype(jnp.int32)
    ends = end[: 2 * SLICE].reshape(-1, FWD_Q)
    bounds = [ends[:, 0] // FWD_K, (ends[:, -1] + FWD_K - 1) // FWD_K, (ends[:, -1] + 255) // 256]
    bounds = jnp.stack(bounds, axis=1)
    forward_spot = jnp.concatenate([spot, bounds.reshape(-1)])
    ends = end.reshape(-1, BWD_Q)
    bounds = jnp.stack([ends[:, 0] // SLICE, (ends[:, -1] + SLICE - 1) // SLICE], axis=1)
    bounds = jnp.concatenate([(bounds - core + 1) // 2, (ends[:, -1:] + 255) // 256], axis=1)
    backward_spot = jnp.concatenate([spot, bounds.reshape(-1)])
    end = end[None, :]

    blocks, normed, unit = on_core(
        project_kernel,
        "project",
        [((4, 768, 128), BF16), ((512, width), BF16), ((512, width), BF16)],
        (place, *pieces, gain_one, shift_one, own3, near3, far3, qv_bias, pair_bias),
        800_000_000,
    )
    blocks, forward_spot, backward_spot, end, out_kept = lax.optimization_barrier(
        (blocks, forward_spot, backward_spot, end, out_kept)
    )
    mine = exchange(blocks, ("zl", "zh"))
    up_parts, down_parts = halves(up_weight, 1, core), halves(down_weight, 0, core)
    units = jnp.concatenate(
        [up_parts[0], down_parts[0].reshape(256, 4, 256).transpose(1, 0, 2).reshape(width, 256)]
    )
    rows_here = to_mirror(jnp.stack([tokens, cotangent]), zl)
    units = after(units, mine)
    tokens_here, cotangent_here = rows_here[0], rows_here[1]
    kv = mine[:, :512].reshape(2, 2, 4, 128, 128).transpose(0, 2, 1, 3, 4).reshape(2, SLICE, 128)
    near, next_near = [None] * 2, [None] * 2
    queries = mine[:, 512:].reshape(2, 2, 4, HEAD_DIM, 128).transpose(0, 2, 1, 3, 4)
    queries = queries.reshape(2, 512, 128)
    near[0], next_near[1] = hop(kv[0], 1), hop(jnp.concatenate([kv[1], queries[1]]), 3)
    near[1], next_near[0] = hop(kv[1], 1), hop(kv[0], 3)
    units_near = swap(units, "zh")
    far = [hop(near[0], 3), hop(next_near[1][:SLICE], 1)]
    far, near[1], next_near[0], units_near = lax.optimization_barrier(
        (far, near[1], next_near[0], units_near)
    )
    kv_pieces = [kv.reshape(2 * SLICE, 128), *near, *next_near, *far]
    kv_pieces += [swap(piece, "co") for piece in kv_pieces]

    queries = jnp.concatenate([queries[0], next_near[1][SLICE:]]).reshape(16, HEAD_DIM, 128)
    both = gather_y(jnp.concatenate([cotangent_here, out_kept]))
    state, mixed = attention_forward(forward_spot, queries, end[:, : 2 * SLICE], kv_pieces)
    mixed, both = lax.optimization_barrier((mixed, both))
    out_kept = jnp.concatenate([piece[128:] for piece in both])
    out_sent = swap(out_kept, "co")
    units_far = swap(units_near, "co")

    def parts_of(units):
        return units[:width], units[width:].reshape(4, 256, 256).transpose(1, 0, 2).reshape(256, width)

    (up_near, down_near), (up_far, down_far) = parts_of(units_near), parts_of(units_far)
    ups = (up_parts[0], up_near, up_parts[1], up_far)
    downs = (down_parts[0], down_near, down_parts[1], down_far)
    own_half, pair_half = halves(up_bias, 0, core), halves(pair_up_bias, 0, core)
    up_bias_all = jnp.concatenate([own_half[0], pair_half[0], own_half[1], pair_half[1]])
    up_bias_all = up_bias_all.astype(F32)[None]
    other_state, other_queries = swap(state, "co"), swap(queries, "co")

    heads = exchange(mixed, ("zl", "y", "zh"))
    resid, mid, att = on_core(
        attend_out_kernel,
        "attend_out",
        [((128, width), F32), ((128, width), BF16), ((2, 512, 128), BF16)],
        (place, heads, out_kept, out_sent, tokens_here, bias_out, gain_two, shift_two),
        270_000_000,
    )

    mids = gather_y(mid)
    row = ((128, width), BF16)
    active, grad_hidden, grad_mids, grad_up_bias = on_core(
        feed_forward_kernel,
        "feed_forward",
        [((512, width), BF16)] * 2 + [((4, 128, width), BF16), ((1, 1024), F32)],
        (place, *mids, *both, up_bias_all, *ups, *downs),
        3_300_000_000,
    )
    grad_mids = exchange(grad_mids, "y")
    (sent,) = on_core(
        functools.partial(unit_grads_kernel, False),
        "unit_grads_sent",
        [((8, 2, 128, 512), BF16)],
        (place, *mids, *both, active, grad_hidden),
        6_000_000_000,
    )
    got = swap(sent, "co")
    (ff_blocks,) = on_core(
        functools.partial(unit_grads_kernel, True),
        "unit_grads_kept",
        [((16, 256, 256), BF16)],
        (place, *mids, *both, active, grad_hidden, got),
        6_000_000_000,
        limit=56,
    )
    grad_mids = after(grad_mids, ff_blocks)
    grad_resid, grad_branch, grad_heads, norm_sums = on_core(
        mid_back_kernel,
        "mid_back",
        [((128, width), F32), row, ((16, HEAD_DIM, 128), BF16), ((4, width), F32)],
        (place, grad_mids, resid, cotangent_here, gain_two, out_kept, out_sent),
        270_000_000,
    )

    grad_mixed = exchange(grad_heads, ("zl", "y", "zh"))
    late = after((att, grad_branch, active), grad_heads)
    out_downs = on_core(
        out_down_kernel,
        "out_down",
        [((384, width), BF16)] * 4,
        (place, *late, *downs),
        1_400_000_000,
        limit=56,
    )
    grad_mixed, backward_spot = after((grad_mixed, backward_spot), ff_blocks, out_downs)
    ff_blocks = after(ff_blocks, out_downs)
    out_downs = send_y(out_downs)
    other_grad = swap(grad_mixed, "co")
    ff_shares = exchange(ff_blocks, ("x", "zl", "zh"))
    all_queries, grads = [queries, other_queries], [grad_mixed, other_grad]
    states = [state, other_state]
    partial, to_near, to_far = attention_backward(
        False, backward_spot, all_queries, grads, states, end, [*near, *far]
    )
    from_near, from_far = hop(to_near, 1), hop(to_far, 2)
    grad_q, grad_q_sent, to_next, grad_kv = attention_backward(
        True, backward_spot, all_queries, grads, states, end, [*next_near, kv[0], kv[1]], partial
    )
    to_next, grad_q_sent, from_near, from_far, ff_shares, out_downs = lax.optimization_barrier(
        (to_next, grad_q_sent, from_near, from_far, ff_shares, out_downs)
    )
    from_next = hop(to_next, 3)
    grad_q = total([grad_q, swap(grad_q_sent, "co")]).astype(BF16)
    grad_q = jnp.stack([grad_q[:8], hop(grad_q[8:], 3)])
    grad_q = grad_q.reshape(2, 4, 2, HEAD_DIM, 128).transpose(0, 2, 1, 3, 4).reshape(4, 256, 128)

    grad_kv = total([grad_kv, from_near, from_far, from_next])
    grad_kv = grad_kv.astype(BF16).reshape(2, SLICE, 128)
    blocks = jnp.concatenate([to_z(grad_kv), grad_q], axis=1)
    ff_shares, out_downs = after((ff_shares, out_downs), blocks)
    blocks = exchange(blocks, ("zl", "zh"))

    ff_share = jnp.sum(ff_shares.astype(F32), axis=0)
    ff_share = jnp.concatenate(
        [ff_share[:128].T, ff_share[128:, :128], ff_share[128:, 128:]]
    ).astype(BF16)
    rows_home, out_kept_sum, out_sent_sum = on_core(
        out_sums_kernel,
        "out_sums",
        [((2, 128, width), F32), ((4, 2, 2, HEAD_DIM, 128), F32), ((4, 2, 2, HEAD_DIM, 128), BF16)],
        (place, *out_downs, resid, down_bias.astype(F32)[None], grad_resid),
        1_000_000,
    )
    unit, out_sent_sum = after((unit, out_sent_sum), rows_home)
    out_got = swap(out_sent_sum, "co")

    *grad_normed, part_sums = on_core(
        project_back_kernel,
        "project_back",
        [row] * 4 + [((2, width), F32)],
        (place, blocks, unit, own3, near3, far3),
        800_000_000,
        scratch=[pltpu.VMEM((512, width), F32)],
    )
    grad_normed = send_y(grad_normed)
    blocks, ff_share = after((blocks, ff_share), part_sums)
    ff_rest = gather(ff_share, ("x", "zl"), 8)

    head_kept, head_sent, head_sums = on_core(
        qkv_grads_kernel,
        "qkv_grads",
        [((4, 2, 2, 192, 128), BF16)] * 2 + [((4, 192, 128), F32)],
        (place, blocks, normed),
        900_000_000,
    )
    head_got = swap(head_sent, "co")
    rows_home = to_mirror(after(rows_home, head_got), zl)

    head_sums = head_sums[:, :, 0].reshape(2, 2, 3, HEAD_DIM)
    bias = jnp.stack([head_sums[:, :, 2], head_sums[:, :, 1]]).transpose(2, 0, 1, 3)
    up_sums = grad_up_bias.reshape(2, 2, 256)
    up_sums = turned(turned(up_sums, 0, core), 1, zh).transpose(1, 0, 2).reshape(1, width)
    bias = jnp.pad(bias.reshape(1, 512), ((0, 0), (0, 512)))
    small = jnp.concatenate([part_sums, norm_sums, up_sums, bias])
    small = small + swap(small, "co")
    (shares,) = on_core(
        shares_kernel,
        "shares",
        [((16, 272, 128), BF16)],
        (place, head_kept, head_got, out_kept_sum, out_got, small),
        1_000_000,
    )
    shares = exchange(shares, ("x", "zl", "zh"))
    share = jnp.sum(shares.astype(F32), axis=0).astype(BF16)
    rest = gather(share, ("x", "zl"), 8)
    small = rest[:, 256:264].astype(F32).transpose(1, 0, 2).reshape(8, width)
    small = jnp.concatenate([total(gather_y(small[:6])), small[6:]])
    grad_up_bias = lax.dynamic_slice_in_dim(small[6], zh * 512, 512, 0)
    grad_qv_bias = lax.dynamic_slice_in_dim(small[7], zh * 256, 256, 0).reshape(2, 128)

    (grad_tokens,) = on_core(
        last_norm_kernel,
        "last_norm",
        [((128, width), F32)],
        (place, *grad_normed, tokens, gain_one, rows_home[1]),
        1_000_000,
    )
    grad_down_weight, grad_up_weight = on_core(
        unit_weights_kernel,
        "unit_weights",
        [((512, width), F32), ((width, 512), F32)],
        (place, ff_rest, swap(ff_rest, "co")),
        1_000_000,
    )
    grad_qkv_weight, grad_out_weight = on_core(
        head_weights_kernel,
        "head_weights",
        [((3, width, 128), F32), ((128, width), F32)],
        (place, rest, swap(rest, "co")),
        1_000_000,
    )
    return (
        rows_home[0],
        grad_tokens,
        small[0],
        small[1],
        grad_qkv_weight.transpose(1, 0, 2),
        grad_qv_bias,
        grad_out_weight,
        small[2],
        small[3],
        small[4],
        grad_up_weight,
        grad_up_bias,
        grad_down_weight,
        small[5],
    )


def solution(mesh):
    fine = Mesh(mesh.devices.reshape(4, 2, 2, 4, 2), AXES)
    slices, shards = ("x", "zl", "co"), ("y", "zh")
    return jax.shard_map(
        on_device,
        mesh=fine,
        in_specs=(
            P(AXES, None),
            P(slices),
            P(),
            P(),
            P(None, None, shards),
            P(None, shards),
            P(shards, None),
            P(),
            P(),
            P(),
            P(None, shards),
            P(shards),
            P(shards, None),
            P(),
            P(AXES, None),
        ),
        out_specs=(
            P(AXES, None),
            P(AXES, None),
            P(),
            P(),
            P(None, None, shards),
            P(None, shards),
            P(shards, None),
            P(),
            P(),
            P(),
            P(None, shards),
            P(shards),
            P(shards, None),
            P(),
        ),
        check_vma=False,
    )
```

```python
import functools

import jax
import jax.numpy as jnp
from jax import lax
from jax.experimental import pallas as pl
from jax.experimental.pallas import tpu as pltpu
from jax.sharding import Mesh
from jax.sharding import PartitionSpec as P

HEAD_DIM = 64
EPSILON = 1e-05
MASKED = -1e30
LOG2E = 1.4426950408889634
TO_LOG2 = LOG2E * HEAD_DIM ** (-0.5)
AXES = ("x", "zl", "co", "y", "zh")
BF16, F32 = jnp.bfloat16, jnp.float32
SLICE = 1024
FWD_Q, FWD_K = 1024, 1024
BWD_Q = 1024


def contract(left, right, left_dim, right_dim):
    return lax.dot_general(
        left, right, (((left_dim,), (right_dim,)), ((), ())), preferred_element_type=F32
    )


def matmul(left, right):
    return contract(left, right, 1, 0)


def shift(values, steps):
    return lax.ppermute(values, "y", [(i, (i + steps) % 4) for i in range(4)])


def hop(values, bit, axis="x"):
    return lax.ppermute(values, axis, [(i, i ^ bit) for i in range(4)])


def swap(values, axis):
    return lax.ppermute(values, axis, [(0, 1), (1, 0)])


def to_mirror(rows, zl):
    moved = lax.ppermute(rows, ("x", "zl"), [(i, 8 - i) for i in (1, 3, 5, 7)])
    return jnp.where(zl == 0, rows, moved)


def exchange(blocks, axes):
    return lax.all_to_all(blocks, axes, 0, 0, tiled=True)


def gather(rows, axes, size):
    return exchange(jnp.broadcast_to(rows[None], (size,) + rows.shape), axes)


def gather_y(rows):
    one, three = shift(rows, 1), shift(rows, 3)
    return rows, one, shift(rows, 2), three


def send_y(blocks):
    return blocks[0], shift(blocks[1], -1), shift(blocks[3], -3), shift(blocks[2], -2)


def total(parts):
    return functools.reduce(jnp.add, [part.astype(F32) for part in parts])


def after(value, *others):
    return lax.optimization_barrier((value, others))[0]


def turned(values, dim, index):
    return jnp.where(index == 0, values, jnp.flip(values, dim))


def halves(values, dim, index):
    half = values.shape[dim] // 2
    return (
        lax.dynamic_slice_in_dim(values, index * half, half, dim),
        lax.dynamic_slice_in_dim(values, (1 - index) * half, half, dim),
    )


def to_z(rows):
    n = rows.shape[-1]
    return rows.reshape(2, 4, 2, 128, n).transpose(0, 2, 1, 3, 4).reshape(4, 512, n)


def on_core(kernel, name, outputs, operands, flops, limit=32, scratch=()):
    whole = pl.BlockSpec(memory_space=pltpu.VMEM)
    outputs = [jax.ShapeDtypeStruct(shape, dtype) for shape, dtype in outputs]
    return pl.pallas_call(
        kernel,
        out_shape=outputs,
        in_specs=[pl.BlockSpec(memory_space=pltpu.SMEM)] + [whole] * (len(operands) - 1),
        out_specs=[whole] * len(outputs),
        scratch_shapes=list(scratch),
        compiler_params=pltpu.CompilerParams(vmem_limit_bytes=limit << 20),
        cost_estimate=pl.CostEstimate(flops=flops, bytes_accessed=4 << 20, transcendentals=0),
        name=name,
    )(*operands)


def joined(refs, dim=0):
    return jnp.concatenate([ref[...] for ref in refs], axis=dim)


def unit_rows(rows):
    centered = rows - jnp.mean(rows, axis=-1, keepdims=True)
    scale = lax.rsqrt(jnp.mean(centered * centered, axis=-1, keepdims=True) + EPSILON)
    return centered * scale, scale


def norm_back(grad, unit, scale, gain):
    grad = grad * gain
    along = jnp.mean(grad * unit, axis=-1, keepdims=True)
    return scale * (grad - jnp.mean(grad, axis=-1, keepdims=True) - unit * along)


def y_rows(place, steps):
    return pl.ds(pl.multiple_of(((place[3] - steps) & 3) * 128, 128), 128)


def merge_lanes(left, right):
    left, right = left.astype(F32), right.astype(F32)
    first = lax.broadcasted_iota(jnp.int32, left.shape, 1) < HEAD_DIM
    return (
        jnp.where(first, left, pltpu.roll(right, HEAD_DIM, 1)).astype(BF16),
        jnp.where(first, pltpu.roll(left, HEAD_DIM, 1), right).astype(BF16),
    )


def project_kernel(place, *refs):
    pieces, (gain, bent, own, near, far, own_bias, pair_bias) = refs[:4], refs[4:11]
    blocks, normed_ref, unit_ref = refs[11:]
    core, zh = place[2], place[4]
    for steps, piece in enumerate(pieces):
        rows = y_rows(place, steps)
        unit, _ = unit_rows(piece[...].astype(F32))
        unit_ref[rows, :] = unit.astype(BF16)
        normed_ref[rows, :] = (unit * gain[...] + bent[...]).astype(BF16)
    normed = normed_ref[...]
    first = normed_ref[:, pl.ds(pl.multiple_of(core * 512, 512), 512)]
    second = normed_ref[:, pl.ds(pl.multiple_of((1 - core) * 512, 512), 512)]
    for pair in range(2):
        bias = (pair_bias if pair else own_bias)[...].astype(F32)

        def projected(i, pair=pair):
            if pair:
                return matmul(first, near[i]) + matmul(second, far[i])
            return matmul(normed, own[i])

        queries = (projected(0) + bias[:1]).T.astype(BF16)
        mixed = merge_lanes(projected(1).astype(BF16), (projected(2) + bias[1:]).astype(BF16))
        for head in range(2):
            where = 2 * head + (zh ^ pair)
            blocks[where, pl.ds(0, 512), :] = mixed[head]
            for y in range(4):
                lanes = slice(y * 128, y * 128 + 128)
                piece = queries[head * HEAD_DIM : head * HEAD_DIM + HEAD_DIM, lanes]
                blocks[where, pl.ds(512 + y * HEAD_DIM, HEAD_DIM), :] = piece


def project_back_kernel(place, blocks, unit_ref, own, near, far, *refs):
    outs, sums, grad_ref = refs[:4], refs[4], refs[5]
    core, zh = place[2], place[4]
    for pair in range(2):
        heads = [blocks[2 * head + (zh ^ pair)] for head in range(2)]
        keys, values = merge_lanes(heads[0][:512], heads[1][:512])
        queries = [
            jnp.concatenate([head[512 + y * HEAD_DIM :][:HEAD_DIM] for y in range(4)], axis=1)
            for head in heads
        ]
        parts = (jnp.concatenate(queries, axis=0).T, keys, values)

        def back(weight, parts=parts):
            return functools.reduce(
                jnp.add, [contract(part, weight[i], 1, 1) for i, part in enumerate(parts)]
            )

        if pair:
            first = pl.ds(pl.multiple_of(core * 512, 512), 512)
            second = pl.ds(pl.multiple_of((1 - core) * 512, 512), 512)
            grad_ref[:, first] += back(near)
            grad_ref[:, second] += back(far)
        else:
            grad_ref[...] = back(own)
    grad = grad_ref[...]
    sums[...] = jnp.concatenate(
        [
            jnp.sum(grad * unit_ref[...].astype(F32), axis=0, keepdims=True),
            jnp.sum(grad, axis=0, keepdims=True),
        ]
    )
    for steps, out in enumerate(outs):
        out[...] = grad_ref[y_rows(place, steps), :].astype(BF16)


def qkv_grads_kernel(place, blocks_ref, normed_ref, kept, sent, sums_ref):
    normed, ones = normed_ref[...], jnp.ones((512, 128), BF16)
    for head in range(2):
        for zh in range(2):
            block = blocks_ref[2 * head + zh]
            queries = [block[512 + y * HEAD_DIM :][:HEAD_DIM] for y in range(4)]
            left = jnp.concatenate([block[:512].T, jnp.concatenate(queries, axis=1)], axis=0)
            grad = matmul(left, normed)
            for half in range(2):

                def store(ref, grad=grad, half=half, head=head, zh=zh):
                    for chunk in range(4):
                        lanes = slice((4 * half + chunk) * 128, (4 * half + chunk) * 128 + 128)
                        ref[chunk, head, zh] = grad[:, lanes].astype(BF16)

                pl.when(place[2] == half)(functools.partial(store, kept))
                pl.when(place[2] != half)(functools.partial(store, sent))
            sums_ref[2 * head + zh] = matmul(left, ones)


def attend_out_kernel(place, heads, kept, sent, tokens, bias, gain, bent, resid_ref, mid_ref, att_ref):
    core, y, zh = place[2], place[3], place[4]
    for side in range(2):
        for steps in range(4):
            for pair in range(2):
                where = 8 * (core ^ side) + 2 * ((y - steps) & 3) + (zh ^ pair)
                att_ref[side, pl.ds(steps * 128 + pair * HEAD_DIM, HEAD_DIM), :] = heads[where]
    branch = matmul(att_ref[0].T, kept[...]) + matmul(att_ref[1].T, sent[...])
    resid = tokens[...].astype(F32) + branch + bias[...]
    resid_ref[...] = resid
    mid_ref[...] = (unit_rows(resid)[0] * gain[...] + bent[...]).astype(BF16)


def mid_back_kernel(place, *refs):
    parts, resid, cotangent, gain, kept, sent = refs[:6]
    grad_resid_ref, branch_ref, heads, sums = refs[6:]
    core, y, zh = place[2], place[3], place[4]
    grad = total([parts[i] for i in range(4)])
    unit, scale = unit_rows(resid[...])
    cot = cotangent[...].astype(F32)
    grad_resid = cot + norm_back(grad, unit, scale, gain[...])
    grad_resid_ref[...] = grad_resid
    branch = grad_resid.astype(BF16)
    branch_ref[...] = branch
    rows = [grad_resid, grad * unit, grad, cot]
    sums[...] = jnp.concatenate([jnp.sum(row, axis=0, keepdims=True) for row in rows])
    for side, weight in enumerate((kept, sent)):
        grads = contract(weight[...], branch, 1, 1).astype(BF16)
        for steps in range(4):
            for pair in range(2):
                where = 8 * (core ^ side) + 2 * ((y - steps) & 3) + (zh ^ pair)
                start = steps * 128 + pair * HEAD_DIM
                heads[where] = grads[start : start + HEAD_DIM]


def feed_forward_kernel(place, *refs):
    mids, cots, (bias,), ups, downs = refs[:4], refs[4:8], refs[8:9], refs[9:13], refs[13:17]
    active_ref, grad_ref, out, bias_grad, sent = refs[17:]
    mid, cot = joined(mids), jnp.concatenate([ref[:128, :] for ref in cots])
    summed = None
    for i, (up_ref, down_ref) in enumerate(zip(ups, downs)):
        span = pl.ds(i * 256, 256)
        up = up_ref[...]
        hidden = matmul(mid, up) + bias[:, span]
        square = hidden * hidden
        bent = jnp.tanh(0.7978845608028654 * hidden * (1.0 + 0.044715 * square))
        active_ref[:, span] = (0.5 * hidden * (1.0 + bent)).astype(BF16)
        slope = 0.7978845608028654 * (1.0 + 3.0 * 0.044715 * square)
        slope = 0.5 * (1.0 + bent) + 0.5 * hidden * (1.0 - bent * bent) * slope
        grad = (slope * contract(cot, down_ref[...], 1, 1)).astype(BF16)
        grad_ref[:, span] = grad
        bias_grad[:, span] = jnp.sum(grad.astype(F32), axis=0, keepdims=True)
        part = contract(grad, up, 1, 1)
        summed = part if summed is None else summed + part
    for steps in range(4):
        piece = summed[steps * 128 : steps * 128 + 128].astype(BF16)
        out[(place[3] - steps) & 3] = piece
    for i, (left, right) in enumerate(((cot, active_ref), (mid, grad_ref))):
        summed = contract(left, right[:, 512:], 0, 0)
        for share in range(8):
            sent[share, i] = summed[share * 128 : share * 128 + 128].astype(BF16)


def unit_grads_kernel(place, *refs):
    mids, cots, (active, grad, got, out) = refs[:4], refs[4:8], refs[8:]
    cot = jnp.concatenate([ref[:128, :] for ref in cots])
    for i, (left, right) in enumerate(((cot, active), (joined(mids), grad))):
        summed = contract(left, right[:, :512], 0, 0)
        for share in range(8):
            block = summed[share * 128 : share * 128 + 128]
            block = (block + got[share, i].astype(F32)).astype(BF16)
            for pair in range(2):
                half = block[:, pair * 256 : pair * 256 + 256]
                out[2 * share + (place[4] ^ pair), pl.ds(i * 128, 128), :] = half


def out_down_kernel(place, att, branch, active, *refs):
    downs, outs = refs[:4], refs[4:]
    grads = [matmul(att[side], branch[...]).astype(BF16) for side in range(2)]
    down = total([matmul(active[:, i * 256 : i * 256 + 256], ref[...]) for i, ref in enumerate(downs)])
    for steps, out in enumerate(outs):
        rows = slice(steps * 128, steps * 128 + 128)
        out[pl.ds(0, 128), :] = grads[0][rows]
        out[pl.ds(128, 128), :] = grads[1][rows]
        out[pl.ds(256, 128), :] = down[rows].astype(BF16)


def out_sums_kernel(place, *refs):
    parts, (resid, bias, grad_resid, home, kept, sent) = refs[:4], refs[4:]
    home[0] = total([part[256:, :] for part in parts]) + resid[...] + bias[...]
    home[1] = grad_resid[...]
    for side, ref in enumerate((kept, sent)):
        summed = total([part[side * 128 : side * 128 + 128, :] for part in parts]).astype(ref.dtype)
        for pair in range(2):
            for share in range(8):
                lanes = slice(share * 128, share * 128 + 128)
                piece = summed[pair * HEAD_DIM : pair * HEAD_DIM + HEAD_DIM, lanes]
                ref[share // 2, share % 2, pair] = piece


def shares_kernel(place, heads, head_got, out, out_got, small, shares):
    for x in range(4):
        for zl in range(2):
            share = 2 * x + zl
            for zh in range(2):
                to = 2 * share + zh
                grad = total([heads[x, zl, zh], head_got[x, zl, zh]])
                shares[to, pl.ds(0, 192), :] = grad.astype(BF16)
                grad = total([out[x, zl, zh], out_got[x, zl, zh]])
                shares[2 * share + (place[4] ^ zh), pl.ds(192, HEAD_DIM), :] = grad.astype(BF16)
                rows = small[:, share * 128 : share * 128 + 128]
                rows = jnp.concatenate([rows, jnp.zeros_like(rows)]).astype(BF16)
                shares[to, pl.ds(256, 16), :] = rows


def last_norm_kernel(place, *refs):
    parts, (tokens, gain, resid, out) = refs[:4], refs[4:]
    unit, scale = unit_rows(tokens[...].astype(F32))
    out[...] = resid[...] + norm_back(total([part[...] for part in parts]), unit, scale, gain[...])


def unit_weights_kernel(place, own, other, down, up):
    for side, ref in enumerate((own, other)):
        half = place[2] ^ side
        for share in range(8):
            lanes = pl.ds(share * 128, 128)
            down[pl.ds(pl.multiple_of(half * 256, 256), 256), lanes] = ref[share, :256].astype(F32)
            for part in range(2):
                lanes = pl.ds(pl.multiple_of(half * 256 + part * 128, 128), 128)
                piece = ref[share, pl.ds(256 + part * 128, 128), :].astype(F32)
                up[pl.ds(share * 128, 128), lanes] = piece


def head_weights_kernel(place, own, other, qkv, out):
    for side, ref in enumerate((own, other)):
        half = place[2] ^ side
        for x in range(4):
            rows = pl.ds(pl.multiple_of(half * 512 + x * 128, 128), 128)
            for i, which in enumerate((1, 2, 0)):
                span = pl.ds(i * HEAD_DIM, HEAD_DIM)
                both = jnp.concatenate([ref[2 * x, span, :], ref[2 * x + 1, span, :]])
                qkv[which, rows, :] = both.astype(F32).T
            for zl in range(2):
                piece = ref[2 * x + zl, pl.ds(192, HEAD_DIM), :].astype(F32)
                span = pl.ds(pl.multiple_of(half * HEAD_DIM, HEAD_DIM), HEAD_DIM)
                out[span, pl.ds((2 * x + zl) * 128, 128)] = piece


def forward_kernel(spot, q_ref, end_ref, *refs):
    pieces, (state_ref, out, kv_ref, vt_ref, qt_ref) = refs[:14], refs[14:]
    x, core = spot[0], spot[1]

    def bring(piece, half, x_from, slice_in_x, parity):
        where = (4 * x_from + 2 * slice_in_x + parity) * SLICE
        rows = pl.ds(pl.multiple_of(where, SLICE), SLICE)
        kv_ref[rows, :] = piece[pl.ds(half * SLICE, SLICE), :]

    for side in range(2):
        parity = core if side == 0 else 1 - core
        pieces_here = pieces[7 * side : 7 * side + 7]
        bring(pieces_here[0], 0, x, 0, parity)
        bring(pieces_here[0], 1, x, 1, parity)
        for i, piece in enumerate(pieces_here[1:]):
            bring(piece, 0, x ^ (1, 1, 3, 3, 2, 2)[i], i % 2, parity)
    qt_ref[HEAD_DIM:, :] = jnp.zeros((HEAD_DIM, 2 * SLICE), BF16)
    for chunk in range(16):
        qt_ref[:HEAD_DIM, pl.ds(chunk * 128, 128)] = q_ref[chunk]
    vt_ref[HEAD_DIM:, :] = jnp.ones((16, vt_ref.shape[1]), BF16)
    def turn(i, largest):
        rows = pl.ds(pl.multiple_of(i * SLICE, SLICE), SLICE)
        both = kv_ref[rows, :].T
        vt_ref[:HEAD_DIM, rows] = both[HEAD_DIM:, :]
        keys = both[:HEAD_DIM, :].astype(F32)
        return jnp.maximum(largest, jnp.sum(keys * keys, axis=0, keepdims=True))

    longest = jnp.max(lax.fori_loop(0, 16, turn, jnp.zeros((1, SLICE), F32)))
    norms = qt_ref[:HEAD_DIM, :].astype(F32)
    norms = jnp.sum(norms * norms, axis=0, keepdims=True)
    limit = jnp.sqrt(norms * longest) * TO_LOG2
    level = limit - 90.0

    def finish(total, log_top, start, wide):
        span = pl.ds(start, wide)
        weight_sum = total[HEAD_DIM : HEAD_DIM + 1]
        mixed = total[:HEAD_DIM] / weight_sum
        state_ref[:HEAD_DIM, span] = mixed
        for chunk in range(wide // 128):
            piece = mixed[:, chunk * 128 : chunk * 128 + 128].astype(BF16)
            out[start // 128 + chunk] = piece
        state_ref[HEAD_DIM:, span] = jnp.broadcast_to(log_top + jnp.log2(weight_sum), (8, wide))

    def masked_at(values, begin, end, other):
        place = begin + lax.broadcasted_iota(jnp.int32, values.shape, 0)
        return jnp.where(place < end, values, other)

    def bounded_tile(tile):
        span = pl.ds(tile * FWD_Q, FWD_Q)
        query, end = qt_ref[:, span], end_ref[:, span]
        base = level[:, tile * FWD_Q : tile * FWD_Q + FWD_Q]

        def step(masked, keys, at, total):
            for piece in range(max(keys // 512, 1)):
                size = min(keys, 512)
                begin = pl.multiple_of(at * keys + piece * size, size)
                rows = pl.ds(begin, size)
                weights = jnp.exp2(matmul(kv_ref[rows, :], query) * TO_LOG2 - base)
                if masked:
                    weights = masked_at(weights, begin, end, 0.0)
                total = total + matmul(vt_ref[:, rows], weights.astype(BF16))
            return total

        total = jnp.zeros((HEAD_DIM + 16, FWD_Q), F32)
        full, last, pieces = spot[2 + 3 * tile], spot[3 + 3 * tile], spot[4 + 3 * tile]
        total = lax.fori_loop(0, full, functools.partial(step, False, FWD_K), total)

        def edge(at, total):
            left = pieces - 4 * at
            long = left > 2
            ranges = ((FWD_K, at, jnp.where(long, 1, 0)), (256, 4 * at, jnp.where(long, 0, left)))
            for keys, begin, count in ranges:
                masked = functools.partial(step, True, keys)
                total = lax.fori_loop(begin, begin + count, masked, total)
            return total

        total = lax.fori_loop(full, last, edge, total)
        finish(total, base, tile * FWD_Q, FWD_Q)

    def running_tile(tile):
        wide = FWD_Q // 2
        starts = [tile * FWD_Q, tile * FWD_Q + wide]
        queries = [qt_ref[:, pl.ds(start, wide)] for start in starts]
        ends = [end_ref[:, pl.ds(start, wide)] for start in starts]

        def step(masked, at, carry):
            rows = pl.ds(pl.multiple_of(at * FWD_K, FWD_K), FWD_K)
            kv, vt = kv_ref[rows, :], vt_ref[:, rows]
            scores = [matmul(kv, query) for query in queries]
            after = []
            for (top, total), score, end in zip(carry, scores, ends):
                if masked:
                    score = masked_at(score, at * FWD_K, end, MASKED)
                new_top = jnp.maximum(top, jnp.max(score, axis=0, keepdims=True))
                weights = jnp.exp2(score * TO_LOG2 - new_top * TO_LOG2)
                factor = jnp.exp2((top - new_top) * TO_LOG2)
                total = total * factor + matmul(vt, weights.astype(BF16))
                after.append((new_top, total))
            return tuple(after)

        begin = (jnp.full((1, wide), MASKED, F32), jnp.zeros((HEAD_DIM + 16, wide), F32))
        full, last = spot[2 + 3 * tile], spot[3 + 3 * tile]
        carry = lax.fori_loop(0, full, functools.partial(step, False), (begin, begin))
        carry = lax.fori_loop(full, last, functools.partial(step, True), carry)
        for (top, total), start in zip(carry, starts):
            finish(total, top * TO_LOG2, start, wide)

    small = jnp.max(limit) <= 100.0

    @pl.when(small)
    def _():
        for tile in range(2 * SLICE // FWD_Q):
            bounded_tile(tile)

    @pl.when(jnp.logical_not(small))
    def _():
        for tile in range(2 * SLICE // FWD_Q):
            running_tile(tile)


def attention_forward(spot, queries, end, pieces):
    rows, total = 2 * SLICE, 16 * SLICE
    whole = pl.BlockSpec(memory_space=pltpu.VMEM)
    return pl.pallas_call(
        forward_kernel,
        out_shape=[
            jax.ShapeDtypeStruct((HEAD_DIM + 8, rows), F32),
            jax.ShapeDtypeStruct((16, HEAD_DIM, 128), BF16),
        ],
        in_specs=[pl.BlockSpec(memory_space=pltpu.SMEM)] + [whole] * 16,
        out_specs=[whole] * 2,
        scratch_shapes=[
            pltpu.VMEM((total, 2 * HEAD_DIM), BF16),
            pltpu.VMEM((HEAD_DIM + 16, total), BF16),
            pltpu.VMEM((2 * HEAD_DIM, rows), BF16),
        ],
        compiler_params=pltpu.CompilerParams(vmem_limit_bytes=32 << 20),
        cost_estimate=pl.CostEstimate(
            flops=20_000_000_000, bytes_accessed=9 << 20, transcendentals=1 << 20
        ),
        name="attention_forward",
    )(spot, queries, end, *pieces)


def backward_kernel(last, spot, *refs):
    q_refs, do_refs, state_refs, (end_ref, *kv_refs) = refs[:2], refs[2:4], refs[4:6], refs[6:11]
    if last:
        partial_ref, *refs = refs[11:]
        dq_refs, dkv_refs, scratch = refs[:2], refs[2:4], refs[4:]
    else:
        partial_ref, dkv_refs, scratch = refs[11], refs[12:14], refs[14:]
    kv_ref, kt_ref, q_ref, do_ref, qt_ref, dot_ref, lse_ref, delta_ref, sum_ref = scratch
    x, core = spot[0], spot[1]
    per_core = 2 * SLICE
    none = jnp.zeros((HEAD_DIM, 2 * per_core), BF16)
    qt_ref[HEAD_DIM:, :] = none
    dot_ref[:HEAD_DIM, :] = none
    for side in range(2):
        for chunk in range(16):
            lanes = pl.ds(side * per_core + chunk * 128, 128)
            qt_ref[:HEAD_DIM, lanes] = q_refs[side][chunk]
            dot_ref[HEAD_DIM:, lanes] = do_refs[side][chunk]
        rows = pl.ds(side * per_core, per_core)
        q_ref[rows, :] = qt_ref[:, rows].T
        do_ref[rows, :] = dot_ref[:, rows].T
        state = state_refs[side]
        lse_ref[:, rows] = state[HEAD_DIM:, :]
        product = state[:HEAD_DIM, :] * dot_ref[HEAD_DIM:, rows].astype(F32)
        delta_ref[:, rows] = jnp.broadcast_to(jnp.sum(product, axis=0, keepdims=True), (8, per_core))
    for i, ref in enumerate(kv_refs):
        rows = pl.ds(i * SLICE, SLICE)
        kv_ref[rows, :] = ref[:SLICE, :]
        kt_ref[:, rows] = kv_ref[rows, :].T[:HEAD_DIM, :]
    sum_ref[...] = jnp.zeros_like(sum_ref)

    @pl.loop(0, 2 * per_core // BWD_Q)
    def _(tile):
        span = pl.ds(pl.multiple_of(tile * BWD_Q, BWD_Q), BWD_Q)
        query_t, grad_t = qt_ref[:, span], dot_ref[:, span]
        query, grad = q_ref[span, :], do_ref[span, :]
        end, lse, delta = end_ref[:, span], lse_ref[:1, span], delta_ref[:1, span]
        full, upto, pieces = spot[2 + 3 * tile], spot[3 + 3 * tile], spot[4 + 3 * tile]

        def step(masked, keys, block, at, grad_query):
            held = pl.ds(pl.multiple_of(block * per_core + at * keys, keys), keys)
            kv = kv_ref[held, :]
            weights = jnp.exp2(matmul(kv, query_t) * TO_LOG2 - lse)
            if masked:
                slices = at // (SLICE // keys)
                begin = (4 * x_of[block] + slices + core) * SLICE + at * keys
                place = begin + lax.broadcasted_iota(jnp.int32, weights.shape, 0)
                weights = jnp.where(place < end, weights, 0.0)
            grad_scores = (weights * (matmul(kv, grad_t) - delta)).astype(BF16)
            sum_ref[held, :] += matmul(weights.astype(BF16), grad) + matmul(grad_scores, query)
            return grad_query + matmul(kt_ref[:, held], grad_scores)

        x_of = [x ^ 3, x] if last else [x ^ 1, x ^ 2]
        grad_query = partial_ref[:, span] if last else jnp.zeros((HEAD_DIM, BWD_Q), F32)
        for block in range(2):
            whole = jnp.clip(full - 2 * x_of[block], 0, 2)
            some = jnp.clip(upto - 2 * x_of[block], 0, 2)
            plain = functools.partial(step, False, SLICE, block)
            grad_query = lax.fori_loop(0, whole, plain, grad_query)

            def edge(at, grad_query, block=block):
                left = pieces - 4 * (4 * x_of[block] + 2 * at + core)
                long = left > 2
                ranges = ((SLICE, at, jnp.where(long, 1, 0)), (256, 4 * at, jnp.where(long, 0, left)))
                for keys, begin, count in ranges:
                    masked = functools.partial(step, True, keys, block)
                    grad_query = lax.fori_loop(begin, begin + count, masked, grad_query)
                return grad_query

            grad_query = lax.fori_loop(whole, some, edge, grad_query)
        if last:
            done = (grad_query * HEAD_DIM ** (-0.5)).astype(BF16)
            chunks = BWD_Q // 128
            for side in range(2):

                @pl.when(tile // (per_core // BWD_Q) == side)
                def _(side=side):
                    base = (tile - side * (per_core // BWD_Q)) * chunks
                    for chunk in range(chunks):
                        dq_refs[side][base + chunk] = done[:, chunk * 128 : chunk * 128 + 128]

        else:
            partial_ref[:, span] = grad_query

    is_key = lax.broadcasted_iota(jnp.int32, (1, 2 * HEAD_DIM), 1) < HEAD_DIM
    scale = jnp.where(is_key, HEAD_DIM ** (-0.5), 1.0)
    for block in range(2):
        dkv_refs[block][...] = (sum_ref[pl.ds(block * per_core, per_core), :] * scale).astype(BF16)


def attention_backward(last, spot, queries, grads, states, end, kvs, partial=None):
    rows, wide = 2 * SLICE, 2 * HEAD_DIM
    whole = pl.BlockSpec(memory_space=pltpu.VMEM)
    block = jax.ShapeDtypeStruct((rows, wide), BF16)
    if last:
        out_shape = [jax.ShapeDtypeStruct((16, HEAD_DIM, 128), BF16)] * 2 + [block] * 2
        operands = (spot, *queries, *grads, *states, end, *kvs, partial)
    else:
        out_shape = [jax.ShapeDtypeStruct((HEAD_DIM, 2 * rows), F32), block, block]
        operands = (spot, *queries, *grads, *states, end, *kvs)
    return pl.pallas_call(
        functools.partial(backward_kernel, last),
        out_shape=out_shape,
        in_specs=[pl.BlockSpec(memory_space=pltpu.SMEM)] + [whole] * (len(operands) - 1),
        out_specs=[whole] * len(out_shape),
        scratch_shapes=[
            pltpu.VMEM((2 * rows, wide), BF16),
            pltpu.VMEM((HEAD_DIM, 2 * rows), BF16),
            pltpu.VMEM((2 * rows, wide), BF16),
            pltpu.VMEM((2 * rows, wide), BF16),
            pltpu.VMEM((wide, 2 * rows), BF16),
            pltpu.VMEM((wide, 2 * rows), BF16),
            pltpu.VMEM((8, 2 * rows), F32),
            pltpu.VMEM((8, 2 * rows), F32),
            pltpu.VMEM((2 * rows, wide), F32),
        ],
        compiler_params=pltpu.CompilerParams(vmem_limit_bytes=36 << 20),
        cost_estimate=pl.CostEstimate(
            flops=8_000_000_000, bytes_accessed=6 << 20, transcendentals=1 << 20
        ),
        name="attention_backward_two" if last else "attention_backward_one",
    )(*operands)


def on_device(
    tokens,
    block_ids,
    ln1_gain,
    ln1_shift,
    qkv_weight,
    qv_bias,
    out_weight,
    out_bias,
    ln2_gain,
    ln2_shift,
    up_weight,
    up_bias,
    down_weight,
    down_bias,
    cotangent,
):
    x, zl, core, y, zh = (lax.axis_index(name) for name in AXES)
    place = jnp.stack([x, zl, core, y, zh]).astype(jnp.int32)
    width = tokens.shape[1]
    gain_one, shift_one, gain_two, shift_two, bias_out = (
        values.astype(F32)[None]
        for values in (ln1_gain, ln1_shift, ln2_gain, ln2_shift, out_bias)
    )

    pieces = gather_y(tokens)
    own3 = qkv_weight.transpose(1, 0, 2)
    near3 = swap(halves(own3, 1, core)[0], "zh")
    far3 = swap(near3, "co")
    out_kept = halves(out_weight, 0, core)[0]
    biases = jnp.concatenate([qv_bias.reshape(256), up_bias])
    biases = jnp.pad(biases[None], ((0, 15), (0, width - 768)))
    out_near = swap(jnp.concatenate([out_kept, biases]), "zh")
    pair_bias, pair_up_bias = out_near[HEAD_DIM, :256].reshape(2, 128), out_near[HEAD_DIM, 256:768]
    out_kept = jnp.concatenate([out_kept, out_near[:HEAD_DIM]])

    table = gather(block_ids, ("x", "zl", "co"), 16)
    counts = jnp.sum(
        (table.reshape(-1)[None, :] <= jnp.arange(128, dtype=jnp.int32)[:, None]).astype(jnp.int32),
        axis=1,
    )
    places = (4 * x + core, 14 - 4 * x + core, 4 * x + 1 - core, 15 - 4 * x - core)
    query_ids = jnp.concatenate([lax.dynamic_index_in_dim(table, p, 0, False) for p in places])
    same = query_ids[None, :] == jnp.arange(128, dtype=jnp.int32)[:, None]
    end = jnp.sum(jnp.where(same, counts[:, None], 0), axis=0)
    spot = jnp.stack([x, core]).astype(jnp.int32)
    ends = end[: 2 * SLICE].reshape(-1, FWD_Q)
    bounds = [ends[:, 0] // FWD_K, (ends[:, -1] + FWD_K - 1) // FWD_K, (ends[:, -1] + 255) // 256]
    bounds = jnp.stack(bounds, axis=1)
    forward_spot = jnp.concatenate([spot, bounds.reshape(-1)])
    ends = end.reshape(-1, BWD_Q)
    bounds = jnp.stack([ends[:, 0] // SLICE, (ends[:, -1] + SLICE - 1) // SLICE], axis=1)
    bounds = jnp.concatenate([(bounds - core + 1) // 2, (ends[:, -1:] + 255) // 256], axis=1)
    backward_spot = jnp.concatenate([spot, bounds.reshape(-1)])
    end = end[None, :]

    blocks, normed, unit = on_core(
        project_kernel,
        "project",
        [((4, 768, 128), BF16), ((512, width), BF16), ((512, width), BF16)],
        (place, *pieces, gain_one, shift_one, own3, near3, far3, qv_bias, pair_bias),
        800_000_000,
    )
    blocks, forward_spot, backward_spot, end, out_kept = lax.optimization_barrier(
        (blocks, forward_spot, backward_spot, end, out_kept)
    )
    mine = exchange(blocks, ("zl", "zh"))
    up_parts, down_parts = halves(up_weight, 1, core), halves(down_weight, 0, core)
    units = jnp.concatenate(
        [up_parts[0], down_parts[0].reshape(256, 4, 256).transpose(1, 0, 2).reshape(width, 256)]
    )
    rows_here = to_mirror(jnp.stack([tokens, cotangent]), zl)
    units = after(units, mine)
    tokens_here, cotangent_here = rows_here[0], rows_here[1]
    kv = mine[:, :512].reshape(2, 2, 4, 128, 128).transpose(0, 2, 1, 3, 4).reshape(2, SLICE, 128)
    near, next_near = [None] * 2, [None] * 2
    queries = mine[:, 512:].reshape(2, 2, 4, HEAD_DIM, 128).transpose(0, 2, 1, 3, 4)
    queries = queries.reshape(2, 512, 128)
    near[0], next_near[1] = hop(kv[0], 1), hop(jnp.concatenate([kv[1], queries[1]]), 3)
    near[1], next_near[0] = hop(kv[1], 1), hop(kv[0], 3)
    units_near = swap(units, "zh")
    far = [hop(near[0], 3), hop(next_near[1][:SLICE], 1)]
    far, near[1], next_near[0], units_near = lax.optimization_barrier(
        (far, near[1], next_near[0], units_near)
    )
    kv_pieces = [kv.reshape(2 * SLICE, 128), *near, *next_near, *far]
    kv_pieces += [swap(piece, "co") for piece in kv_pieces]

    queries = jnp.concatenate([queries[0], next_near[1][SLICE:]]).reshape(16, HEAD_DIM, 128)
    both = gather_y(jnp.concatenate([cotangent_here, out_kept]))
    state, mixed = attention_forward(forward_spot, queries, end[:, : 2 * SLICE], kv_pieces)
    mixed, both = lax.optimization_barrier((mixed, both))
    out_kept = jnp.concatenate([piece[128:] for piece in both])
    out_sent = swap(out_kept, "co")
    units_far = swap(units_near, "co")

    def parts_of(units):
        return units[:width], units[width:].reshape(4, 256, 256).transpose(1, 0, 2).reshape(256, width)

    (up_near, down_near), (up_far, down_far) = parts_of(units_near), parts_of(units_far)
    ups = (up_parts[0], up_near, up_parts[1], up_far)
    downs = (down_parts[0], down_near, down_parts[1], down_far)
    own_half, pair_half = halves(up_bias, 0, core), halves(pair_up_bias, 0, core)
    up_bias_all = jnp.concatenate([own_half[0], pair_half[0], own_half[1], pair_half[1]])
    up_bias_all = up_bias_all.astype(F32)[None]
    other_state, other_queries = swap(state, "co"), swap(queries, "co")

    heads = exchange(mixed, ("zl", "y", "zh"))
    resid, mid, att = on_core(
        attend_out_kernel,
        "attend_out",
        [((128, width), F32), ((128, width), BF16), ((2, 512, 128), BF16)],
        (place, heads, out_kept, out_sent, tokens_here, bias_out, gain_two, shift_two),
        270_000_000,
    )

    mids = gather_y(mid)
    row = ((128, width), BF16)
    active, grad_hidden, grad_mids, grad_up_bias, sent = on_core(
        feed_forward_kernel,
        "feed_forward",
        [((512, width), BF16)] * 2
        + [((4, 128, width), BF16), ((1, 1024), F32), ((8, 2, 128, 512), BF16)],
        (place, *mids, *both, up_bias_all, *ups, *downs),
        3_300_000_000,
    )
    grad_mids = exchange(grad_mids, "y")
    got = swap(sent, "co")
    (ff_blocks,) = on_core(
        unit_grads_kernel,
        "unit_grads",
        [((16, 256, 256), BF16)],
        (place, *mids, *both, active, grad_hidden, got),
        6_000_000_000,
        limit=56,
    )
    grad_mids = after(grad_mids, ff_blocks)
    grad_resid, grad_branch, grad_heads, norm_sums = on_core(
        mid_back_kernel,
        "mid_back",
        [((128, width), F32), row, ((16, HEAD_DIM, 128), BF16), ((4, width), F32)],
        (place, grad_mids, resid, cotangent_here, gain_two, out_kept, out_sent),
        270_000_000,
    )

    grad_mixed = exchange(grad_heads, ("zl", "y", "zh"))
    late = after((att, grad_branch, active), grad_heads)
    out_downs = on_core(
        out_down_kernel,
        "out_down",
        [((384, width), BF16)] * 4,
        (place, *late, *downs),
        1_400_000_000,
        limit=56,
    )
    grad_mixed, backward_spot = after((grad_mixed, backward_spot), ff_blocks, out_downs)
    ff_blocks = after(ff_blocks, out_downs)
    out_downs = send_y(out_downs)
    other_grad = swap(grad_mixed, "co")
    ff_shares = exchange(ff_blocks, ("x", "zl", "zh"))
    all_queries, grads = [queries, other_queries], [grad_mixed, other_grad]
    states = [state, other_state]
    partial, to_near, to_far = attention_backward(
        False, backward_spot, all_queries, grads, states, end, [*near, *far]
    )
    from_near, from_far = hop(to_near, 1), hop(to_far, 2)
    grad_q, grad_q_sent, to_next, grad_kv = attention_backward(
        True, backward_spot, all_queries, grads, states, end, [*next_near, kv[0], kv[1]], partial
    )
    to_next, grad_q_sent, from_near, from_far, ff_shares, out_downs = lax.optimization_barrier(
        (to_next, grad_q_sent, from_near, from_far, ff_shares, out_downs)
    )
    from_next = hop(to_next, 3)
    grad_q = total([grad_q, swap(grad_q_sent, "co")]).astype(BF16)
    grad_q = jnp.stack([grad_q[:8], hop(grad_q[8:], 3)])
    grad_q = grad_q.reshape(2, 4, 2, HEAD_DIM, 128).transpose(0, 2, 1, 3, 4).reshape(4, 256, 128)

    grad_kv = total([grad_kv, from_near, from_far, from_next])
    grad_kv = grad_kv.astype(BF16).reshape(2, SLICE, 128)
    blocks = jnp.concatenate([to_z(grad_kv), grad_q], axis=1)
    ff_shares, out_downs = after((ff_shares, out_downs), blocks)
    blocks = exchange(blocks, ("zl", "zh"))

    ff_share = jnp.sum(ff_shares.astype(F32), axis=0)
    ff_share = jnp.concatenate(
        [ff_share[:128].T, ff_share[128:, :128], ff_share[128:, 128:]]
    ).astype(BF16)
    rows_home, out_kept_sum, out_sent_sum = on_core(
        out_sums_kernel,
        "out_sums",
        [((2, 128, width), F32), ((4, 2, 2, HEAD_DIM, 128), F32), ((4, 2, 2, HEAD_DIM, 128), BF16)],
        (place, *out_downs, resid, down_bias.astype(F32)[None], grad_resid),
        1_000_000,
    )
    unit, out_sent_sum = after((unit, out_sent_sum), rows_home)
    out_got = swap(out_sent_sum, "co")

    *grad_normed, part_sums = on_core(
        project_back_kernel,
        "project_back",
        [row] * 4 + [((2, width), F32)],
        (place, blocks, unit, own3, near3, far3),
        800_000_000,
        scratch=[pltpu.VMEM((512, width), F32)],
    )
    grad_normed = send_y(grad_normed)
    ff_rest = gather(after(ff_share, blocks), ("x", "zl"), 8)
    blocks = after(blocks, part_sums)

    head_kept, head_sent, head_sums = on_core(
        qkv_grads_kernel,
        "qkv_grads",
        [((4, 2, 2, 192, 128), BF16)] * 2 + [((4, 192, 128), F32)],
        (place, blocks, normed),
        900_000_000,
    )
    head_got = swap(head_sent, "co")
    rows_home = to_mirror(after(rows_home, head_got), zl)

    head_sums = head_sums[:, :, 0].reshape(2, 2, 3, HEAD_DIM)
    bias = jnp.stack([head_sums[:, :, 2], head_sums[:, :, 1]]).transpose(2, 0, 1, 3)
    up_sums = grad_up_bias.reshape(2, 2, 256)
    up_sums = turned(turned(up_sums, 0, core), 1, zh).transpose(1, 0, 2).reshape(1, width)
    bias = jnp.pad(bias.reshape(1, 512), ((0, 0), (0, 512)))
    small = jnp.concatenate([part_sums, norm_sums, up_sums, bias])
    small = small + swap(small, "co")
    (shares,) = on_core(
        shares_kernel,
        "shares",
        [((16, 272, 128), BF16)],
        (place, head_kept, head_got, out_kept_sum, out_got, small),
        1_000_000,
    )
    shares = exchange(shares, ("x", "zl", "zh"))
    share = jnp.sum(shares.astype(F32), axis=0).astype(BF16)
    rest = gather(share, ("x", "zl"), 8)
    small = rest[:, 256:264].astype(F32).transpose(1, 0, 2).reshape(8, width)
    small = jnp.concatenate([total(gather_y(small[:6])), small[6:]])
    grad_up_bias = lax.dynamic_slice_in_dim(small[6], zh * 512, 512, 0)
    grad_qv_bias = lax.dynamic_slice_in_dim(small[7], zh * 256, 256, 0).reshape(2, 128)

    (grad_tokens,) = on_core(
        last_norm_kernel,
        "last_norm",
        [((128, width), F32)],
        (place, *grad_normed, tokens, gain_one, rows_home[1]),
        1_000_000,
    )
    grad_down_weight, grad_up_weight = on_core(
        unit_weights_kernel,
        "unit_weights",
        [((512, width), F32), ((width, 512), F32)],
        (place, ff_rest, swap(ff_rest, "co")),
        1_000_000,
    )
    grad_qkv_weight, grad_out_weight = on_core(
        head_weights_kernel,
        "head_weights",
        [((3, width, 128), F32), ((128, width), F32)],
        (place, rest, swap(rest, "co")),
        1_000_000,
    )
    return (
        rows_home[0],
        grad_tokens,
        small[0],
        small[1],
        grad_qkv_weight.transpose(1, 0, 2),
        grad_qv_bias,
        grad_out_weight,
        small[2],
        small[3],
        small[4],
        grad_up_weight,
        grad_up_bias,
        grad_down_weight,
        small[5],
    )


def solution(mesh):
    fine = Mesh(mesh.devices.reshape(4, 2, 2, 4, 2), AXES)
    slices, shards = ("x", "zl", "co"), ("y", "zh")
    return jax.shard_map(
        on_device,
        mesh=fine,
        in_specs=(
            P(AXES, None),
            P(slices),
            P(),
            P(),
            P(None, None, shards),
            P(None, shards),
            P(shards, None),
            P(),
            P(),
            P(),
            P(None, shards),
            P(shards),
            P(shards, None),
            P(),
            P(AXES, None),
        ),
        out_specs=(
            P(AXES, None),
            P(AXES, None),
            P(),
            P(),
            P(None, None, shards),
            P(None, shards),
            P(shards, None),
            P(),
            P(),
            P(),
            P(None, shards),
            P(shards),
            P(shards, None),
            P(),
        ),
        check_vma=False,
    )
```
